32 devices in a mesh: groups: 2 (over x), ff: 8 (over z, y), var: 2 (over core).
Axes of the slice: x: 2, y: 2, z: 4, core: 2. Of those that a mesh axis runs over, the one named last changes fastest.
Arguments:
- tokens: bfloat16 [128, 8192], P(('groups', 'ff'), 'var'), parts along dimension 0, may hold values from -6 to 6
- gate_weight: bfloat16 [8192, 16384], P('var', 'ff'), may hold values from -0.0625 to 0.0625
- up_weight: bfloat16 [8192, 16384], P('var', 'ff'), may hold values from -0.0625 to 0.0625
- down_weight: bfloat16 [16384, 8192], P('ff', 'var'), may hold values from -0.046875 to 0.046875
- shrink_gu: bfloat16 [64, 32, 8192], P(('groups', 'ff'), None, 'var'), parts along dimension 0, may hold values from -0.0625 to 0.0625
- expand_gu: bfloat16 [64, 2, 16, 16384], P(('groups', 'ff'), None, 'var'), parts along dimension 0, may hold values from -1.5 to 1.5
- shrink_down: bfloat16 [64, 16, 16384], P(('groups', 'ff')), parts along dimension 0, may hold values from -0.046875 to 0.046875
- expand_down: bfloat16 [64, 16, 8192], P(('groups', 'ff'), None, 'var'), parts along dimension 0, may hold values from -1.5 to 1.5
- variant_ids: int32 [128, 1], P('groups'), parts along dimension 0, may hold values from 0 to 31; in each aligned block of 64 rows (0 to 63, 64 to 127, ...) at most 8 rows name the same one
- variant_slot: int32 [64], P('groups'), parts along dimension 0, may hold values from 0 to 31, each once
Outputs:
- mixed: bfloat16 [128, 8192], P(('groups', 'ff'), 'var'), parts along dimension 0
The draws below stay inside these ranges and needn't reach their ends.
There are 2 independent parts, one for each index of `groups`. The reference program is written for one: setup_inputs(seed, part) draws one part's arguments, and reference() takes and returns one part's arrays. A program takes and returns all parts, laid end to end along the dimension named above; an argument that names none is the same for every part. Nothing has to cross between parts.
Inputs may be any that keep to these rules, and one draw needn't show every extreme that they name: `variant_ids`: no variant is used by more than 8 rows of a group and one variant by exactly 8; every variant is used by some row. `variant_slot`: each slot holds exactly one variant.
All inputs are finite; a program needn't handle non-finite values.
Results may differ from the reference program's by a relative error of at most 0.0063.
Values may be sent and summed in bfloat16 or wider, within the bound.
No kernel may reach another device: no remote copies, remote signals or barrier semaphores. Data moves between devices by JAX's collectives and lax.ppermute only.
A program may use at most 192 MiB of HBM per device.

```python
import math
import jax
import jax.numpy as jnp
import numpy as np
from jax import lax

D = 8192
FF = 16384
RANK = 16
MOST = 8
ROW_DEV = 8
ROWS = 64
VARIANTS = 32
N_FF = 8


def shard_levels(rng, shape, shards, low, high):
    loudness, own = 1.0, jax.random.fold_in(rng, 6)
    for axis_at, blocks in shards:
        draws = jnp.exp(jax.random.uniform(jax.random.fold_in(own, axis_at), (blocks,), jnp.float32, low / len(shards), high / len(shards)))
        loudness = loudness * jnp.repeat(draws, shape[axis_at] // blocks).reshape([-1 if axis == axis_at else 1 for axis in range(len(shape))])
    return loudness


def assign_block(own_key, own, number, rows, amount, top, most, skew):
    ranking = jax.random.permutation(own_key, amount)
    packed, ordinary = portions_of(amount, rows * top, most, skew, True), portions_of(amount, rows * top, most, skew, False)
    places = jnp.arange(amount)

    def named(sizes, rotation):
        used = int((sizes > 0).sum())
        fixed = max(1, used // 4)
        passed = fixed + (places - fixed + rotation * (used - fixed)) % max(1, amount - fixed)
        return jnp.zeros((amount,), jnp.int32).at[ranking[jnp.where(places < fixed, places, passed)]].set(jnp.asarray(sizes, jnp.int32))

    sizes = jnp.where(number % 4 == 0, named(packed, number // 4), named(ordinary, number - number // 4 - 1))
    mixed = jax.random.permutation(jax.random.fold_in(own, 3), amount)
    source_of, receiver = mixed[0:amount // 2 * 2:2], mixed[1:amount // 2 * 2:2]
    slack = jnp.minimum(sizes[source_of] - 1, most - sizes[receiver]) // 2
    slack = jnp.where((source_of == ranking[0]) | (receiver == ranking[0]) | (sizes[receiver] == 0), 0, jnp.maximum(slack, 0))
    passed = jax.random.randint(jax.random.fold_in(own, 4), (amount // 2,), 0, 1 << 20) % (slack + 1)
    sizes = sizes.at[source_of].add(-passed).at[receiver].add(passed)
    items = jnp.searchsorted(jnp.cumsum(sizes), jnp.arange(rows * top), side="right").astype(jnp.int32)
    table = items.reshape(top, rows).T
    table = table[jax.random.permutation(jax.random.fold_in(own, 1), rows)]
    rotation = jax.random.randint(jax.random.fold_in(own, 2), (rows, 1), 0, top)
    return jnp.take_along_axis(table, (jnp.arange(top)[None, :] + rotation) % top, axis=1)


def portions_of(number_of, total, bound, slope, full):
    portions = [(1 << 20) // math.isqrt(grade ** slope) + 1 for grade in range(1, number_of + 1)]
    largest = bound if full else min(bound, max(-(-total // number_of), total * portions[0] // sum(portions)))
    least = 1 if total - largest >= number_of - 1 else 0
    given, spare = [largest] + [least] * (number_of - 1), total - largest - least * (number_of - 1)
    while spare > 0:
        movable = [i for i in range(1, number_of) if given[i] < largest] or [i for i in range(1, number_of) if given[i] < bound]
        whole, remaining = sum([portions[i] for i in movable]), spare
        for i in movable:
            extra = min(bound - given[i], max(1, remaining * portions[i] // whole), spare)
            given[i] = given[i] + extra
            spare = spare - extra
    return np.array(given)


def centred(own_key, dims, spread, reach, pieces=(), kind=jnp.bfloat16):
    factor_of = shard_levels(own_key, dims, pieces, -0.22, 0.18) if pieces else 1.0
    array = jax.random.normal(own_key, dims, jnp.float32) * spread * factor_of
    return jnp.minimum(jnp.maximum(array, -reach), reach).astype(kind)


def setup_inputs(seed: int = 0, part: int = 0) -> dict:
    keys = jax.random.split(jax.random.key(seed), 11)
    part_splits = jax.random.split(jax.random.fold_in(keys[10], part), 11)
    tokens = centred(part_splits[0], (ROWS, D), 1.0, 6.0, ((0, 8), (1, 2)))
    gate_weight = centred(keys[1], (D, FF), D ** -0.5, 0.0625, ((0, 2), (1, 8)))
    up_weight = centred(keys[2], (D, FF), D ** -0.5, 0.0625, ((0, 2), (1, 8)))
    down_weight = centred(keys[3], (FF, D), FF ** -0.5, 0.046875, ((0, 8), (1, 2)))
    shrink_gu = centred(part_splits[4], (VARIANTS, 2 * RANK, D), D ** -0.5, 0.0625, ((0, 8), (2, 2)))
    expand_gu = centred(part_splits[5], (VARIANTS, 2, RANK, FF), 0.25, 1.5, ((0, 8), (2, 2)))
    shrink_down = centred(part_splits[6], (VARIANTS, RANK, FF), FF ** -0.5, 0.046875, ((0, 8),))
    expand_down = centred(part_splits[7], (VARIANTS, RANK, D), 0.25, 1.5, ((0, 8), (2, 2)))
    variant_ids_keys = jax.random.split(jax.random.fold_in(part_splits[8], 1), ROWS // ROWS)
    variant_ids_turns = jax.random.permutation(jax.random.fold_in(part_splits[8], 3), ROWS // ROWS)
    variant_ids = jax.vmap(lambda own, number: assign_block(jax.random.fold_in(part_splits[8], 2), own, number, ROWS, VARIANTS, 1, MOST, 2))(variant_ids_keys, variant_ids_turns).reshape((ROWS, 1))
    variant_slot = jax.random.permutation(part_splits[9], VARIANTS).astype(jnp.int32)
    return dict(tokens=tokens, gate_weight=gate_weight, up_weight=up_weight, down_weight=down_weight, shrink_gu=shrink_gu, expand_gu=expand_gu, shrink_down=shrink_down, expand_down=expand_down, variant_ids=variant_ids, variant_slot=variant_slot)


def slot_of_rows(variant_ids, variant_slot):
    matches = variant_ids[:, 0][:, None] == jnp.arange(VARIANTS, dtype=jnp.int32)[None, :]
    return jnp.sum(jnp.where(matches, variant_slot[None, :], 0), axis=1).astype(jnp.int32)


def reference(tokens, gate_weight, up_weight, down_weight, shrink_gu, expand_gu, shrink_down, expand_down, variant_ids, variant_slot):
    slot_row = slot_of_rows(variant_ids, variant_slot)
    slot_blocks = slot_row.reshape(N_FF, ROW_DEV)

    def shrink_block(block_args):
        token_block, slot_block = block_args
        factor_block = shrink_gu[slot_block].astype(jnp.float32)
        return jnp.einsum("td,tjd->tj", token_block.astype(jnp.float32), factor_block)

    low_in = lax.map(shrink_block, (tokens.reshape(N_FF, ROW_DEV, D), slot_blocks))
    low_in = low_in.reshape(ROWS, 2, RANK).astype(jnp.bfloat16)

    def expand_block(block_args):
        low_block, slot_block = block_args
        factor_block = expand_gu[slot_block].astype(jnp.float32)
        return jnp.einsum("tgk,tgkf->tgf", low_block.astype(jnp.float32), factor_block)

    delta_gu = lax.map(expand_block, (low_in.reshape(N_FF, ROW_DEV, 2, RANK), slot_blocks)).reshape(ROWS, 2, FF)
    gate = jnp.dot(tokens, gate_weight, preferred_element_type=jnp.float32) + delta_gu[:, 0]
    up_value = jnp.dot(tokens, up_weight, preferred_element_type=jnp.float32) + delta_gu[:, 1]
    hidden = (jax.nn.silu(gate) * up_value).astype(jnp.bfloat16)

    def down_shrink_block(block_args):
        hidden_block, slot_block = block_args
        factor_block = shrink_down[slot_block].astype(jnp.float32)
        return jnp.einsum("tf,tkf->tk", hidden_block.astype(jnp.float32), factor_block)

    low_out = lax.map(down_shrink_block, (hidden.reshape(N_FF, ROW_DEV, FF), slot_blocks))
    low_out = low_out.reshape(ROWS, RANK).astype(jnp.bfloat16)

    def down_expand_block(block_args):
        low_block, slot_block = block_args
        factor_block = expand_down[slot_block].astype(jnp.float32)
        return jnp.einsum("tk,tkd->td", low_block.astype(jnp.float32), factor_block)

    delta_out = lax.map(down_expand_block, (low_out.reshape(N_FF, ROW_DEV, RANK), slot_blocks)).reshape(ROWS, D)
    base_out = jnp.dot(hidden, down_weight, preferred_element_type=jnp.float32)
    return (base_out + delta_out).astype(jnp.bfloat16)
```

```python
import functools

import jax
import jax.numpy as jnp
from jax import lax
from jax.experimental import pallas as pl
from jax.experimental.pallas import tpu as pltpu
from jax.sharding import PartitionSpec as P

MOST = 8
BF = jnp.bfloat16
F32 = jnp.float32
MIB = 1024 * 1024


def dot(a, b):
    return jnp.dot(a, b, preferred_element_type=F32)


def dot_last(a, b):
    return lax.dot_general(a, b, (((1,), (1,)), ((), ())), preferred_element_type=F32)


def params(mib):
    return pltpu.CompilerParams(vmem_limit_bytes=mib * MIB)


def cost(flops, moved):
    return pl.CostEstimate(flops=flops, bytes_accessed=moved, transcendentals=0)


def copy_kernel(core_ref, in_ref, out_ref):
    out_ref[...] = in_ref[...]


def other_half(core, factors, shards, half):
    depth = factors.shape[0]
    return pl.pallas_call(
        copy_kernel,
        out_shape=jax.ShapeDtypeStruct((depth, shards * half), factors.dtype),
        grid_spec=pltpu.PrefetchScalarGridSpec(
            num_scalar_prefetch=1,
            grid=(shards,),
            in_specs=[pl.BlockSpec((depth, half), lambda j, core: (0, 2 * j + 1 - core[0]))],
            out_specs=pl.BlockSpec((depth, half), lambda j, core: (0, j)),
        ),
        compiler_params=params(8),
        cost_estimate=cost(0, 4 * depth * shards * half),
    )(core, factors)


def low_in_kernel(x_ref, shrink_ref, mask_ref, out_ref):
    pairs = dot_last(x_ref[...], shrink_ref[...])
    out_ref[...] = jnp.where(mask_ref[...] > 0, pairs, 0.0)


def low_in_pairs(x, shrink, mask):
    rows, width = x.shape
    return pl.pallas_call(
        low_in_kernel,
        out_shape=jax.ShapeDtypeStruct(mask.shape, F32),
        compiler_params=params(16),
        cost_estimate=cost(2 * rows * width * shrink.shape[0], 2 * shrink.size + 2 * x.size),
    )(x, shrink, mask)


def expand_kernel(
    core_ref, own_ref, got_ref, pick_ref, cols_ref, near_ref, far_ref, out_ref, lhs_near, lhs_far
):
    cap = pick_ref.shape[0]

    @pl.when(pl.program_id(0) == 0)
    def _():
        low = (own_ref[...] + got_ref[...]).astype(BF)
        picked = dot(pick_ref[...], low).astype(BF)
        for kind in range(2):
            at = pl.ds(kind * cap, cap)
            lhs_near[at] = dot(picked, cols_ref[kind, 0]).astype(BF)
            lhs_far[at] = dot(picked, cols_ref[kind, 1]).astype(BF)

    delta = dot(lhs_near[...], near_ref[...]) + dot(lhs_far[...], far_ref[...])
    out_ref[0] = delta.astype(BF)


def expand_rows(core, own, got, pick, cols, near, far, shards, half):
    cap = pick.shape[0]
    depth = near.shape[0]
    whole = lambda shape: pl.BlockSpec(shape, lambda j, core: (0,) * len(shape))
    return pl.pallas_call(
        expand_kernel,
        out_shape=jax.ShapeDtypeStruct((shards, 2 * cap, half), BF),
        grid_spec=pltpu.PrefetchScalarGridSpec(
            num_scalar_prefetch=1,
            grid=(shards,),
            in_specs=[
                whole(own.shape),
                whole(got.shape),
                whole(pick.shape),
                whole(cols.shape),
                pl.BlockSpec((depth, half), lambda j, core: (0, 2 * j + core[0])),
                pl.BlockSpec((depth, half), lambda j, core: (0, j)),
            ],
            out_specs=pl.BlockSpec((1, 2 * cap, half), lambda j, core: (j, 0, 0)),
            scratch_shapes=[pltpu.VMEM((2 * cap, depth), BF), pltpu.VMEM((2 * cap, depth), BF)],
        ),
        compiler_params=params(16),
        cost_estimate=cost(8 * cap * depth * shards * half, 4 * (depth + cap) * shards * half),
    )(core, own, got, pick, cols, near, far)


def base_kernel(side_ref, x_ref, gate_ref, up_ref, out_ref):
    out_ref[0] = dot(x_ref[...], gate_ref[...]).astype(out_ref.dtype)
    out_ref[1] = dot(x_ref[...], up_ref[...]).astype(out_ref.dtype)


def base_half(side, x, gate_weight, up_weight, half, kind):
    rows, width = x.shape
    block = min(256, half)
    steps = half // block
    weight = pl.BlockSpec((width, block), lambda n, side: (0, side[0] * steps + n))
    return pl.pallas_call(
        base_kernel,
        out_shape=jax.ShapeDtypeStruct((2, rows, half), kind),
        grid_spec=pltpu.PrefetchScalarGridSpec(
            num_scalar_prefetch=1,
            grid=(steps,),
            in_specs=[pl.BlockSpec((rows, width), lambda n, side: (0, 0)), weight, weight],
            out_specs=pl.BlockSpec((2, rows, block), lambda n, side: (0, 0, n)),
        ),
        compiler_params=params(24),
        cost_estimate=cost(4 * rows * width * half, 4 * width * half + 2 * rows * width),
    )(side, x, gate_weight, up_weight)


def hidden_kernel(own_ref, got_ref, delta_ref, place_ref, send_ref, hid_ref, out_ref):
    rows = hid_ref.shape[0]
    delta = dot(place_ref[...], delta_ref[...])
    gate = own_ref[0] + got_ref[0].astype(F32) + delta[:rows]
    up = own_ref[1] + got_ref[1].astype(F32) + delta[rows:]
    hidden = (gate / (1.0 + jnp.exp(-gate)) * up).astype(BF)
    hid_ref[...] = hidden
    out_ref[...] = dot(send_ref[...], hidden).astype(BF)


def hidden_half(own, got, delta, place, send):
    rows, half = own.shape[1:]
    block = min(256, half)
    cells = send.shape[0]
    return pl.pallas_call(
        hidden_kernel,
        out_shape=(
            jax.ShapeDtypeStruct((rows, half), BF),
            jax.ShapeDtypeStruct((cells, half), BF),
        ),
        grid=(half // block,),
        in_specs=[
            pl.BlockSpec((2, rows, block), lambda n: (0, 0, n)),
            pl.BlockSpec((2, rows, block), lambda n: (0, 0, n)),
            pl.BlockSpec((delta.shape[0], block), lambda n: (0, n)),
            pl.BlockSpec(place.shape, lambda n: (0, 0)),
            pl.BlockSpec(send.shape, lambda n: (0, 0)),
        ],
        out_specs=(
            pl.BlockSpec((rows, block), lambda n: (0, n)),
            pl.BlockSpec((cells, block), lambda n: (0, n)),
        ),
        compiler_params=params(40),
        cost_estimate=cost(
            2 * half * (place.size + send.size), 2 * half * (6 * rows + delta.shape[0] + cells)
        ),
    )(own, got, delta, place, send)


def down_kernel(core_ref, near_ref, far_ref, near_weight, far_weight, out_ref):
    out_ref[...] = dot(near_ref[...], near_weight[...]) + dot(far_ref[...], far_weight[...])


def down_base(core, near, far, weight):
    rows, half = near.shape
    width = weight.shape[1]
    block = min(512, width)
    return pl.pallas_call(
        down_kernel,
        out_shape=jax.ShapeDtypeStruct((rows, width), F32),
        grid_spec=pltpu.PrefetchScalarGridSpec(
            num_scalar_prefetch=1,
            grid=(width // block,),
            in_specs=[
                pl.BlockSpec((rows, half), lambda n, core: (0, 0)),
                pl.BlockSpec((rows, half), lambda n, core: (0, 0)),
                pl.BlockSpec((half, block), lambda n, core: (core[0], n)),
                pl.BlockSpec((half, block), lambda n, core: (1 - core[0], n)),
            ],
            out_specs=pl.BlockSpec((rows, block), lambda n, core: (0, n)),
        ),
        compiler_params=params(24),
        cost_estimate=cost(4 * rows * half * width, 4 * half * width + 4 * rows * width),
    )(core, near, far, weight, weight)


def low_out_kernel(core_ref, hid_ref, shrink_ref, mask_ref, out_ref):
    step = pl.program_id(0)

    @pl.when(step == 0)
    def _():
        out_ref[...] = jnp.zeros_like(out_ref)

    out_ref[...] += dot_last(hid_ref[0], shrink_ref[...])

    @pl.when(step == pl.num_programs(0) - 1)
    def _():
        out_ref[...] = jnp.where(mask_ref[...] > 0, out_ref[...], 0.0)


def low_out_pairs(core, hidden, shrink, mask):
    shards, cap, half = hidden.shape
    depth = shrink.shape[0]
    return pl.pallas_call(
        low_out_kernel,
        out_shape=jax.ShapeDtypeStruct((cap, depth), F32),
        grid_spec=pltpu.PrefetchScalarGridSpec(
            num_scalar_prefetch=1,
            grid=(shards,),
            in_specs=[
                pl.BlockSpec((1, cap, half), lambda j, core: (j, 0, 0)),
                pl.BlockSpec((depth, half), lambda j, core: (0, 2 * j + core[0])),
                pl.BlockSpec(mask.shape, lambda j, core: (0, 0)),
            ],
            out_specs=pl.BlockSpec((cap, depth), lambda j, core: (0, 0)),
        ),
        compiler_params=params(8),
        cost_estimate=cost(2 * cap * depth * shards * half, 2 * shards * half * (depth + cap)),
    )(core, hidden, shrink, mask)


def add_kernel(base_ref, own_ref, got_ref, pick_ref, expand_ref, out_ref):
    low = (own_ref[...] + got_ref[...]).astype(BF)
    spread = lax.dot_general(
        pick_ref[...], low, (((0,), (0,)), ((), ())), preferred_element_type=F32
    ).astype(BF)
    out_ref[...] = (base_ref[...] + dot(spread, expand_ref[...])).astype(BF)


def add_delta(base, own, got, pick, expand):
    rows, width = base.shape
    block = min(1024, width)
    depth = expand.shape[0]
    fixed = lambda shape: pl.BlockSpec(shape, lambda n: (0, 0))
    return pl.pallas_call(
        add_kernel,
        out_shape=jax.ShapeDtypeStruct((rows, width), BF),
        grid=(width // block,),
        in_specs=[
            pl.BlockSpec((rows, block), lambda n: (0, n)),
            fixed(own.shape),
            fixed(got.shape),
            fixed(pick.shape),
            pl.BlockSpec((depth, block), lambda n: (0, n)),
        ],
        out_specs=pl.BlockSpec((rows, block), lambda n: (0, n)),
        compiler_params=params(24),
        cost_estimate=cost(2 * rows * depth * width, width * (6 * rows + 2 * depth)),
    )(base, own, got, pick, expand)


def per_device(
    tokens,
    gate_weight,
    up_weight,
    down_weight,
    shrink_gu,
    expand_gu,
    shrink_down,
    expand_down,
    variant_ids,
    variant_slot,
):
    shards = lax.axis_size("ff")
    me = lax.axis_index("ff")
    core = lax.axis_index("var")
    own_rows, width = tokens.shape
    rows = own_rows * shards
    slots = shrink_gu.shape[0]
    variants = variant_slot.shape[0]
    rank = shrink_down.shape[1]
    half_rank = expand_gu.shape[2]
    half = gate_weight.shape[1] // 2
    cap = min(slots * MOST, rows)
    first = me * slots
    here = core.astype(jnp.int32).reshape(1)
    there = 1 - here
    swap = lambda a: lax.ppermute(a, "var", [(0, 1), (1, 0)])
    spread = lambda a: lax.all_to_all(a, "ff", split_axis=0, concat_axis=0, tiled=True)

    x = spread(jnp.broadcast_to(tokens, (shards, own_rows, width))).reshape(rows, width)

    near = expand_gu.reshape(slots * 2 * half_rank, -1)
    far = swap(other_half(here, near, shards, half))

    ids = variant_ids[:, 0]
    matches = ids[:, None] == jnp.arange(variants, dtype=jnp.int32)[None, :]
    slot_row = jnp.sum(jnp.where(matches, variant_slot[None, :], 0), axis=1)
    owner = slot_row // slots
    order = jnp.arange(rows, dtype=jnp.int32)
    earlier = (owner[:, None] == owner[None, :]) & (order[None, :] < order[:, None])
    place = jnp.sum(earlier.astype(jnp.int32), axis=1)
    cells = jnp.arange(shards * cap, dtype=jnp.int32)
    cell = owner * cap + place
    send_rows = (cells[:, None] == cell[None, :]).astype(BF)
    kinds = jnp.arange(2, dtype=jnp.int32)
    kind_cell = (owner * 2 + kinds[:, None]) * cap + place
    kind_cells = jnp.arange(2 * shards * cap, dtype=jnp.int32)
    place_rows = (kind_cell.reshape(-1)[:, None] == kind_cells[None, :]).astype(BF)
    spots = jnp.arange(cap, dtype=jnp.int32)
    picked = (spots[:, None] == place[None, :]) & (owner[None, :] == me)
    pick = picked.astype(BF)
    local = slot_row - first
    in_cols = jnp.arange(slots * 2 * rank, dtype=jnp.int32)
    mask_in = (local[:, None] == (in_cols // (2 * rank))[None, :]).astype(F32)
    spot_slot = jnp.sum(jnp.where(picked, local[None, :] + 1, 0), axis=1) - 1
    out_cols = jnp.arange(slots * rank, dtype=jnp.int32)
    mask_out = (spot_slot[:, None] == (out_cols // rank)[None, :]).astype(F32)
    rank_at = in_cols % rank
    kind_at = in_cols // rank % 2
    row_at = in_cols // (2 * rank) * (2 * half_rank) + kind_at * half_rank + rank_at % half_rank
    near_cols = jnp.arange(slots * 2 * half_rank, dtype=jnp.int32)
    hit = row_at[:, None] == near_cols[None, :]
    side = jnp.stack([core, 1 - core])
    cols = (
        hit[None, None]
        & (kind_at[None, :] == kinds[:, None])[:, None, :, None]
        & ((rank_at // half_rank)[None, :] == side[:, None])[None, :, :, None]
    ).astype(BF)

    low_own = low_in_pairs(x, shrink_gu.reshape(slots * 2 * rank, width), mask_in)
    low_got = swap(low_own)
    base_got = swap(base_half(there, x, gate_weight, up_weight, half, BF))
    delta = spread(
        expand_rows(here, low_own, low_got, pick, cols, near, far, shards, half)
    ).reshape(2 * shards * cap, half)
    base_own = base_half(here, x, gate_weight, up_weight, half, F32)
    hidden, hidden_send = hidden_half(base_own, base_got, delta, place_rows, send_rows)
    hidden_far = swap(hidden)
    hidden_rows = spread(hidden_send.reshape(shards, cap, half))
    base = down_base(here, hidden, hidden_far, down_weight)
    out_own = low_out_pairs(here, hidden_rows, shrink_down.reshape(slots * rank, -1), mask_out)
    out_got = swap(out_own)
    partial = add_delta(base, out_own, out_got, pick, expand_down.reshape(slots * rank, width))
    parts = spread(partial.reshape(shards, own_rows, width))
    return jnp.sum(parts.astype(F32), axis=0).astype(BF)


def solution(mesh):
    placed = (
        P(("groups", "ff"), "var"),
        P("var", "ff"),
        P("var", "ff"),
        P("ff", "var"),
        P(("groups", "ff"), None, "var"),
        P(("groups", "ff"), None, "var", None),
        P(("groups", "ff"), None, None),
        P(("groups", "ff"), None, "var"),
        P("groups", None),
        P("groups"),
    )
    return jax.shard_map(
        per_device,
        mesh=mesh,
        in_specs=placed,
        out_specs=P(("groups", "ff"), "var"),
        check_vma=False,
    )
```

```python
import jax
import jax.numpy as jnp
from jax import lax
from jax.experimental import pallas as pl
from jax.experimental.pallas import tpu as pltpu
from jax.sharding import PartitionSpec as P

MOST = 8
DIRECT = 8
BF = jnp.bfloat16
F32 = jnp.float32
I32 = jnp.int32
MIB = 1024 * 1024


def dot(a, b):
    return jnp.dot(a, b, preferred_element_type=F32)


def dot_last(a, b):
    return lax.dot_general(a, b, (((1,), (1,)), ((), ())), preferred_element_type=F32)


def params(mib):
    return pltpu.CompilerParams(vmem_limit_bytes=mib * MIB)


def cost(flops, moved):
    return pl.CostEstimate(flops=flops, bytes_accessed=moved, transcendentals=0)


def fixed(array):
    zeros = (0,) * array.ndim
    return pl.BlockSpec(array.shape, lambda *_: zeros)


class Ways:
    def __init__(self):
        self.shards = lax.axis_size("ff")
        self.fast = 2 if self.shards % 2 == 0 else 1
        self.slow = self.shards // self.fast
        self.direct = self.shards <= DIRECT
        me = lax.axis_index("ff").astype(I32)
        steps = jnp.arange(self.shards, dtype=I32)
        if self.direct:
            slow = (me // self.fast - steps // self.fast) % self.slow
            fast = (me % self.fast - steps % self.fast) % self.fast
            self.order = slow * self.fast + fast
        else:
            self.order = steps

    def back(self, a, c):
        S, F = self.slow, self.fast
        return [(s * F + f, (s - a) % S * F + (f - c) % F) for s in range(S) for f in range(F)]

    def gather(self, block):
        if not self.direct:
            return list(lax.all_gather(block, "ff"))
        got = [None] * self.shards
        for a in range(self.slow):
            got[a * self.fast] = lax.ppermute(block, "ff", self.back(-a, 0)) if a else block
        for a in range(self.slow):
            for c in range(1, self.fast):
                got[a * self.fast + c] = lax.ppermute(
                    got[a * self.fast], "ff", self.back(0, -c)
                )
        return got

    def deliver(self, blocks):
        if not self.direct:
            return list(lax.all_to_all(jnp.stack(blocks), "ff", 0, 0, tiled=True))
        got = [None] * self.shards
        got[0] = blocks[0]
        for b in range(1, self.shards):
            a, c = b // self.fast, b % self.fast
            back = (-a) % self.slow * self.fast + (-c) % self.fast
            got[back] = lax.ppermute(blocks[b], "ff", self.back(a, c))
        return got


def copy_kernel(at_ref, in_ref, out_ref):
    out_ref[...] = in_ref[...]


def pick_columns(at, factors, half):
    depth, count = factors.shape[0], at.shape[0]
    return pl.pallas_call(
        copy_kernel,
        out_shape=jax.ShapeDtypeStruct((depth, count * half), factors.dtype),
        grid_spec=pltpu.PrefetchScalarGridSpec(
            num_scalar_prefetch=1,
            grid=(count,),
            in_specs=[pl.BlockSpec((depth, half), lambda j, at: (0, at[j]))],
            out_specs=pl.BlockSpec((depth, half), lambda j, at: (0, j)),
        ),
        compiler_params=params(8),
        cost_estimate=cost(0, 4 * depth * count * half),
    )(at, factors)


def low_in_kernel(count, shrink_ref, mask_ref, *refs):
    parts, x_ref, out_ref = refs[:count], refs[count], refs[count + 1]
    x = jnp.concatenate([part[...].astype(F32) for part in parts], axis=0).astype(BF)
    x_ref[...] = x

    @pl.when(pl.program_id(0) == 0)
    def _():
        out_ref[...] = jnp.zeros_like(out_ref)

    out_ref[...] += jnp.where(mask_ref[...] > 0, dot_last(x, shrink_ref[...]), 0.0)


def low_in_pairs(parts, shrink, mask):
    count = len(parts)
    own_rows, width = parts[0].shape
    rows, block = count * own_rows, min(1024, width)
    return pl.pallas_call(
        lambda *refs: low_in_kernel(count, *refs),
        out_shape=(
            jax.ShapeDtypeStruct((rows, width), BF),
            jax.ShapeDtypeStruct(mask.shape, F32),
        ),
        grid=(width // block,),
        in_specs=[pl.BlockSpec((shrink.shape[0], block), lambda n: (0, n)), fixed(mask)]
        + [pl.BlockSpec((own_rows, block), lambda n: (0, n))] * count,
        out_specs=(pl.BlockSpec((rows, block), lambda n: (0, n)), fixed(mask)),
        compiler_params=params(16),
        cost_estimate=cost(2 * rows * width * shrink.shape[0], 2 * shrink.size + 4 * rows * width),
    )(shrink, mask, *parts)


def expand_kernel(count, at_ref, own_ref, got_ref, pick_ref, cols_ref, far_ref, *refs):
    near_refs, out_refs = refs[:count], refs[count:]
    cap = pick_ref.shape[0]
    half = out_refs[0].shape[1]
    low = (own_ref[...] + got_ref[...]).astype(BF)
    picked = dot(pick_ref[...], low).astype(BF)
    lhs = [
        jnp.concatenate([dot(picked, cols_ref[kind, side]) for kind in range(2)], axis=0)
        for side in range(2)
    ]
    lhs = [side.astype(BF) for side in lhs]
    for b in range(count):
        far = far_ref[:, b * half : (b + 1) * half]
        out_refs[b][...] = (dot(lhs[0], near_refs[b][...]) + dot(lhs[1], far)).astype(BF)


def expand_rows(at, own, got, pick, cols, near, far, half):
    cap, count, depth = pick.shape[0], at.shape[0], near.shape[0]
    column = lambda b: pl.BlockSpec((depth, half), lambda i, at: (0, at[b]))
    out = jax.ShapeDtypeStruct((2 * cap, half), BF)
    return pl.pallas_call(
        lambda *refs: expand_kernel(count, *refs),
        out_shape=(out,) * count,
        grid_spec=pltpu.PrefetchScalarGridSpec(
            num_scalar_prefetch=1,
            grid=(1,),
            in_specs=[fixed(own), fixed(got), fixed(pick), fixed(cols), fixed(far)]
            + [column(b) for b in range(count)],
            out_specs=(fixed(out),) * count,
        ),
        compiler_params=params(16),
        cost_estimate=cost(8 * cap * depth * count * half, 4 * (depth + cap) * count * half),
    )(at, own, got, pick, cols, far, *[near] * count)


def base_kernel(side_ref, x_ref, gate_ref, up_ref, out_ref, gate_sum, up_sum):
    step = pl.program_id(0)

    @pl.when(step == 0)
    def _():
        gate_sum[...] = jnp.zeros_like(gate_sum)
        up_sum[...] = jnp.zeros_like(up_sum)

    gate_sum[...] += dot(x_ref[...], gate_ref[...])
    up_sum[...] += dot(x_ref[...], up_ref[...])

    @pl.when(step == pl.num_programs(0) - 1)
    def _():
        out_ref[0] = gate_sum[...].astype(out_ref.dtype)
        out_ref[1] = up_sum[...].astype(out_ref.dtype)


def base_half(side, x, gate_weight, up_weight, half, kind):
    rows, width = x.shape
    block = min(512, width)
    weight = pl.BlockSpec((block, half), lambda n, side: (n, side[0]))
    return pl.pallas_call(
        base_kernel,
        out_shape=jax.ShapeDtypeStruct((2, rows, half), kind),
        grid_spec=pltpu.PrefetchScalarGridSpec(
            num_scalar_prefetch=1,
            grid=(width // block,),
            in_specs=[pl.BlockSpec((rows, block), lambda n, side: (0, n)), weight, weight],
            out_specs=pl.BlockSpec((2, rows, half), lambda n, side: (0, 0, 0)),
            scratch_shapes=[pltpu.VMEM((rows, half), F32), pltpu.VMEM((rows, half), F32)],
        ),
        compiler_params=params(56),
        cost_estimate=cost(4 * rows * width * half, 4 * width * half + 2 * rows * width),
    )(side, x, gate_weight, up_weight)


def hidden_kernel(count, own_ref, got_ref, place_ref, send_ref, *refs):
    parts, hid_ref, out_refs = refs[:count], refs[count], refs[count + 1 :]
    rows = hid_ref.shape[0]
    cap = out_refs[0].shape[0]
    delta = dot(place_ref[...], jnp.concatenate([part[...] for part in parts], axis=0))
    gate = own_ref[0] + got_ref[0].astype(F32) + delta[:rows]
    up = own_ref[1] + got_ref[1].astype(F32) + delta[rows:]
    hidden = (gate / (1.0 + jnp.exp(-gate)) * up).astype(BF)
    hid_ref[...] = hidden
    sent = dot(send_ref[...], hidden).astype(BF)
    for b in range(count):
        out_refs[b][...] = sent[b * cap : (b + 1) * cap]


def hidden_half(own, got, parts, place, send):
    count = len(parts)
    rows, half = own.shape[1:]
    block = min(256, half)
    cap = send.shape[0] // count
    both = pl.BlockSpec((2, rows, block), lambda n: (0, 0, n))
    flat = lambda depth: pl.BlockSpec((depth, block), lambda n: (0, n))
    return pl.pallas_call(
        lambda *refs: hidden_kernel(count, *refs),
        out_shape=(jax.ShapeDtypeStruct((rows, half), BF),)
        + (jax.ShapeDtypeStruct((cap, half), BF),) * count,
        grid=(half // block,),
        in_specs=[both, both, fixed(place), fixed(send)] + [flat(parts[0].shape[0])] * count,
        out_specs=(flat(rows),) + (flat(cap),) * count,
        compiler_params=params(40),
        cost_estimate=cost(
            2 * half * (place.size + send.size), 2 * half * (6 * rows + 3 * count * cap)
        ),
    )(own, got, place, send, *parts)


def down_kernel(core_ref, near_ref, far_ref, near_weight, far_weight, out_ref):
    out_ref[...] = dot(near_ref[...], near_weight[...]) + dot(far_ref[...], far_weight[...])


def down_base(core, near, far, weight):
    rows, half = near.shape
    width = weight.shape[1]
    block = min(512, width)
    return pl.pallas_call(
        down_kernel,
        out_shape=jax.ShapeDtypeStruct((rows, width), F32),
        grid_spec=pltpu.PrefetchScalarGridSpec(
            num_scalar_prefetch=1,
            grid=(width // block,),
            in_specs=[
                fixed(near),
                fixed(far),
                pl.BlockSpec((half, block), lambda n, core: (core[0], n)),
                pl.BlockSpec((half, block), lambda n, core: (1 - core[0], n)),
            ],
            out_specs=pl.BlockSpec((rows, block), lambda n, core: (0, n)),
        ),
        compiler_params=params(56),
        cost_estimate=cost(4 * rows * half * width, 4 * half * width + 4 * rows * width),
    )(core, near, far, weight, weight)


def low_out_kernel(count, at_ref, mask_ref, *refs):
    parts, shrinks, out_ref = refs[:count], refs[count : 2 * count], refs[2 * count]
    pairs = sum(dot_last(part[...], shrink[...]) for part, shrink in zip(parts, shrinks))
    out_ref[...] = jnp.where(mask_ref[...] > 0, pairs, 0.0)


def low_out_pairs(at, parts, shrink, mask):
    count = len(parts)
    cap, half = parts[0].shape
    depth = shrink.shape[0]
    column = lambda b: pl.BlockSpec((depth, half), lambda i, at: (0, at[b]))
    return pl.pallas_call(
        lambda *refs: low_out_kernel(count, *refs),
        out_shape=jax.ShapeDtypeStruct((cap, depth), F32),
        grid_spec=pltpu.PrefetchScalarGridSpec(
            num_scalar_prefetch=1,
            grid=(1,),
            in_specs=[fixed(mask)]
            + [fixed(part) for part in parts]
            + [column(b) for b in range(count)],
            out_specs=fixed(mask),
        ),
        compiler_params=params(16),
        cost_estimate=cost(2 * cap * depth * count * half, 2 * count * half * (depth + cap)),
    )(at, mask, *parts, *[shrink] * count)


def add_kernel(base_ref, own_ref, got_ref, pick_ref, expand_ref, *out_refs):
    low = (own_ref[...] + got_ref[...]).astype(BF)
    spread = lax.dot_general(
        pick_ref[...], low, (((0,), (0,)), ((), ())), preferred_element_type=F32
    ).astype(BF)
    total = base_ref[...] + dot(spread, expand_ref[...])
    own_rows = out_refs[0].shape[0]
    for b, out_ref in enumerate(out_refs):
        out_ref[...] = total[b * own_rows : (b + 1) * own_rows].astype(BF)


def add_delta(base, own, got, pick, expand, count):
    rows, width = base.shape
    block = min(1024, width)
    depth = expand.shape[0]
    flat = lambda tall: pl.BlockSpec((tall, block), lambda n: (0, n))
    return pl.pallas_call(
        add_kernel,
        out_shape=(jax.ShapeDtypeStruct((rows // count, width), BF),) * count,
        grid=(width // block,),
        in_specs=[flat(rows), fixed(own), fixed(got), fixed(pick), flat(depth)],
        out_specs=(flat(rows // count),) * count,
        compiler_params=params(24),
        cost_estimate=cost(2 * rows * depth * width, width * (6 * rows + 2 * depth)),
    )(base, own, got, pick, expand)


def per_device(
    tokens,
    gate_weight,
    up_weight,
    down_weight,
    shrink_gu,
    expand_gu,
    shrink_down,
    expand_down,
    variant_ids,
    variant_slot,
):
    ways = Ways()
    shards, order = ways.shards, ways.order
    me = lax.axis_index("ff").astype(I32)
    core = lax.axis_index("var").astype(I32)
    own_rows, width = tokens.shape
    rows = own_rows * shards
    slots = shrink_gu.shape[0]
    variants = variant_slot.shape[0]
    rank = shrink_down.shape[1]
    half_rank = expand_gu.shape[2]
    half = gate_weight.shape[1] // 2
    cap = min(slots * MOST, rows)
    here = core.reshape(1)
    there = 1 - here
    at_here = 2 * order + core
    at_there = 2 * order + 1 - core
    swap = lambda a: lax.ppermute(a, "var", [(0, 1), (1, 0)])

    token_parts = ways.gather(tokens)

    near = expand_gu.reshape(slots * 2 * half_rank, -1)
    far = swap(pick_columns(at_there, near, half))

    ids = variant_ids[:, 0]
    matches = ids[:, None] == jnp.arange(variants, dtype=I32)[None, :]
    slot_row = jnp.sum(jnp.where(matches, variant_slot[None, :], 0), axis=1)
    owner = slot_row // slots
    index = jnp.arange(rows, dtype=I32)
    earlier = (owner[:, None] == owner[None, :]) & (index[None, :] < index[:, None])
    place = jnp.sum(earlier.astype(I32), axis=1)
    where_row = order[:, None] == jnp.arange(shards, dtype=I32)[None, :]
    turn = lambda a: jnp.sum(
        jnp.where(where_row[:, :, None], a.reshape(1, shards, own_rows), 0), axis=1
    ).reshape(rows)
    slot_row, place = turn(slot_row), turn(place)
    owner = slot_row // slots
    step = jnp.sum(
        jnp.where(owner[:, None] == order[None, :], jnp.arange(shards, dtype=I32)[None, :], 0),
        axis=1,
    )
    cells = jnp.arange(shards * cap, dtype=I32)
    send_rows = (cells[:, None] == (step * cap + place)[None, :]).astype(BF)
    kinds = jnp.arange(2, dtype=I32)
    kind_cell = (step * 2 + kinds[:, None]) * cap + place
    kind_cells = jnp.arange(2 * shards * cap, dtype=I32)
    place_rows = (kind_cell[:, :, None] == kind_cells).astype(BF).reshape(2 * rows, -1)
    spots = jnp.arange(cap, dtype=I32)
    picked = (spots[:, None] == place[None, :]) & (owner[None, :] == me)
    pick = picked.astype(BF)
    local = slot_row - me * slots
    in_cols = jnp.arange(slots * 2 * rank, dtype=I32)
    mask_in = (local[:, None] == (in_cols // (2 * rank))[None, :]).astype(F32)
    spot_slot = jnp.sum(jnp.where(picked, local[None, :] + 1, 0), axis=1) - 1
    out_cols = jnp.arange(slots * rank, dtype=I32)
    mask_out = (spot_slot[:, None] == (out_cols // rank)[None, :]).astype(F32)
    rank_at = in_cols % rank
    kind_at = in_cols // rank % 2
    row_at = in_cols // (2 * rank) * (2 * half_rank) + kind_at * half_rank + rank_at % half_rank
    near_cols = jnp.arange(slots * 2 * half_rank, dtype=I32)
    hit = row_at[:, None] == near_cols[None, :]
    side = jnp.stack([core, 1 - core])
    cols = (
        hit[None, None]
        & (kind_at[None, :] == kinds[:, None])[:, None, :, None]
        & ((rank_at // half_rank)[None, :] == side[:, None])[None, :, :, None]
    ).astype(BF)

    x, low_own = low_in_pairs(token_parts, shrink_gu.reshape(slots * 2 * rank, width), mask_in)
    low_got = swap(low_own)
    base_got = swap(base_half(there, x, gate_weight, up_weight, half, BF))
    delta = ways.deliver(expand_rows(at_here, low_own, low_got, pick, cols, near, far, half))
    base_own = base_half(here, x, gate_weight, up_weight, half, F32)
    hidden, *sent = hidden_half(base_own, base_got, delta, place_rows, send_rows)
    hidden_far = swap(hidden)
    hidden_rows = ways.deliver(sent)
    base = down_base(here, hidden, hidden_far, down_weight)
    out_own = low_out_pairs(at_here, hidden_rows, shrink_down.reshape(slots * rank, -1), mask_out)
    out_got = swap(out_own)
    expand = expand_down.reshape(slots * rank, width)
    parts = ways.deliver(add_delta(base, out_own, out_got, pick, expand, shards))
    return sum(part.astype(F32) for part in parts).astype(BF)


def solution(mesh):
    placed = (
        P(("groups", "ff"), "var"),
        P("var", "ff"),
        P("var", "ff"),
        P("ff", "var"),
        P(("groups", "ff"), None, "var"),
        P(("groups", "ff"), None, "var", None),
        P(("groups", "ff"), None, None),
        P(("groups", "ff"), None, "var"),
        P("groups", None),
        P("groups"),
    )
    return jax.shard_map(
        per_device,
        mesh=mesh,
        in_specs=placed,
        out_specs=P(("groups", "ff"), "var"),
        check_vma=False,
    )
```

```python
import jax
import jax.numpy as jnp
from jax import lax
from jax.experimental import pallas as pl
from jax.experimental.pallas import tpu as pltpu
from jax.sharding import PartitionSpec as P

MOST = 8
DIRECT = 8
USUAL = 16
BF = jnp.bfloat16
F32 = jnp.float32
I32 = jnp.int32
MIB = 1024 * 1024


def dot(a, b):
    return jnp.dot(a, b, preferred_element_type=F32)


def dot_last(a, b):
    return lax.dot_general(a, b, (((1,), (1,)), ((), ())), preferred_element_type=F32)


def params(mib):
    return pltpu.CompilerParams(vmem_limit_bytes=mib * MIB)


def cost(flops, moved):
    return pl.CostEstimate(flops=flops, bytes_accessed=moved, transcendentals=0)


def fixed(array):
    zeros = (0,) * array.ndim
    return pl.BlockSpec(array.shape, lambda *_: zeros)


class Ways:
    def __init__(self):
        self.shards = lax.axis_size("ff")
        self.fast = 2 if self.shards % 2 == 0 else 1
        self.slow = self.shards // self.fast
        self.direct = self.shards <= DIRECT
        me = lax.axis_index("ff").astype(I32)
        steps = jnp.arange(self.shards, dtype=I32)
        if self.direct:
            slow = (me // self.fast - steps // self.fast) % self.slow
            fast = (me % self.fast - steps % self.fast) % self.fast
            self.order = slow * self.fast + fast
        else:
            self.order = steps

    def back(self, a, c):
        S, F = self.slow, self.fast
        return [(s * F + f, (s - a) % S * F + (f - c) % F) for s in range(S) for f in range(F)]

    def gather(self, block):
        if not self.direct:
            return list(lax.all_gather(block, "ff"))
        got = [None] * self.shards
        for a in range(self.slow):
            got[a * self.fast] = lax.ppermute(block, "ff", self.back(-a, 0)) if a else block
        for a in range(self.slow):
            for c in range(1, self.fast):
                got[a * self.fast + c] = lax.ppermute(
                    got[a * self.fast], "ff", self.back(0, -c)
                )
        return got

    def deliver(self, blocks):
        if not self.direct:
            return list(lax.all_to_all(jnp.stack(blocks), "ff", 0, 0, tiled=True))
        got = [None] * self.shards
        got[0] = blocks[0]
        for b in range(1, self.shards):
            a, c = b // self.fast, b % self.fast
            back = (-a) % self.slow * self.fast + (-c) % self.fast
            got[back] = lax.ppermute(blocks[b], "ff", self.back(a, c))
        return got


def copy_kernel(at_ref, in_ref, out_ref):
    out_ref[...] = in_ref[...]


def pick_columns(at, factors, half):
    depth, count = factors.shape[0], at.shape[0]
    return pl.pallas_call(
        copy_kernel,
        out_shape=jax.ShapeDtypeStruct((depth, count * half), factors.dtype),
        grid_spec=pltpu.PrefetchScalarGridSpec(
            num_scalar_prefetch=1,
            grid=(count,),
            in_specs=[pl.BlockSpec((depth, half), lambda j, at: (0, at[j]))],
            out_specs=pl.BlockSpec((depth, half), lambda j, at: (0, j)),
        ),
        compiler_params=params(8),
        cost_estimate=cost(0, 4 * depth * count * half),
    )(at, factors)


def low_in_kernel(count, shrink_ref, mask_ref, *refs):
    parts, x_ref, out_ref = refs[:count], refs[count], refs[count + 1]
    x = jnp.concatenate([part[...].astype(F32) for part in parts], axis=0).astype(BF)
    x_ref[...] = x

    @pl.when(pl.program_id(0) == 0)
    def _():
        out_ref[...] = jnp.zeros_like(out_ref)

    out_ref[...] += jnp.where(mask_ref[...] > 0, dot_last(x, shrink_ref[...]), 0.0)


def low_in_pairs(parts, shrink, mask):
    count = len(parts)
    own_rows, width = parts[0].shape
    rows, block = count * own_rows, min(1024, width)
    return pl.pallas_call(
        lambda *refs: low_in_kernel(count, *refs),
        out_shape=(
            jax.ShapeDtypeStruct((rows, width), BF),
            jax.ShapeDtypeStruct(mask.shape, F32),
        ),
        grid=(width // block,),
        in_specs=[pl.BlockSpec((shrink.shape[0], block), lambda n: (0, n)), fixed(mask)]
        + [pl.BlockSpec((own_rows, block), lambda n: (0, n))] * count,
        out_specs=(pl.BlockSpec((rows, block), lambda n: (0, n)), fixed(mask)),
        compiler_params=params(16),
        cost_estimate=cost(2 * rows * width * shrink.shape[0], 2 * shrink.size + 4 * rows * width),
    )(shrink, mask, *parts)


def expand_kernel(count, at_ref, own_ref, got_ref, pick_ref, cols_ref, far_ref, *refs):
    near_refs, out_refs = refs[:count], refs[count:]
    cap = pick_ref.shape[0]
    half = out_refs[0].shape[1]
    low = (own_ref[...] + got_ref[...]).astype(BF)
    picked = dot(pick_ref[...], low).astype(BF)
    lhs = [
        jnp.concatenate([dot(picked, cols_ref[kind, side]) for kind in range(2)], axis=0)
        for side in range(2)
    ]
    lhs = [side.astype(BF) for side in lhs]
    for b in range(count):
        far = far_ref[:, b * half : (b + 1) * half]
        out_refs[b][...] = (dot(lhs[0], near_refs[b][...]) + dot(lhs[1], far)).astype(BF)


def expand_rows(at, own, got, pick, cols, near, far, half):
    cap, count, depth = pick.shape[0], at.shape[0], near.shape[0]
    column = lambda b: pl.BlockSpec((depth, half), lambda i, at: (0, at[b]))
    out = jax.ShapeDtypeStruct((2 * cap, half), BF)
    return pl.pallas_call(
        lambda *refs: expand_kernel(count, *refs),
        out_shape=(out,) * count,
        grid_spec=pltpu.PrefetchScalarGridSpec(
            num_scalar_prefetch=1,
            grid=(1,),
            in_specs=[fixed(own), fixed(got), fixed(pick), fixed(cols), fixed(far)]
            + [column(b) for b in range(count)],
            out_specs=(fixed(out),) * count,
        ),
        compiler_params=params(16),
        cost_estimate=cost(8 * cap * depth * count * half, 4 * (depth + cap) * count * half),
    )(at, own, got, pick, cols, far, *[near] * count)


def base_kernel(side_ref, x_ref, gate_ref, up_ref, out_ref, held, sums, sems):
    half = held.shape[2]
    chunks = sems.shape[1]
    depth = held.shape[1] // chunks
    columns = pl.ds(pl.multiple_of(side_ref[0] * half, half), half)
    copies = []
    for c in range(chunks):
        here = pl.ds(c * depth, depth)
        for kind, weight in enumerate((gate_ref, up_ref)):
            copy = pltpu.make_async_copy(
                weight.at[here, columns], held.at[kind, here], sems.at[kind, c]
            )
            copy.start()
            copies.append((kind, here, copy))
    for kind, here, copy in copies:
        copy.wait()
        part = dot(x_ref[:, here], held[kind, here])
        sums[kind] = part if here.start == 0 else sums[kind] + part
    out_ref[...] = sums[...].astype(out_ref.dtype)


def base_half(side, x, gate_weight, up_weight, half, kind):
    rows, width = x.shape
    chunks = max(width // 512, 1)
    return pl.pallas_call(
        base_kernel,
        out_shape=jax.ShapeDtypeStruct((2, rows, half), kind),
        grid_spec=pltpu.PrefetchScalarGridSpec(
            num_scalar_prefetch=1,
            grid=(1,),
            in_specs=[fixed(x), pl.BlockSpec(memory_space=pl.ANY), pl.BlockSpec(memory_space=pl.ANY)],
            out_specs=pl.BlockSpec((2, rows, half), lambda n, side: (0, 0, 0)),
            scratch_shapes=[
                pltpu.VMEM((2, width, half), BF),
                pltpu.VMEM((2, rows, half), F32),
                pltpu.SemaphoreType.DMA((2, chunks)),
            ],
        ),
        compiler_params=params(48),
        cost_estimate=cost(4 * rows * width * half, 4 * width * half + 2 * rows * width),
    )(side, x, gate_weight, up_weight)


def hidden_kernel(count, own_ref, got_ref, place_ref, send_ref, *refs):
    parts, hid_ref, out_refs = refs[:count], refs[count], refs[count + 1 :]
    rows = hid_ref.shape[0]
    cap = out_refs[0].shape[0]
    delta = dot(place_ref[...], jnp.concatenate([part[...] for part in parts], axis=0))
    gate = own_ref[0] + got_ref[0].astype(F32) + delta[:rows]
    up = own_ref[1] + got_ref[1].astype(F32) + delta[rows:]
    hidden = (gate / (1.0 + jnp.exp(-gate)) * up).astype(BF)
    hid_ref[...] = hidden
    sent = dot(send_ref[...], hidden).astype(BF)
    for b in range(count):
        out_refs[b][...] = sent[b * cap : (b + 1) * cap]


def hidden_half(own, got, parts, place, send):
    count = len(parts)
    rows, half = own.shape[1:]
    block = min(256, half)
    cap = send.shape[0] // count
    both = pl.BlockSpec((2, rows, block), lambda n: (0, 0, n))
    flat = lambda depth: pl.BlockSpec((depth, block), lambda n: (0, n))
    return pl.pallas_call(
        lambda *refs: hidden_kernel(count, *refs),
        out_shape=(jax.ShapeDtypeStruct((rows, half), BF),)
        + (jax.ShapeDtypeStruct((cap, half), BF),) * count,
        grid=(half // block,),
        in_specs=[both, both, fixed(place), fixed(send)] + [flat(parts[0].shape[0])] * count,
        out_specs=(flat(rows),) + (flat(cap),) * count,
        compiler_params=params(40),
        cost_estimate=cost(
            2 * half * (place.size + send.size), 2 * half * (6 * rows + 3 * count * cap)
        ),
    )(own, got, place, send, *parts)


def down_kernel(core_ref, near_ref, far_ref, weight_ref, out_ref, held, sems):
    chunks = sems.shape[1]
    half, width = held.shape[1:]
    block = width // chunks
    copies = []
    for c in range(chunks):
        here = pl.ds(c * block, block)
        for side, at in enumerate((core_ref[0], 1 - core_ref[0])):
            lines = pl.ds(pl.multiple_of(at * half, half), half)
            copy = pltpu.make_async_copy(
                weight_ref.at[lines, here], held.at[side, :, here], sems.at[side, c]
            )
            copy.start()
            copies.append(copy)
    for c in range(chunks):
        here = pl.ds(c * block, block)
        copies[2 * c].wait()
        copies[2 * c + 1].wait()
        out_ref[:, here] = dot(near_ref[...], held[0, :, here]) + dot(
            far_ref[...], held[1, :, here]
        )


def down_base(core, near, far, weight):
    rows, half = near.shape
    width = weight.shape[1]
    chunks = max(width // 512, 1)
    return pl.pallas_call(
        down_kernel,
        out_shape=jax.ShapeDtypeStruct((rows, width), F32),
        grid_spec=pltpu.PrefetchScalarGridSpec(
            num_scalar_prefetch=1,
            grid=(1,),
            in_specs=[fixed(near), fixed(far), pl.BlockSpec(memory_space=pl.ANY)],
            out_specs=pl.BlockSpec((rows, width), lambda n, core: (0, 0)),
            scratch_shapes=[
                pltpu.VMEM((2, half, width), BF),
                pltpu.SemaphoreType.DMA((2, chunks)),
            ],
        ),
        compiler_params=params(48),
        cost_estimate=cost(4 * rows * half * width, 4 * half * width + 4 * rows * width),
    )(core, near, far, weight)


def low_out_kernel(count, at_ref, mask_ref, *refs):
    parts, shrinks, out_ref = refs[:count], refs[count : 2 * count], refs[2 * count]
    pairs = sum(dot_last(part[...], shrink[...]) for part, shrink in zip(parts, shrinks))
    out_ref[...] = jnp.where(mask_ref[...] > 0, pairs, 0.0)


def low_out_pairs(at, parts, shrink, mask):
    count = len(parts)
    cap, half = parts[0].shape
    depth = shrink.shape[0]
    column = lambda b: pl.BlockSpec((depth, half), lambda i, at: (0, at[b]))
    return pl.pallas_call(
        lambda *refs: low_out_kernel(count, *refs),
        out_shape=jax.ShapeDtypeStruct((cap, depth), F32),
        grid_spec=pltpu.PrefetchScalarGridSpec(
            num_scalar_prefetch=1,
            grid=(1,),
            in_specs=[fixed(mask)]
            + [fixed(part) for part in parts]
            + [column(b) for b in range(count)],
            out_specs=fixed(mask),
        ),
        compiler_params=params(16),
        cost_estimate=cost(2 * cap * depth * count * half, 2 * count * half * (depth + cap)),
    )(at, mask, *parts, *[shrink] * count)


def add_kernel(base_ref, own_ref, got_ref, pick_ref, expand_ref, *out_refs):
    low = (own_ref[...] + got_ref[...]).astype(BF)
    spread = lax.dot_general(
        pick_ref[...], low, (((0,), (0,)), ((), ())), preferred_element_type=F32
    ).astype(BF)
    total = base_ref[...] + dot(spread, expand_ref[...])
    own_rows = out_refs[0].shape[0]
    for b, out_ref in enumerate(out_refs):
        out_ref[...] = total[b * own_rows : (b + 1) * own_rows].astype(BF)


def add_delta(base, own, got, pick, expand, count):
    rows, width = base.shape
    block = min(1024, width)
    depth = expand.shape[0]
    flat = lambda tall: pl.BlockSpec((tall, block), lambda n: (0, n))
    return pl.pallas_call(
        add_kernel,
        out_shape=(jax.ShapeDtypeStruct((rows // count, width), BF),) * count,
        grid=(width // block,),
        in_specs=[flat(rows), fixed(own), fixed(got), fixed(pick), flat(depth)],
        out_specs=(flat(rows // count),) * count,
        compiler_params=params(24),
        cost_estimate=cost(2 * rows * depth * width, width * (6 * rows + 2 * depth)),
    )(base, own, got, pick, expand)


def tied(first, *others):
    return lax.optimization_barrier((first, *others))


def per_device(
    tokens,
    gate_weight,
    up_weight,
    down_weight,
    shrink_gu,
    expand_gu,
    shrink_down,
    expand_down,
    variant_ids,
    variant_slot,
):
    ways = Ways()
    shards, order = ways.shards, ways.order
    me = lax.axis_index("ff").astype(I32)
    core = lax.axis_index("var").astype(I32)
    groups = lax.axis_size("groups")
    own_rows, width = tokens.shape
    rows = own_rows * shards
    slots = shrink_gu.shape[0]
    variants = variant_slot.shape[0]
    rank = shrink_down.shape[1]
    half_rank = expand_gu.shape[2]
    half = gate_weight.shape[1] // 2
    most = min(slots * MOST, rows)
    here = core.reshape(1)
    there = 1 - here
    at_here = 2 * order + core
    at_there = 2 * order + 1 - core
    swap = lambda a: lax.ppermute(a, "var", [(0, 1), (1, 0)])

    token_parts = ways.gather(tokens)
    at_there, *token_parts[:: ways.fast] = tied(at_there, *token_parts[:: ways.fast])

    near = expand_gu.reshape(slots * 2 * half_rank, -1)
    far = swap(pick_columns(at_there, near, half))

    ids = variant_ids[:, 0]
    matches = ids[:, None] == jnp.arange(variants, dtype=I32)[None, :]
    slot_row = jnp.sum(jnp.where(matches, variant_slot[None, :], 0), axis=1)
    owner = slot_row // slots
    index = jnp.arange(rows, dtype=I32)
    earlier = (owner[:, None] == owner[None, :]) & (index[None, :] < index[:, None])
    place = jnp.sum(earlier.astype(I32), axis=1)
    highest = jnp.max(place).reshape(1)
    for turn in range(1, groups):
        pairs = [(g, (g + turn) % groups) for g in range(groups)]
        highest = jnp.maximum(highest, lax.ppermute(highest, "groups", pairs))
    where_row = order[:, None] == jnp.arange(shards, dtype=I32)[None, :]
    turned = lambda a: jnp.sum(
        jnp.where(where_row[:, :, None], a.reshape(1, shards, own_rows), 0), axis=1
    ).reshape(rows)
    slot_row, place = turned(slot_row), turned(place)
    owner = slot_row // slots
    step = jnp.sum(
        jnp.where(owner[:, None] == order[None, :], jnp.arange(shards, dtype=I32)[None, :], 0),
        axis=1,
    )
    local = slot_row - me * slots
    kinds = jnp.arange(2, dtype=I32)
    in_cols = jnp.arange(slots * 2 * rank, dtype=I32)
    mask_in = (local[:, None] == (in_cols // (2 * rank))[None, :]).astype(F32)
    rank_at = in_cols % rank
    kind_at = in_cols // rank % 2
    row_at = in_cols // (2 * rank) * (2 * half_rank) + kind_at * half_rank + rank_at % half_rank
    near_cols = jnp.arange(slots * 2 * half_rank, dtype=I32)
    hit = row_at[:, None] == near_cols[None, :]
    side = jnp.stack([core, 1 - core])
    cols = (
        hit[None, None]
        & (kind_at[None, :] == kinds[:, None])[:, None, :, None]
        & ((rank_at // half_rank)[None, :] == side[:, None])[None, :, :, None]
    ).astype(BF)

    def finish(cap):
        cells = jnp.arange(shards * cap, dtype=I32)
        send_rows = (cells[:, None] == (step * cap + place)[None, :]).astype(BF)
        kind_cell = (step * 2 + kinds[:, None]) * cap + place
        kind_cells = jnp.arange(2 * shards * cap, dtype=I32)
        place_rows = (kind_cell[:, :, None] == kind_cells).astype(BF).reshape(2 * rows, -1)
        spots = jnp.arange(cap, dtype=I32)
        picked = (spots[:, None] == place[None, :]) & (owner[None, :] == me)
        pick = picked.astype(BF)
        spot_slot = jnp.sum(jnp.where(picked, local[None, :] + 1, 0), axis=1) - 1
        out_cols = jnp.arange(slots * rank, dtype=I32)
        mask_out = (spot_slot[:, None] == (out_cols // rank)[None, :]).astype(F32)

        x, low_own = low_in_pairs(token_parts, shrink_gu.reshape(slots * 2 * rank, width), mask_in)
        low_got = swap(low_own)
        made = expand_rows(at_here, low_own, low_got, pick, cols, near, far, half)
        x, *made = tied(x, *made)
        base_got = swap(base_half(there, x, gate_weight, up_weight, half, BF))
        delta = ways.deliver(made)
        base_own = base_half(here, x, gate_weight, up_weight, half, F32)
        hidden, *sent = hidden_half(base_own, base_got, delta, place_rows, send_rows)
        hidden_far = swap(hidden)
        hidden_rows = ways.deliver(sent)
        base = down_base(here, hidden, hidden_far, down_weight)
        base, *hidden_rows = tied(base, *hidden_rows)
        shrink = shrink_down.reshape(slots * rank, -1)
        out_own = low_out_pairs(at_here, hidden_rows, shrink, mask_out)
        out_got = swap(out_own)
        expand = expand_down.reshape(slots * rank, width)
        parts = ways.deliver(add_delta(base, out_own, out_got, pick, expand, shards))
        return sum(part.astype(F32) for part in parts).astype(BF)

    if most <= USUAL:
        return finish(most)
    return lax.cond(highest[0] < USUAL, lambda: finish(USUAL), lambda: finish(most))


def solution(mesh):
    placed = (
        P(("groups", "ff"), "var"),
        P("var", "ff"),
        P("var", "ff"),
        P("ff", "var"),
        P(("groups", "ff"), None, "var"),
        P(("groups", "ff"), None, "var", None),
        P(("groups", "ff"), None, None),
        P(("groups", "ff"), None, "var"),
        P("groups", None),
        P("groups"),
    )
    return jax.shard_map(
        per_device,
        mesh=mesh,
        in_specs=placed,
        out_specs=P(("groups", "ff"), "var"),
        check_vma=False,
    )
```

```python
import functools

import jax
import jax.numpy as jnp
from jax import lax
from jax.experimental import pallas as pl
from jax.experimental.pallas import tpu as pltpu
from jax.sharding import PartitionSpec as P

MOST = 8
DIRECT = 8
USUAL = 16
BF = jnp.bfloat16
F32 = jnp.float32
I32 = jnp.int32
MIB = 1024 * 1024


def dot(a, b):
    return jnp.dot(a, b, preferred_element_type=F32)


def dot_last(a, b):
    return lax.dot_general(a, b, (((1,), (1,)), ((), ())), preferred_element_type=F32)


def params(mib):
    return pltpu.CompilerParams(vmem_limit_bytes=mib * MIB)


def cost(flops, moved):
    return pl.CostEstimate(flops=flops, bytes_accessed=moved, transcendentals=0)


def fixed(array):
    zeros = (0,) * array.ndim
    return pl.BlockSpec(array.shape, lambda *_: zeros)


class Ways:
    def __init__(self):
        self.shards = lax.axis_size("ff")
        self.fast = 2 if self.shards % 2 == 0 else 1
        self.slow = self.shards // self.fast
        self.direct = self.shards <= DIRECT
        me = lax.axis_index("ff").astype(I32)
        steps = jnp.arange(self.shards, dtype=I32)
        if self.direct:
            slow = (me // self.fast - steps // self.fast) % self.slow
            fast = (me % self.fast - steps % self.fast) % self.fast
            self.order = slow * self.fast + fast
        else:
            self.order = steps

    def sent_at(self):
        steps = jnp.arange(self.shards, dtype=I32)
        if not self.direct:
            return steps
        return steps % self.fast * self.slow + steps // self.fast

    def back(self, a, c):
        S, F = self.slow, self.fast
        return [(s * F + f, (s - a) % S * F + (f - c) % F) for s in range(S) for f in range(F)]

    def gather(self, block):
        if not self.direct:
            return list(lax.all_gather(block, "ff"))
        got = [None] * self.shards
        for a in range(self.slow):
            got[a * self.fast] = lax.ppermute(block, "ff", self.back(-a, 0)) if a else block
        for a in range(self.slow):
            for c in range(1, self.fast):
                got[a * self.fast + c] = lax.ppermute(
                    got[a * self.fast], "ff", self.back(0, -c)
                )
        return got

    def spread(self, blocks):
        return lax.all_to_all(blocks, "ff", 0, 0, tiled=True)

    def deliver(self, blocks):
        if not self.direct:
            return list(self.spread(jnp.stack(blocks)))
        got = [None] * self.shards
        got[0] = blocks[0]
        for b in range(1, self.shards):
            a, c = b // self.fast, b % self.fast
            back = (-a) % self.slow * self.fast + (-c) % self.fast
            got[back] = lax.ppermute(blocks[b], "ff", self.back(a, c))
        return got

    def slow_steps(self, blocks):
        got = [blocks[0]] + [None] * (self.slow - 1)
        for a in range(1, self.slow):
            got[(-a) % self.slow] = lax.ppermute(blocks[a], "ff", self.back(a, 0))
        return got


def stage_kernel(
    here_ref, there_ref, x_ref, expand_ref, shrink_ref, kept_ref, near_ref, far_ref, held_ref, sems
):
    half = near_ref.shape[1] // (sems.shape[0] - 1)
    copies = []
    for side, (at_ref, out) in enumerate(((there_ref, far_ref), (here_ref, near_ref))):
        for b in range(sems.shape[0] - 1):
            columns = pl.ds(pl.multiple_of(at_ref[b] * half, half), half)
            put = out.at[:, pl.ds(b * half, half)]
            copies.append(pltpu.make_async_copy(expand_ref.at[:, columns], put, sems.at[b, side]))
    copies.append(pltpu.make_async_copy(shrink_ref, held_ref, sems.at[sems.shape[0] - 1, 0]))
    for copy in copies:
        copy.start()
    kept_ref[...] = x_ref[...]
    for copy in copies:
        copy.wait()


def stage(at_here, at_there, x, expand, shrink):
    depth, width = expand.shape
    shards = at_here.shape[0]
    out = jax.ShapeDtypeStruct((depth, width // 2), BF)
    return pl.pallas_call(
        stage_kernel,
        out_shape=(
            jax.ShapeDtypeStruct(x.shape, BF),
            out,
            out,
            jax.ShapeDtypeStruct(shrink.shape, BF),
        ),
        grid_spec=pltpu.PrefetchScalarGridSpec(
            num_scalar_prefetch=2,
            grid=(1,),
            in_specs=[fixed(x)] + [pl.BlockSpec(memory_space=pl.ANY)] * 2,
            out_specs=(fixed(x), fixed(out), fixed(out), fixed(shrink)),
            scratch_shapes=[pltpu.SemaphoreType.DMA((shards + 1, 2))],
        ),
        compiler_params=params(16),
        cost_estimate=cost(0, 2 * (2 * expand.size + 2 * shrink.size)),
    )(at_here, at_there, x, expand, shrink)


def low_in_kernel(count, shrink_ref, mask_ref, *refs):
    parts, x_ref, out_ref = refs[:count], refs[count], refs[count + 1]
    x = jnp.concatenate([part[...].astype(F32) for part in parts], axis=0).astype(BF)
    x_ref[...] = x

    @pl.when(pl.program_id(0) == 0)
    def _():
        out_ref[...] = jnp.zeros_like(out_ref)

    out_ref[...] += jnp.where(mask_ref[...] > 0, dot_last(x, shrink_ref[...]), 0.0)


def low_in_pairs(parts, shrink, mask):
    count = len(parts)
    own_rows, width = parts[0].shape
    rows, block = count * own_rows, min(1024, width)
    return pl.pallas_call(
        lambda *refs: low_in_kernel(count, *refs),
        out_shape=(
            jax.ShapeDtypeStruct((rows, width), BF),
            jax.ShapeDtypeStruct(mask.shape, F32),
        ),
        grid=(width // block,),
        in_specs=[pl.BlockSpec((shrink.shape[0], block), lambda n: (0, n)), fixed(mask)]
        + [pl.BlockSpec((own_rows, block), lambda n: (0, n))] * count,
        out_specs=(pl.BlockSpec((rows, block), lambda n: (0, n)), fixed(mask)),
        compiler_params=params(16),
        cost_estimate=cost(2 * rows * width * shrink.shape[0], 2 * shrink.size + 4 * rows * width),
    )(shrink, mask, *parts)


def expand_kernel(fast, own_ref, got_ref, pick_ref, cols_ref, near_ref, far_ref, *out_refs):
    low = (own_ref[...] + got_ref[...]).astype(BF)
    picked = dot(pick_ref[...], low).astype(BF)
    lhs = [
        jnp.concatenate([dot(picked, cols_ref[kind, side]) for kind in range(2)], axis=0)
        for side in range(2)
    ]
    lhs = [side.astype(BF) for side in lhs]
    tall = lhs[0].shape[0]
    half = out_refs[0].shape[1]
    for b in range(near_ref.shape[1] // half):
        here = pl.ds(b * half, half)
        delta = dot(lhs[0], near_ref[:, here]) + dot(lhs[1], far_ref[:, here])
        out_refs[b % fast][pl.ds(b // fast * tall, tall)] = delta.astype(BF)


def expand_rows(own, got, pick, cols, near, far, shards, fast):
    cap = pick.shape[0]
    depth, width = near.shape
    out = jax.ShapeDtypeStruct((2 * cap * shards // fast, width // shards), BF)
    return pl.pallas_call(
        functools.partial(expand_kernel, fast),
        out_shape=(out,) * fast,
        compiler_params=params(16),
        cost_estimate=cost(8 * cap * depth * width, 4 * (depth + cap) * width),
    )(own, got, pick, cols, near, far)


def base_kernel(side_ref, x_ref, gate_ref, up_ref, out_ref, held, sums, sems):
    half = held.shape[2]
    chunks = sems.shape[1]
    depth = held.shape[1] // chunks
    columns = pl.ds(pl.multiple_of(side_ref[0] * half, half), half)
    copies = []
    for c in range(chunks):
        here = pl.ds(c * depth, depth)
        for kind, weight in enumerate((gate_ref, up_ref)):
            copy = pltpu.make_async_copy(
                weight.at[here, columns], held.at[kind, here], sems.at[kind, c]
            )
            copy.start()
            copies.append((kind, here, copy))
    for kind, here, copy in copies:
        copy.wait()
        part = dot(x_ref[:, here], held[kind, here])
        sums[kind] = part if here.start == 0 else sums[kind] + part
    out_ref[...] = sums[...].astype(out_ref.dtype)


def base_half(side, x, gate_weight, up_weight, half, kind):
    rows, width = x.shape
    chunks = max(width // 512, 1)
    return pl.pallas_call(
        base_kernel,
        out_shape=jax.ShapeDtypeStruct((2, rows, half), kind),
        grid_spec=pltpu.PrefetchScalarGridSpec(
            num_scalar_prefetch=1,
            grid=(1,),
            in_specs=[fixed(x), pl.BlockSpec(memory_space=pl.ANY), pl.BlockSpec(memory_space=pl.ANY)],
            out_specs=pl.BlockSpec((2, rows, half), lambda n, side: (0, 0, 0)),
            scratch_shapes=[
                pltpu.VMEM((2, width, half), BF),
                pltpu.VMEM((2, rows, half), F32),
                pltpu.SemaphoreType.DMA((2, chunks)),
            ],
        ),
        compiler_params=params(48),
        cost_estimate=cost(4 * rows * width * half, 4 * width * half + 2 * rows * width),
    )(side, x, gate_weight, up_weight)


def hidden_kernel(count, own_ref, got_ref, place_ref, send_ref, *refs):
    parts, hid_ref, out_refs = refs[:count], refs[count], refs[count + 1 :]
    rows = hid_ref.shape[0]
    tall = out_refs[0].shape[0]
    delta = dot(place_ref[...], jnp.concatenate([part[...] for part in parts], axis=0))
    gate = own_ref[0] + got_ref[0].astype(F32) + delta[:rows]
    up = own_ref[1] + got_ref[1].astype(F32) + delta[rows:]
    hidden = (gate / (1.0 + jnp.exp(-gate)) * up).astype(BF)
    hid_ref[...] = hidden
    sent = dot(send_ref[...], hidden).astype(BF)
    for n, out_ref in enumerate(out_refs):
        out_ref[...] = sent[n * tall : (n + 1) * tall]


def hidden_half(own, got, parts, place, send, count):
    rows, half = own.shape[1:]
    block = min(256, half)
    tall = send.shape[0] // count
    both = pl.BlockSpec((2, rows, block), lambda n: (0, 0, n))
    flat = lambda depth: pl.BlockSpec((depth, block), lambda n: (0, n))
    return pl.pallas_call(
        functools.partial(hidden_kernel, len(parts)),
        out_shape=(jax.ShapeDtypeStruct((rows, half), BF),)
        + (jax.ShapeDtypeStruct((tall, half), BF),) * count,
        grid=(half // block,),
        in_specs=[both, both, fixed(place), fixed(send)] + [flat(part.shape[0]) for part in parts],
        out_specs=(flat(rows),) + (flat(tall),) * count,
        compiler_params=params(40),
        cost_estimate=cost(
            2 * half * (place.size + send.size),
            2 * half * (6 * rows + place.shape[1] + send.shape[0]),
        ),
    )(own, got, place, send, *parts)


def relay_kernel(own_ref, got_ref, *out_refs):
    cap = out_refs[0].shape[0] // 2
    for a, out_ref in enumerate(out_refs):
        here = pl.ds(a * cap, cap)
        out_ref[:cap] = own_ref[here]
        out_ref[cap:] = got_ref[here]


def relay(own, got, count):
    tall, half = own.shape
    return pl.pallas_call(
        relay_kernel,
        out_shape=(jax.ShapeDtypeStruct((2 * tall // count, half), BF),) * count,
        compiler_params=params(16),
        cost_estimate=cost(0, 8 * tall * half),
    )(own, got)


def down_kernel(first, core_ref, near_ref, far_ref, weight_ref, out_ref, held, sems):
    chunks = sems.shape[1]
    half, width = held.shape[1:]
    block = width // chunks
    copies = []
    for c in range(chunks):
        here = pl.ds(c * block, block)
        for side, at in enumerate((core_ref[0], 1 - core_ref[0])):
            lines = pl.ds(pl.multiple_of(at * half, half), half)
            copy = pltpu.make_async_copy(
                weight_ref.at[lines, pl.ds(first + c * block, block)],
                held.at[side, :, here],
                sems.at[side, c],
            )
            copy.start()
            copies.append(copy)
    for c in range(chunks):
        here = pl.ds(c * block, block)
        copies[2 * c].wait()
        copies[2 * c + 1].wait()
        out_ref[:, here] = dot(near_ref[...], held[0, :, here]) + dot(
            far_ref[...], held[1, :, here]
        )


def down_base(core, near, far, weight, first, width):
    rows, half = near.shape
    chunks = max(width // 512, 1)
    return pl.pallas_call(
        functools.partial(down_kernel, first),
        out_shape=jax.ShapeDtypeStruct((rows, width), F32),
        grid_spec=pltpu.PrefetchScalarGridSpec(
            num_scalar_prefetch=1,
            grid=(1,),
            in_specs=[fixed(near), fixed(far), pl.BlockSpec(memory_space=pl.ANY)],
            out_specs=pl.BlockSpec((rows, width), lambda n, core: (0, 0)),
            scratch_shapes=[
                pltpu.VMEM((2, half, width), BF),
                pltpu.SemaphoreType.DMA((2, chunks)),
            ],
        ),
        compiler_params=params(48),
        cost_estimate=cost(4 * rows * half * width, 4 * half * width + 4 * rows * width),
    )(core, near, far, weight)


def low_out_kernel(count, at_ref, mask_ref, *refs):
    parts, shrinks, out_ref = refs[:count], refs[count:-1], refs[-1]
    cap = out_ref.shape[0]
    blocks = [part[r : r + cap] for part in parts for r in range(0, part.shape[0], cap)]
    pairs = sum(dot_last(block, shrink[...]) for block, shrink in zip(blocks, shrinks))
    out_ref[...] = jnp.where(mask_ref[...] > 0, pairs, 0.0)


def low_out_pairs(at, parts, shrink, mask):
    count = len(parts)
    half = parts[0].shape[1]
    cap, depth = mask.shape
    column = lambda b: pl.BlockSpec((depth, half), lambda i, at: (0, at[b]))
    return pl.pallas_call(
        functools.partial(low_out_kernel, count),
        out_shape=jax.ShapeDtypeStruct((cap, depth), F32),
        grid_spec=pltpu.PrefetchScalarGridSpec(
            num_scalar_prefetch=1,
            grid=(1,),
            in_specs=[fixed(mask)]
            + [fixed(part) for part in parts]
            + [column(b) for b in range(at.shape[0])],
            out_specs=fixed(mask),
        ),
        compiler_params=params(16),
        cost_estimate=cost(
            2 * cap * depth * at.shape[0] * half, 2 * at.shape[0] * half * (depth + cap)
        ),
    )(at, mask, *parts, *[shrink] * at.shape[0])


def add_kernel(count, *refs):
    bases = refs[:count]
    own_ref, got_ref, pick_ref, expand_ref = refs[count : count + 4]
    out_refs = refs[count + 4 :]
    low = (own_ref[...] + got_ref[...]).astype(BF)
    spread = lax.dot_general(
        pick_ref[...], low, (((0,), (0,)), ((), ())), preferred_element_type=F32
    ).astype(BF)
    own_rows = out_refs[0].shape[0]
    first = 0
    for base_ref in bases:
        here = pl.ds(first, base_ref.shape[1])
        total = base_ref[...] + dot(spread, expand_ref[:, here])
        for b, out_ref in enumerate(out_refs):
            out_ref[:, here] = total[b * own_rows : (b + 1) * own_rows].astype(BF)
        first += base_ref.shape[1]


def add_delta(bases, own, got, pick, expand, count):
    rows = bases[0].shape[0]
    depth, width = expand.shape
    return pl.pallas_call(
        functools.partial(add_kernel, len(bases)),
        out_shape=(jax.ShapeDtypeStruct((rows // count, width), BF),) * count,
        compiler_params=params(32),
        cost_estimate=cost(2 * rows * depth * width, width * (6 * rows + 2 * depth)),
    )(*bases, own, got, pick, expand)


def tied(first, *others):
    return lax.optimization_barrier((first, *others))


def per_device(
    tokens,
    gate_weight,
    up_weight,
    down_weight,
    shrink_gu,
    expand_gu,
    shrink_down,
    expand_down,
    variant_ids,
    variant_slot,
):
    ways = Ways()
    shards, order = ways.shards, ways.order
    me = lax.axis_index("ff").astype(I32)
    core = lax.axis_index("var").astype(I32)
    groups = lax.axis_size("groups")
    own_rows, width = tokens.shape
    rows = own_rows * shards
    slots = shrink_gu.shape[0]
    variants = variant_slot.shape[0]
    rank = shrink_down.shape[1]
    half_rank = expand_gu.shape[2]
    half = gate_weight.shape[1] // 2
    most = min(slots * MOST, rows)
    here = core.reshape(1)
    there = 1 - here
    at_here = 2 * order + core
    at_there = 2 * order + 1 - core
    split = ways.fast if ways.direct else 1
    swap = lambda a: lax.ppermute(a, "var", [(0, 1), (1, 0)])

    token_parts = ways.gather(tokens)
    kept, near, far, shrink_in = stage(
        at_here,
        at_there,
        tokens,
        expand_gu.reshape(slots * 2 * half_rank, -1),
        shrink_gu.reshape(slots * 2 * rank, width),
    )
    if ways.direct:
        token_parts[0] = kept
        variant_ids, far, *token_parts[:: ways.fast] = tied(
            variant_ids, far, *token_parts[:: ways.fast]
        )
    far = swap(far)

    ids = variant_ids[:, 0]
    matches = ids[:, None] == jnp.arange(variants, dtype=I32)[None, :]
    slot_row = jnp.sum(jnp.where(matches, variant_slot[None, :], 0), axis=1)
    owner = slot_row // slots
    index = jnp.arange(rows, dtype=I32)
    earlier = (owner[:, None] == owner[None, :]) & (index[None, :] < index[:, None])
    place = jnp.sum(earlier.astype(I32), axis=1)
    highest = jnp.max(place).reshape(1)
    for turn in range(1, groups):
        pairs = [(g, (g + turn) % groups) for g in range(groups)]
        highest = jnp.maximum(highest, lax.ppermute(highest, "groups", pairs))
    where_row = order[:, None] == jnp.arange(shards, dtype=I32)[None, :]
    turned = lambda a: jnp.sum(
        jnp.where(where_row[:, :, None], a.reshape(1, shards, own_rows), 0), axis=1
    ).reshape(rows)
    slot_row, place = turned(slot_row), turned(place)
    owner = slot_row // slots
    named = owner[:, None] == order[None, :]
    block = jnp.sum(jnp.where(named, jnp.arange(shards, dtype=I32)[None, :], 0), axis=1)
    step = jnp.sum(jnp.where(named, ways.sent_at()[None, :], 0), axis=1)
    local = slot_row - me * slots
    kinds = jnp.arange(2, dtype=I32)
    in_cols = jnp.arange(slots * 2 * rank, dtype=I32)
    mask_in = (local[:, None] == (in_cols // (2 * rank))[None, :]).astype(F32)
    rank_at = in_cols % rank
    kind_at = in_cols // rank % 2
    row_at = in_cols // (2 * rank) * (2 * half_rank) + kind_at * half_rank + rank_at % half_rank
    near_cols = jnp.arange(slots * 2 * half_rank, dtype=I32)
    hit = row_at[:, None] == near_cols[None, :]
    side = jnp.stack([core, 1 - core])
    cols = (
        hit[None, None]
        & (kind_at[None, :] == kinds[:, None])[:, None, :, None]
        & ((rank_at // half_rank)[None, :] == side[:, None])[None, :, :, None]
    ).astype(BF)

    highest, token_parts[-1] = tied(highest, token_parts[-1])
    x, low_own = low_in_pairs(token_parts, shrink_in, mask_in)
    low_got = swap(low_own)

    def partial_sums(cap):
        cells = jnp.arange(shards * cap, dtype=I32)
        send_rows = (cells[:, None] == (step * cap + place)[None, :]).astype(BF)
        kind_cell = (block * 2 + kinds[:, None]) * cap + place
        kind_cells = jnp.arange(2 * shards * cap, dtype=I32)
        place_rows = (kind_cell[:, :, None] == kind_cells).astype(BF).reshape(2 * rows, -1)
        spots = jnp.arange(cap, dtype=I32)
        picked = (spots[:, None] == place[None, :]) & (owner[None, :] == me)
        pick = picked.astype(BF)
        spot_slot = jnp.sum(jnp.where(picked, local[None, :] + 1, 0), axis=1) - 1
        out_cols = jnp.arange(slots * rank, dtype=I32)
        mask_out = (spot_slot[:, None] == (out_cols // rank)[None, :]).astype(F32)

        made = expand_rows(low_own, low_got, pick, cols, near, far, shards, split)
        held, *made = tied(x, *made)
        if split == 2:
            beside = lax.ppermute(made[1], "ff", ways.back(0, 1))
            base_there = base_half(there, held, gate_weight, up_weight, half, BF)
            base_there, beside = tied(base_there, beside)
            made = relay(made[0], beside, ways.slow)
            held, *made = tied(held, *made)
            delta = ways.slow_steps(made)
        else:
            base_there = base_half(there, held, gate_weight, up_weight, half, BF)
            delta = [ways.spread(made[0].reshape(shards, 2 * cap, half))]
            delta = [delta[0].reshape(2 * shards * cap, half)]
        base_got = swap(base_there)
        base_own = base_half(here, held, gate_weight, up_weight, half, F32)
        hidden, *sent = hidden_half(base_own, base_got, delta, place_rows, send_rows, split)
        hidden_far = swap(hidden)
        side = width // 2
        if split == 2:
            beside = lax.ppermute(sent[1], "ff", ways.back(0, 1))
            left = down_base(here, hidden, hidden_far, down_weight, 0, side)
            left, beside = tied(left, beside)
            sent = relay(sent[0], beside, ways.slow)
            hidden, *sent = tied(hidden, *sent)
            got = ways.slow_steps(sent)
        else:
            left = down_base(here, hidden, hidden_far, down_weight, 0, side)
            got = [ways.spread(sent[0].reshape(shards, cap, half)).reshape(shards * cap, half)]
        right = down_base(here, hidden, hidden_far, down_weight, side, width - side)
        right, *got = tied(right, *got)
        shrink = shrink_down.reshape(slots * rank, -1)
        out_own = low_out_pairs(at_here, got, shrink, mask_out)
        out_got = swap(out_own)
        expand = expand_down.reshape(slots * rank, width)
        return ways.deliver(add_delta([left, right], out_own, out_got, pick, expand, shards))

    if most <= USUAL:
        parts = partial_sums(most)
    else:
        parts = lax.cond(
            highest[0] < USUAL, lambda: partial_sums(USUAL), lambda: partial_sums(most)
        )
    return sum(part.astype(F32) for part in parts).astype(BF)


def solution(mesh):
    placed = (
        P(("groups", "ff"), "var"),
        P("var", "ff"),
        P("var", "ff"),
        P("ff", "var"),
        P(("groups", "ff"), None, "var"),
        P(("groups", "ff"), None, "var", None),
        P(("groups", "ff"), None, None),
        P(("groups", "ff"), None, "var"),
        P("groups", None),
        P("groups"),
    )
    return jax.shard_map(
        per_device,
        mesh=mesh,
        in_specs=placed,
        out_specs=P(("groups", "ff"), "var"),
        check_vma=False,
    )
```

```python
import functools

import jax
import jax.numpy as jnp
from jax import lax
from jax.experimental import pallas as pl
from jax.experimental.pallas import tpu as pltpu
from jax.sharding import PartitionSpec as P

MOST = 8
DIRECT = 8
USUAL = 16
BF = jnp.bfloat16
F32 = jnp.float32
I32 = jnp.int32
MIB = 1024 * 1024


def dot(a, b):
    return jnp.dot(a, b, preferred_element_type=F32)


def dot_last(a, b):
    return lax.dot_general(a, b, (((1,), (1,)), ((), ())), preferred_element_type=F32)


def params(mib):
    return pltpu.CompilerParams(vmem_limit_bytes=int(mib * MIB))


def cost(flops, moved):
    return pl.CostEstimate(flops=flops, bytes_accessed=moved, transcendentals=0)


def fixed(array):
    zeros = (0,) * array.ndim
    return pl.BlockSpec(array.shape, lambda *_: zeros)


class Ways:
    def __init__(self):
        self.shards = lax.axis_size("ff")
        self.fast = 2 if self.shards % 2 == 0 else 1
        self.slow = self.shards // self.fast
        self.direct = self.shards <= DIRECT
        me = lax.axis_index("ff").astype(I32)
        steps = jnp.arange(self.shards, dtype=I32)
        if self.direct:
            slow = (me // self.fast - steps % self.slow) % self.slow
            fast = (me % self.fast - steps // self.slow) % self.fast
            self.order = slow * self.fast + fast
        else:
            self.order = steps

    def arrival(self):
        steps = jnp.arange(self.shards, dtype=I32)
        if not self.direct:
            return steps
        return steps % self.slow * self.fast + steps // self.slow

    def back(self, a, c):
        S, F = self.slow, self.fast
        return [(s * F + f, (s - a) % S * F + (f - c) % F) for s in range(S) for f in range(F)]

    def gather(self, block):
        if not self.direct:
            return list(lax.all_gather(block, "ff"))
        got = [block] + [
            lax.ppermute(block, "ff", self.back(-a, 0)) for a in range(1, self.slow)
        ]
        for c in range(1, self.fast):
            got += [lax.ppermute(part, "ff", self.back(0, -c)) for part in got[: self.slow]]
        return got

    def spread(self, blocks):
        return lax.all_to_all(blocks, "ff", 0, 0, tiled=True)

    def slow_steps(self, blocks):
        got = [blocks[0]] + [None] * (self.slow - 1)
        for a in range(1, self.slow):
            got[(-a) % self.slow] = lax.ppermute(blocks[a], "ff", self.back(a, 0))
        return got


def stage_kernel(
    here_ref, there_ref, x_ref, expand_ref, shrink_ref, kept_ref, near_ref, far_ref, held_ref, sems
):
    half = near_ref.shape[1] // (sems.shape[0] - 1)
    copies = []
    for side, (at_ref, out) in enumerate(((there_ref, far_ref), (here_ref, near_ref))):
        for b in range(sems.shape[0] - 1):
            columns = pl.ds(pl.multiple_of(at_ref[b] * half, half), half)
            put = out.at[:, pl.ds(b * half, half)]
            copies.append(pltpu.make_async_copy(expand_ref.at[:, columns], put, sems.at[b, side]))
    copies.append(pltpu.make_async_copy(shrink_ref, held_ref, sems.at[sems.shape[0] - 1, 0]))
    copies.append(pltpu.make_async_copy(x_ref, kept_ref, sems.at[sems.shape[0] - 1, 1]))
    for copy in copies:
        copy.start()
    for copy in copies:
        copy.wait()


def stage(at_here, at_there, x, expand, shrink):
    depth, width = expand.shape
    shards = at_here.shape[0]
    out = jax.ShapeDtypeStruct((depth, width // 2), BF)
    return pl.pallas_call(
        stage_kernel,
        out_shape=(
            jax.ShapeDtypeStruct(x.shape, BF),
            out,
            out,
            jax.ShapeDtypeStruct(shrink.shape, BF),
        ),
        grid_spec=pltpu.PrefetchScalarGridSpec(
            num_scalar_prefetch=2,
            grid=(1,),
            in_specs=[pl.BlockSpec(memory_space=pltpu.HBM)] * 3,
            out_specs=(pl.BlockSpec(memory_space=pl.ANY),) * 4,
            scratch_shapes=[pltpu.SemaphoreType.DMA((shards + 1, 2))],
        ),
        compiler_params=params(51.25),
        cost_estimate=cost(0, 2 * (2 * expand.size + 2 * shrink.size)),
    )(at_here, at_there, x, expand, shrink)


def low_in_kernel(count, shrink_ref, mask_ref, *refs):
    parts, x_ref, out_ref = refs[:count], refs[count], refs[count + 1]
    x = jnp.concatenate([part[...].astype(F32) for part in parts], axis=0).astype(BF)
    x_ref[...] = x

    @pl.when(pl.program_id(0) == 0)
    def _():
        out_ref[...] = jnp.zeros_like(out_ref)

    out_ref[...] += jnp.where(mask_ref[...] > 0, dot_last(x, shrink_ref[...]), 0.0)


def low_in_pairs(parts, shrink, mask):
    count = len(parts)
    own_rows, width = parts[0].shape
    rows, block = count * own_rows, min(1024, width)
    return pl.pallas_call(
        lambda *refs: low_in_kernel(count, *refs),
        out_shape=(
            jax.ShapeDtypeStruct((rows, width), BF),
            jax.ShapeDtypeStruct(mask.shape, F32),
        ),
        grid=(width // block,),
        in_specs=[pl.BlockSpec((shrink.shape[0], block), lambda n: (0, n)), fixed(mask)]
        + [pl.BlockSpec((own_rows, block), lambda n: (0, n))] * count,
        out_specs=(pl.BlockSpec((rows, block), lambda n: (0, n)), fixed(mask)),
        compiler_params=params(16),
        cost_estimate=cost(2 * rows * width * shrink.shape[0], 2 * shrink.size + 4 * rows * width),
    )(shrink, mask, *parts)


def expand_kernel(fast, own_ref, got_ref, pick_ref, cols_ref, near_ref, far_ref, *out_refs):
    low = (own_ref[...] + got_ref[...]).astype(BF)
    picked = dot(pick_ref[...], low).astype(BF)
    lhs = jnp.concatenate([dot(picked, cols_ref[kind]) for kind in range(2)], axis=0).astype(BF)
    tall = lhs.shape[0]
    half = out_refs[0].shape[1]
    count = near_ref.shape[1] // half
    for b in range(count):
        here = pl.ds(b * half, half)
        both = jnp.concatenate([near_ref[:, here], far_ref[:, here]], axis=0)
        at = b % (count // fast)
        out_refs[b * fast // count][pl.ds(at * tall, tall)] = dot(lhs, both).astype(BF)


def expand_rows(own, got, pick, cols, near, far, shards, fast):
    cap = pick.shape[0]
    depth, width = near.shape
    out = jax.ShapeDtypeStruct((2 * cap * shards // fast, width // shards), BF)
    return pl.pallas_call(
        functools.partial(expand_kernel, fast),
        out_shape=(out,) * fast,
        compiler_params=params(16),
        cost_estimate=cost(8 * cap * depth * width, 4 * (depth + cap) * width),
    )(own, got, pick, cols, near, far)


def base_kernel(side_ref, x_ref, gate_ref, up_ref, out_ref, held, sums, sems):
    half = held.shape[2]
    chunks = sems.shape[1]
    depth = held.shape[1] // chunks
    columns = pl.ds(pl.multiple_of(side_ref[0] * half, half), half)
    copies = []
    for c in range(chunks):
        here = pl.ds(c * depth, depth)
        for kind, weight in enumerate((gate_ref, up_ref)):
            copy = pltpu.make_async_copy(
                weight.at[here, columns], held.at[kind, here], sems.at[kind, c]
            )
            copy.start()
            copies.append((kind, here, copy))
    for kind, here, copy in copies:
        copy.wait()
        part = dot(x_ref[:, here], held[kind, here])
        sums[kind] = part if here.start == 0 else sums[kind] + part
    out_ref[...] = sums[...].astype(out_ref.dtype)


def base_half(side, x, gate_weight, up_weight, half, kind):
    rows, width = x.shape
    chunks = max(width // 512, 1)
    return pl.pallas_call(
        base_kernel,
        out_shape=jax.ShapeDtypeStruct((2, rows, half), kind),
        grid_spec=pltpu.PrefetchScalarGridSpec(
            num_scalar_prefetch=1,
            grid=(1,),
            in_specs=[fixed(x)] + [pl.BlockSpec(memory_space=pltpu.HBM)] * 2,
            out_specs=pl.BlockSpec((2, rows, half), lambda n, side: (0, 0, 0)),
            scratch_shapes=[
                pltpu.VMEM((2, width, half), BF),
                pltpu.VMEM((2, rows, half), F32),
                pltpu.SemaphoreType.DMA((2, chunks)),
            ],
        ),
        compiler_params=params(48),
        cost_estimate=cost(4 * rows * width * half, 4 * width * half + 2 * rows * width),
    )(side, x, gate_weight, up_weight)


def hidden_kernel(count, own_ref, got_ref, place_ref, send_ref, *refs):
    parts, hid_ref, out_refs = refs[:count], refs[count], refs[count + 1 :]
    rows = hid_ref.shape[0]
    tall = out_refs[0].shape[0]
    delta = dot(place_ref[...], jnp.concatenate([part[...] for part in parts], axis=0))
    gate = own_ref[0] + got_ref[0].astype(F32) + delta[:rows]
    up = own_ref[1] + got_ref[1].astype(F32) + delta[rows:]
    hidden = (gate / (1.0 + jnp.exp(-gate)) * up).astype(BF)
    hid_ref[...] = hidden
    sent = dot(send_ref[...], hidden).astype(BF)
    for n, out_ref in enumerate(out_refs):
        out_ref[...] = sent[n * tall : (n + 1) * tall]


def hidden_half(own, got, parts, place, send, count):
    rows, half = own.shape[1:]
    block = min(256, half)
    tall = send.shape[0] // count
    both = pl.BlockSpec((2, rows, block), lambda n: (0, 0, n))
    flat = lambda depth: pl.BlockSpec((depth, block), lambda n: (0, n))
    return pl.pallas_call(
        functools.partial(hidden_kernel, len(parts)),
        out_shape=(jax.ShapeDtypeStruct((rows, half), BF),)
        + (jax.ShapeDtypeStruct((tall, half), BF),) * count,
        grid=(half // block,),
        in_specs=[both, both, fixed(place), fixed(send)] + [flat(part.shape[0]) for part in parts],
        out_specs=(flat(rows),) + (flat(tall),) * count,
        compiler_params=params(40),
        cost_estimate=cost(
            2 * half * (place.size + send.size),
            2 * half * (6 * rows + place.shape[1] + send.shape[0]),
        ),
    )(own, got, place, send, *parts)


def relay_kernel(own_ref, got_ref, *out_refs):
    cap = out_refs[0].shape[0] // 2
    for a, out_ref in enumerate(out_refs):
        here = pl.ds(a * cap, cap)
        out_ref[:cap] = own_ref[here]
        out_ref[cap:] = got_ref[here]


def relay(own, got, count):
    tall, half = own.shape
    return pl.pallas_call(
        relay_kernel,
        out_shape=(jax.ShapeDtypeStruct((2 * tall // count, half), BF),) * count,
        compiler_params=params(16),
        cost_estimate=cost(0, 8 * tall * half),
    )(own, got)


def down_kernel(core_ref, near_ref, far_ref, weight_ref, *refs):
    out_refs, held, sems = refs[:-2], refs[-2], refs[-1]
    chunks = sems.shape[1]
    half, width = held.shape[1:]
    block = width // chunks
    tall = out_refs[0].shape[0]
    copies = []
    for c in range(chunks):
        here = pl.ds(c * block, block)
        for side, at in enumerate((core_ref[0], 1 - core_ref[0])):
            lines = pl.ds(pl.multiple_of(at * half, half), half)
            copy = pltpu.make_async_copy(
                weight_ref.at[lines, here], held.at[side, :, here], sems.at[side, c]
            )
            copy.start()
            copies.append(copy)
    for c in range(chunks):
        here = pl.ds(c * block, block)
        copies[2 * c].wait()
        copies[2 * c + 1].wait()
        total = dot(near_ref[...], held[0, :, here]) + dot(far_ref[...], held[1, :, here])
        for n, out_ref in enumerate(out_refs):
            out_ref[:, here] = total[n * tall : (n + 1) * tall].astype(out_ref.dtype)


def down_base(core, near, far, weight, kinds):
    rows, half = near.shape
    width = weight.shape[1]
    chunks = max(width // 512, 1)
    outs = tuple(jax.ShapeDtypeStruct((rows // len(kinds), width), kind) for kind in kinds)
    return pl.pallas_call(
        down_kernel,
        out_shape=outs,
        grid_spec=pltpu.PrefetchScalarGridSpec(
            num_scalar_prefetch=1,
            grid=(1,),
            in_specs=[fixed(near), fixed(far), pl.BlockSpec(memory_space=pltpu.HBM)],
            out_specs=tuple(fixed(out) for out in outs),
            scratch_shapes=[
                pltpu.VMEM((2, half, width), BF),
                pltpu.SemaphoreType.DMA((2, chunks)),
            ],
        ),
        compiler_params=params(48),
        cost_estimate=cost(4 * rows * half * width, 4 * half * width + 4 * rows * width),
    )(core, near, far, weight)


def low_out_kernel(count, at_ref, mask_ref, *refs):
    parts, shrinks, out_ref = refs[:count], refs[count:-1], refs[-1]
    cap = out_ref.shape[0]
    blocks = [part[r : r + cap] for r in range(0, parts[0].shape[0], cap) for part in parts]
    pairs = sum(dot_last(block, shrink[...]) for block, shrink in zip(blocks, shrinks))
    out_ref[...] = jnp.where(mask_ref[...] > 0, pairs, 0.0)


def low_out_pairs(at, parts, shrink, mask):
    count = len(parts)
    half = parts[0].shape[1]
    cap, depth = mask.shape
    column = lambda b: pl.BlockSpec((depth, half), lambda i, at: (0, at[b]))
    return pl.pallas_call(
        functools.partial(low_out_kernel, count),
        out_shape=jax.ShapeDtypeStruct((cap, depth), F32),
        grid_spec=pltpu.PrefetchScalarGridSpec(
            num_scalar_prefetch=1,
            grid=(1,),
            in_specs=[fixed(mask)]
            + [fixed(part) for part in parts]
            + [column(b) for b in range(at.shape[0])],
            out_specs=fixed(mask),
        ),
        compiler_params=params(16),
        cost_estimate=cost(
            2 * cap * depth * at.shape[0] * half, 2 * at.shape[0] * half * (depth + cap)
        ),
    )(at, mask, *parts, *[shrink] * at.shape[0])


def add_kernel(owners, *refs):
    base_refs, refs = refs[:owners], refs[owners:]
    low_refs, refs = refs[: 2 * owners], refs[2 * owners :]
    pick_refs, expand_refs, out_refs = refs[:owners], refs[owners : 2 * owners], refs[2 * owners :]
    spreads = []
    for n in range(owners):
        low = (low_refs[2 * n][...] + low_refs[2 * n + 1][...]).astype(BF)
        spread = lax.dot_general(
            pick_refs[n][...], low, (((0,), (0,)), ((), ())), preferred_element_type=F32
        )
        spreads.append(spread.astype(BF))
    spread = jnp.concatenate(spreads, axis=1)
    own_rows, width = out_refs[0].shape
    block = min(1024, width)
    for first in range(0, width, block):
        here = pl.ds(first, block)
        expand = jnp.concatenate([ref[:, here] for ref in expand_refs], axis=0)
        total = dot(spread, expand)
        for base_ref in base_refs:
            total += base_ref[:, here].astype(F32)
        for b, out_ref in enumerate(out_refs):
            out_ref[:, here] = total[b * own_rows : (b + 1) * own_rows].astype(BF)


def add_delta(bases, lows, picks, expands, count):
    rows, width = bases[0].shape
    depth = expands[0].shape[0]
    return pl.pallas_call(
        functools.partial(add_kernel, len(bases)),
        out_shape=(jax.ShapeDtypeStruct((rows // count, width), BF),) * count,
        compiler_params=params(32),
        cost_estimate=cost(
            2 * rows * depth * len(bases) * width, width * (6 * rows + 2 * depth) * len(bases)
        ),
    )(*bases, *lows, *picks, *expands)


def tied(first, *others):
    return lax.optimization_barrier((first, *others))


def per_device(
    tokens,
    gate_weight,
    up_weight,
    down_weight,
    shrink_gu,
    expand_gu,
    shrink_down,
    expand_down,
    variant_ids,
    variant_slot,
):
    ways = Ways()
    shards, order = ways.shards, ways.order
    me = lax.axis_index("ff").astype(I32)
    core = lax.axis_index("var").astype(I32)
    groups = lax.axis_size("groups")
    own_rows, width = tokens.shape
    rows = own_rows * shards
    slots = shrink_gu.shape[0]
    variants = variant_slot.shape[0]
    rank = shrink_down.shape[1]
    half_rank = expand_gu.shape[2]
    half = gate_weight.shape[1] // 2
    most = min(slots * MOST, rows)
    here = core.reshape(1)
    there = 1 - here
    at_here = 2 * order + core
    at_there = 2 * order + 1 - core
    split = ways.fast if ways.direct else 1
    swap = lambda a: lax.ppermute(a, "var", [(0, 1), (1, 0)])

    token_parts = ways.gather(tokens)
    kept, near, far, shrink_in = stage(
        at_here,
        at_there,
        tokens,
        expand_gu.reshape(slots * 2 * half_rank, -1),
        shrink_gu.reshape(slots * 2 * rank, width),
    )
    far = swap(far)
    if ways.direct:
        token_parts[0] = kept
        variant_ids, token_parts[ways.slow + 1] = tied(variant_ids, token_parts[ways.slow + 1])

    ids = variant_ids[:, 0]
    matches = ids[:, None] == jnp.arange(variants, dtype=I32)[None, :]
    slot_row = jnp.sum(jnp.where(matches, variant_slot[None, :], 0), axis=1)
    owner = slot_row // slots
    index = jnp.arange(rows, dtype=I32)
    earlier = (owner[:, None] == owner[None, :]) & (index[None, :] < index[:, None])
    place = jnp.sum(earlier.astype(I32), axis=1)
    highest = jnp.max(place).reshape(1)
    for turn in range(1, groups):
        pairs = [(g, (g + turn) % groups) for g in range(groups)]
        highest = jnp.maximum(highest, lax.ppermute(highest, "groups", pairs))
    where_row = order[:, None] == jnp.arange(shards, dtype=I32)[None, :]
    turned = lambda a: jnp.sum(
        jnp.where(where_row[:, :, None], a.reshape(1, shards, own_rows), 0), axis=1
    ).reshape(rows)
    slot_row, place = turned(slot_row), turned(place)
    owner = slot_row // slots
    named = owner[:, None] == order[None, :]
    step = jnp.sum(jnp.where(named, jnp.arange(shards, dtype=I32)[None, :], 0), axis=1)
    arrival = jnp.sum(jnp.where(named, ways.arrival()[None, :], 0), axis=1)
    local = slot_row - me * slots
    kinds = jnp.arange(2, dtype=I32)
    in_cols = jnp.arange(slots * 2 * rank, dtype=I32)
    mask_in = (local[:, None] == (in_cols // (2 * rank))[None, :]).astype(F32)
    rank_at = in_cols % rank
    kind_at = in_cols // rank % 2
    row_at = in_cols // (2 * rank) * (2 * half_rank) + kind_at * half_rank + rank_at % half_rank
    depth = slots * 2 * half_rank
    both_cols = jnp.arange(2 * depth, dtype=I32)
    wanted = row_at + jnp.where(rank_at // half_rank == core, 0, depth)
    hit = wanted[:, None] == both_cols[None, :]
    cols = (hit[None] & (kind_at[None, :] == kinds[:, None])[:, :, None]).astype(BF)

    highest, token_parts[-1] = tied(highest, token_parts[-1])
    x, low_own = low_in_pairs(token_parts, shrink_in, mask_in)
    low_got = swap(low_own)

    def partial_sums(cap):
        cells = jnp.arange(shards * cap, dtype=I32)
        send_rows = (cells[:, None] == (step * cap + place)[None, :]).astype(BF)
        kind_cell = (arrival * 2 + kinds[:, None]) * cap + place
        kind_cells = jnp.arange(2 * shards * cap, dtype=I32)
        place_rows = (kind_cell[:, :, None] == kind_cells).astype(BF).reshape(2 * rows, -1)
        spots = jnp.arange(cap, dtype=I32)
        picked = (spots[:, None] == place[None, :]) & (owner[None, :] == me)
        pick = picked.astype(BF)
        spot_slot = jnp.sum(jnp.where(picked, local[None, :] + 1, 0), axis=1) - 1
        out_cols = jnp.arange(slots * rank, dtype=I32)
        mask_out = (spot_slot[:, None] == (out_cols // rank)[None, :]).astype(F32)

        made = expand_rows(low_own, low_got, pick, cols, near, far, shards, split)
        held, *made = tied(x, *made)
        expand = expand_down.reshape(slots * rank, width)
        if split == 2:
            beside = lax.ppermute(made[1], "ff", ways.back(0, 1))
            base_there = base_half(there, held, gate_weight, up_weight, half, BF)
            base_there, beside, expand = tied(base_there, beside, expand)
            made = relay(made[0], beside, ways.slow)
            held, *made = tied(held, *made)
            delta = ways.slow_steps(made)
            expand_beside = lax.ppermute(expand, "ff", ways.back(0, 1))
        else:
            base_there = base_half(there, held, gate_weight, up_weight, half, BF)
            delta = ways.spread(made[0].reshape(shards, 2 * cap, half))
            delta = [delta.reshape(2 * shards * cap, half)]
        base_got = swap(base_there)
        base_own = base_half(here, held, gate_weight, up_weight, half, F32)
        if split == 2:
            base_own, expand_beside = tied(base_own, expand_beside)
        hidden, *sent = hidden_half(base_own, base_got, delta, place_rows, send_rows, split)
        hidden_far = swap(hidden)
        shrink = shrink_down.reshape(slots * rank, -1)
        if split == 2:
            beside = lax.ppermute(sent[1], "ff", ways.back(0, 1))
            base, base_sent = down_base(here, hidden, hidden_far, down_weight, (F32, BF))
            base_sent, beside = tied(base_sent, beside)
            base_beside = lax.ppermute(base_sent, "ff", ways.back(0, 1))
            got = ways.slow_steps(relay(sent[0], beside, ways.slow))
        else:
            (base,) = down_base(here, hidden, hidden_far, down_weight, (F32,))
            got = [ways.spread(sent[0].reshape(shards, cap, half)).reshape(shards * cap, half)]
        base, *got = tied(base, *got)
        out_own = low_out_pairs(at_here, got, shrink, mask_out)
        out_got = swap(out_own)
        if split == 1:
            parts = add_delta([base], [out_own, out_got], [pick], [expand], shards)
            return list(ways.spread(jnp.stack(parts)))
        out_beside = lax.ppermute(out_own, "ff", ways.back(0, 1))
        across = [
            (2 * f + v, 2 * g + 1 - v) for f, g in ways.back(0, 1) for v in range(2)
        ]
        out_across = lax.ppermute(out_own, ("ff", "var"), across)
        near_rows = rows // 2
        next_owner = order[ways.slow]
        next_pick = (spots[:, None] == place[None, :]) & (owner[None, :] == next_owner)
        parts = add_delta(
            [base, base_beside],
            [out_own, out_got, out_beside, out_across],
            [pick[:, :near_rows], next_pick.astype(BF)[:, :near_rows]],
            [expand, expand_beside],
            ways.slow,
        )
        return ways.slow_steps(parts)

    if most <= USUAL:
        parts = partial_sums(most)
    else:
        parts = lax.cond(
            highest[0] < USUAL, lambda: partial_sums(USUAL), lambda: partial_sums(most)
        )
    return sum(part.astype(F32) for part in parts).astype(BF)


def solution(mesh):
    placed = (
        P(("groups", "ff"), "var"),
        P("var", "ff"),
        P("var", "ff"),
        P("ff", "var"),
        P(("groups", "ff"), None, "var"),
        P(("groups", "ff"), None, "var", None),
        P(("groups", "ff"), None, None),
        P(("groups", "ff"), None, "var"),
        P("groups", None),
        P("groups"),
    )
    return jax.shard_map(
        per_device,
        mesh=mesh,
        in_specs=placed,
        out_specs=P(("groups", "ff"), "var"),
        check_vma=False,
    )
```

```python
import functools

import jax
import jax.numpy as jnp
from jax import lax
from jax.experimental import pallas as pl
from jax.experimental.pallas import tpu as pltpu
from jax.sharding import PartitionSpec as P

MOST = 8
DIRECT = 8
USUAL = 16
BF = jnp.bfloat16
F32 = jnp.float32
I32 = jnp.int32
MIB = 1024 * 1024


def dot(a, b):
    return jnp.dot(a, b, preferred_element_type=F32)


def dot_last(a, b):
    return lax.dot_general(a, b, (((1,), (1,)), ((), ())), preferred_element_type=F32)


def params(mib):
    return pltpu.CompilerParams(vmem_limit_bytes=int(mib * MIB))


def cost(flops, moved):
    return pl.CostEstimate(flops=flops, bytes_accessed=moved, transcendentals=0)


def fixed(array):
    zeros = (0,) * array.ndim
    return pl.BlockSpec(array.shape, lambda *_: zeros)


class Ways:
    def __init__(self):
        self.shards = lax.axis_size("ff")
        self.fast = 2 if self.shards % 2 == 0 else 1
        self.slow = self.shards // self.fast
        self.direct = self.shards <= DIRECT
        me = lax.axis_index("ff").astype(I32)
        steps = jnp.arange(self.shards, dtype=I32)
        if self.direct:
            slow = (me // self.fast - steps % self.slow) % self.slow
            fast = (me % self.fast - steps // self.slow) % self.fast
            self.order = slow * self.fast + fast
        else:
            self.order = steps

    def arrival(self):
        steps = jnp.arange(self.shards, dtype=I32)
        if not self.direct:
            return steps
        return steps % self.slow * self.fast + steps // self.slow

    def back(self, a, c):
        S, F = self.slow, self.fast
        return [(s * F + f, (s - a) % S * F + (f - c) % F) for s in range(S) for f in range(F)]

    def gather(self, block):
        if not self.direct:
            return list(lax.all_gather(block, "ff"))
        got = [block] + [
            lax.ppermute(block, "ff", self.back(-a, 0)) for a in range(1, self.slow)
        ]
        for c in range(1, self.fast):
            got += [lax.ppermute(part, "ff", self.back(0, -c)) for part in got[: self.slow]]
        return got

    def spread(self, blocks):
        return lax.all_to_all(blocks, "ff", 0, 0, tiled=True)

    def slow_steps(self, blocks):
        got = [blocks[0]] + [None] * (self.slow - 1)
        for a in range(1, self.slow):
            got[(-a) % self.slow] = lax.ppermute(blocks[a], "ff", self.back(a, 0))
        return got


def stage_kernel(
    here_ref, there_ref, x_ref, expand_ref, shrink_ref, kept_ref, near_ref, far_ref, held_ref, sems
):
    half = near_ref.shape[1] // (sems.shape[0] - 1)
    copies = []
    for side, (at_ref, out) in enumerate(((there_ref, far_ref), (here_ref, near_ref))):
        for b in range(sems.shape[0] - 1):
            columns = pl.ds(pl.multiple_of(at_ref[b] * half, half), half)
            put = out.at[:, pl.ds(b * half, half)]
            copies.append(pltpu.make_async_copy(expand_ref.at[:, columns], put, sems.at[b, side]))
    copies.append(pltpu.make_async_copy(shrink_ref, held_ref, sems.at[sems.shape[0] - 1, 0]))
    copies.append(pltpu.make_async_copy(x_ref, kept_ref, sems.at[sems.shape[0] - 1, 1]))
    for copy in copies:
        copy.start()
    for copy in copies:
        copy.wait()


def stage(at_here, at_there, x, expand, shrink):
    depth, width = expand.shape
    shards = at_here.shape[0]
    out = jax.ShapeDtypeStruct((depth, width // 2), BF)
    return pl.pallas_call(
        stage_kernel,
        out_shape=(
            jax.ShapeDtypeStruct(x.shape, BF),
            out,
            out,
            jax.ShapeDtypeStruct(shrink.shape, BF),
        ),
        grid_spec=pltpu.PrefetchScalarGridSpec(
            num_scalar_prefetch=2,
            grid=(1,),
            in_specs=[pl.BlockSpec(memory_space=pltpu.HBM)] * 3,
            out_specs=(fixed(x), fixed(out), fixed(out), fixed(shrink)),
            scratch_shapes=[pltpu.SemaphoreType.DMA((shards + 1, 2))],
        ),
        compiler_params=params(51),
        cost_estimate=cost(0, 2 * (2 * expand.size + 2 * shrink.size)),
    )(at_here, at_there, x, expand, shrink)


def low_in_kernel(count, shrink_ref, mask_ref, *refs):
    parts, x_ref, out_ref = refs[:count], refs[count], refs[count + 1]
    x = jnp.concatenate([part[...].astype(F32) for part in parts], axis=0).astype(BF)
    x_ref[...] = x

    @pl.when(pl.program_id(0) == 0)
    def _():
        out_ref[...] = jnp.zeros_like(out_ref)

    out_ref[...] += jnp.where(mask_ref[...] > 0, dot_last(x, shrink_ref[...]), 0.0)


def low_in_pairs(parts, shrink, mask):
    count = len(parts)
    own_rows, width = parts[0].shape
    rows, block = count * own_rows, min(1024, width)
    return pl.pallas_call(
        lambda *refs: low_in_kernel(count, *refs),
        out_shape=(
            jax.ShapeDtypeStruct((rows, width), BF),
            jax.ShapeDtypeStruct(mask.shape, F32),
        ),
        grid=(width // block,),
        in_specs=[pl.BlockSpec((shrink.shape[0], block), lambda n: (0, n)), fixed(mask)]
        + [pl.BlockSpec((own_rows, block), lambda n: (0, n))] * count,
        out_specs=(pl.BlockSpec((rows, block), lambda n: (0, n)), fixed(mask)),
        compiler_params=params(16),
        cost_estimate=cost(2 * rows * width * shrink.shape[0], 2 * shrink.size + 4 * rows * width),
    )(shrink, mask, *parts)


def expand_kernel(fast, own_ref, got_ref, pick_ref, cols_ref, near_ref, far_ref, *out_refs):
    low = (own_ref[...] + got_ref[...]).astype(BF)
    picked = dot(pick_ref[...], low).astype(BF)
    lhs = jnp.concatenate([dot(picked, cols_ref[kind]) for kind in range(2)], axis=0).astype(BF)
    tall = lhs.shape[0]
    half = out_refs[0].shape[1]
    count = near_ref.shape[1] // half
    for b in range(count):
        here = pl.ds(b * half, half)
        both = jnp.concatenate([near_ref[:, here], far_ref[:, here]], axis=0)
        at = b % (count // fast)
        out_refs[b * fast // count][pl.ds(at * tall, tall)] = dot(lhs, both).astype(BF)


def expand_rows(own, got, pick, cols, near, far, shards, fast):
    cap = pick.shape[0]
    depth, width = near.shape
    out = jax.ShapeDtypeStruct((2 * cap * shards // fast, width // shards), BF)
    return pl.pallas_call(
        functools.partial(expand_kernel, fast),
        out_shape=(out,) * fast,
        compiler_params=params(16),
        cost_estimate=cost(8 * cap * depth * width, 4 * (depth + cap) * width),
    )(own, got, pick, cols, near, far)


def base_kernel(side_ref, x_ref, gate_ref, up_ref, out_ref, held, sums, sems):
    half = held.shape[2]
    chunks = sems.shape[1]
    depth = held.shape[1] // chunks
    columns = pl.ds(pl.multiple_of(side_ref[0] * half, half), half)
    copies = []
    for c in range(chunks):
        here = pl.ds(c * depth, depth)
        for kind, weight in enumerate((gate_ref, up_ref)):
            copy = pltpu.make_async_copy(
                weight.at[here, columns], held.at[kind, here], sems.at[kind, c]
            )
            copy.start()
            copies.append((kind, here, copy))
    for kind, here, copy in copies:
        copy.wait()
        part = dot(x_ref[:, here], held[kind, here])
        sums[kind] = part if here.start == 0 else sums[kind] + part
    out_ref[...] = sums[...].astype(out_ref.dtype)


def base_half(side, x, gate_weight, up_weight, half, kind):
    rows, width = x.shape
    chunks = max(width // 512, 1)
    return pl.pallas_call(
        base_kernel,
        out_shape=jax.ShapeDtypeStruct((2, rows, half), kind),
        grid_spec=pltpu.PrefetchScalarGridSpec(
            num_scalar_prefetch=1,
            grid=(1,),
            in_specs=[fixed(x)] + [pl.BlockSpec(memory_space=pltpu.HBM)] * 2,
            out_specs=pl.BlockSpec((2, rows, half), lambda n, side: (0, 0, 0)),
            scratch_shapes=[
                pltpu.VMEM((2, width, half), BF),
                pltpu.VMEM((2, rows, half), F32),
                pltpu.SemaphoreType.DMA((2, chunks)),
            ],
        ),
        compiler_params=params(48),
        cost_estimate=cost(4 * rows * width * half, 4 * width * half + 2 * rows * width),
    )(side, x, gate_weight, up_weight)


def hidden_kernel(count, own_ref, got_ref, place_ref, send_ref, *refs):
    parts, hid_ref, out_refs = refs[:count], refs[count], refs[count + 1 :]
    rows = hid_ref.shape[0]
    tall = out_refs[0].shape[0]
    delta = dot(place_ref[...], jnp.concatenate([part[...] for part in parts], axis=0))
    gate = own_ref[0] + got_ref[0].astype(F32) + delta[:rows]
    up = own_ref[1] + got_ref[1].astype(F32) + delta[rows:]
    hidden = (gate / (1.0 + jnp.exp(-gate)) * up).astype(BF)
    hid_ref[...] = hidden
    sent = dot(send_ref[...], hidden).astype(BF)
    for n, out_ref in enumerate(out_refs):
        out_ref[...] = sent[n * tall : (n + 1) * tall]


def hidden_half(own, got, parts, place, send, count):
    rows, half = own.shape[1:]
    block = min(256, half)
    tall = send.shape[0] // count
    both = pl.BlockSpec((2, rows, block), lambda n: (0, 0, n))
    flat = lambda depth: pl.BlockSpec((depth, block), lambda n: (0, n))
    return pl.pallas_call(
        functools.partial(hidden_kernel, len(parts)),
        out_shape=(jax.ShapeDtypeStruct((rows, half), BF),)
        + (jax.ShapeDtypeStruct((tall, half), BF),) * count,
        grid=(half // block,),
        in_specs=[both, both, fixed(place), fixed(send)] + [flat(part.shape[0]) for part in parts],
        out_specs=(flat(rows),) + (flat(tall),) * count,
        compiler_params=params(40),
        cost_estimate=cost(
            2 * half * (place.size + send.size),
            2 * half * (6 * rows + place.shape[1] + send.shape[0]),
        ),
    )(own, got, place, send, *parts)


def relay_kernel(own_ref, got_ref, *out_refs):
    cap = out_refs[0].shape[0] // 2
    for a, out_ref in enumerate(out_refs):
        here = pl.ds(a * cap, cap)
        out_ref[:cap] = own_ref[here]
        out_ref[cap:] = got_ref[here]


def relay(own, got, count):
    tall, half = own.shape
    return pl.pallas_call(
        relay_kernel,
        out_shape=(jax.ShapeDtypeStruct((2 * tall // count, half), BF),) * count,
        compiler_params=params(16),
        cost_estimate=cost(0, 8 * tall * half),
    )(own, got)


def down_kernel(core_ref, near_ref, far_ref, weight_ref, *refs):
    out_refs, held, sems = refs[:-2], refs[-2], refs[-1]
    chunks = sems.shape[1]
    half, width = held.shape[1:]
    block = width // chunks
    tall = out_refs[0].shape[0]
    copies = []
    for c in range(chunks):
        here = pl.ds(c * block, block)
        for side, at in enumerate((core_ref[0], 1 - core_ref[0])):
            lines = pl.ds(pl.multiple_of(at * half, half), half)
            copy = pltpu.make_async_copy(
                weight_ref.at[lines, here], held.at[side, :, here], sems.at[side, c]
            )
            copy.start()
            copies.append(copy)
    for c in range(chunks):
        here = pl.ds(c * block, block)
        copies[2 * c].wait()
        copies[2 * c + 1].wait()
        total = dot(near_ref[...], held[0, :, here]) + dot(far_ref[...], held[1, :, here])
        for n, out_ref in enumerate(out_refs):
            out_ref[:, here] = total[n * tall : (n + 1) * tall].astype(out_ref.dtype)


def down_base(core, near, far, weight, kinds):
    rows, half = near.shape
    width = weight.shape[1]
    chunks = max(width // 512, 1)
    outs = tuple(jax.ShapeDtypeStruct((rows // len(kinds), width), kind) for kind in kinds)
    return pl.pallas_call(
        down_kernel,
        out_shape=outs,
        grid_spec=pltpu.PrefetchScalarGridSpec(
            num_scalar_prefetch=1,
            grid=(1,),
            in_specs=[fixed(near), fixed(far), pl.BlockSpec(memory_space=pltpu.HBM)],
            out_specs=tuple(fixed(out) for out in outs),
            scratch_shapes=[
                pltpu.VMEM((2, half, width), BF),
                pltpu.SemaphoreType.DMA((2, chunks)),
            ],
        ),
        compiler_params=params(48),
        cost_estimate=cost(4 * rows * half * width, 4 * half * width + 4 * rows * width),
    )(core, near, far, weight)


def low_out_kernel(count, at_ref, mask_ref, *refs):
    parts, shrinks, out_ref = refs[:count], refs[count:-1], refs[-1]
    cap = out_ref.shape[0]
    blocks = [part[r : r + cap] for r in range(0, parts[0].shape[0], cap) for part in parts]
    pairs = sum(dot_last(block, shrink[...]) for block, shrink in zip(blocks, shrinks))
    out_ref[...] = jnp.where(mask_ref[...] > 0, pairs, 0.0)


def low_out_pairs(at, parts, shrink, mask):
    count = len(parts)
    half = parts[0].shape[1]
    cap, depth = mask.shape
    column = lambda b: pl.BlockSpec((depth, half), lambda i, at: (0, at[b]))
    return pl.pallas_call(
        functools.partial(low_out_kernel, count),
        out_shape=jax.ShapeDtypeStruct((cap, depth), F32),
        grid_spec=pltpu.PrefetchScalarGridSpec(
            num_scalar_prefetch=1,
            grid=(1,),
            in_specs=[fixed(mask)]
            + [fixed(part) for part in parts]
            + [column(b) for b in range(at.shape[0])],
            out_specs=fixed(mask),
        ),
        compiler_params=params(16),
        cost_estimate=cost(
            2 * cap * depth * at.shape[0] * half, 2 * at.shape[0] * half * (depth + cap)
        ),
    )(at, mask, *parts, *[shrink] * at.shape[0])


def add_kernel(owners, *refs):
    base_refs, refs = refs[:owners], refs[owners:]
    low_refs, refs = refs[: 2 * owners], refs[2 * owners :]
    pick_refs, expand_refs, out_refs = refs[:owners], refs[owners : 2 * owners], refs[2 * owners :]
    spreads = []
    for n in range(owners):
        low = (low_refs[2 * n][...] + low_refs[2 * n + 1][...]).astype(BF)
        spread = lax.dot_general(
            pick_refs[n][...], low, (((0,), (0,)), ((), ())), preferred_element_type=F32
        )
        spreads.append(spread.astype(BF))
    spread = jnp.concatenate(spreads, axis=1)
    own_rows, width = out_refs[0].shape
    block = min(1024, width)
    for first in range(0, width, block):
        here = pl.ds(first, block)
        expand = jnp.concatenate([ref[:, here] for ref in expand_refs], axis=0)
        total = dot(spread, expand)
        for base_ref in base_refs:
            total += base_ref[:, here].astype(F32)
        for b, out_ref in enumerate(out_refs):
            out_ref[:, here] = total[b * own_rows : (b + 1) * own_rows].astype(BF)


def add_delta(bases, lows, picks, expands, count):
    rows, width = bases[0].shape
    depth = expands[0].shape[0]
    return pl.pallas_call(
        functools.partial(add_kernel, len(bases)),
        out_shape=(jax.ShapeDtypeStruct((rows // count, width), BF),) * count,
        compiler_params=params(32),
        cost_estimate=cost(
            2 * rows * depth * len(bases) * width, width * (6 * rows + 2 * depth) * len(bases)
        ),
    )(*bases, *lows, *picks, *expands)


def tied(first, *others):
    return lax.optimization_barrier((first, *others))


def per_device(
    tokens,
    gate_weight,
    up_weight,
    down_weight,
    shrink_gu,
    expand_gu,
    shrink_down,
    expand_down,
    variant_ids,
    variant_slot,
):
    ways = Ways()
    shards, order = ways.shards, ways.order
    me = lax.axis_index("ff").astype(I32)
    core = lax.axis_index("var").astype(I32)
    groups = lax.axis_size("groups")
    own_rows, width = tokens.shape
    rows = own_rows * shards
    slots = shrink_gu.shape[0]
    variants = variant_slot.shape[0]
    rank = shrink_down.shape[1]
    half_rank = expand_gu.shape[2]
    half = gate_weight.shape[1] // 2
    most = min(slots * MOST, rows)
    here = core.reshape(1)
    there = 1 - here
    at_here = 2 * order + core
    at_there = 2 * order + 1 - core
    split = ways.fast if ways.direct else 1
    swap = lambda a: lax.ppermute(a, "var", [(0, 1), (1, 0)])

    named = jnp.concatenate([variant_ids[:, 0], variant_slot])
    all_named = [named]
    for turn in range(1, groups):
        pairs = [(g, (g + turn) % groups) for g in range(groups)]
        all_named.append(lax.ppermute(named, "groups", pairs))
    all_named = jnp.stack(all_named)

    token_parts = ways.gather(tokens)
    if ways.direct:
        all_named, at_here, at_there, token_parts[ways.slow + 1] = tied(
            all_named, at_here, at_there, token_parts[ways.slow + 1]
        )
    kept, near, far, shrink_in = stage(
        at_here,
        at_there,
        tokens,
        expand_gu.reshape(slots * 2 * half_rank, -1),
        shrink_gu.reshape(slots * 2 * rank, width),
    )
    far = swap(far)
    if ways.direct:
        token_parts[0] = kept

    ids, id_slots = all_named[:, :rows], all_named[:, rows:]
    matches = ids[:, :, None] == jnp.arange(variants, dtype=I32)
    slot_row = jnp.sum(jnp.where(matches, id_slots[:, None, :], 0), axis=2)
    owner = slot_row // slots
    index = jnp.arange(rows, dtype=I32)
    earlier = (owner[:, :, None] == owner[:, None, :]) & (index[None, :] < index[:, None])
    place = jnp.sum(earlier.astype(I32), axis=2)
    highest = jnp.max(place).reshape(1)
    slot_row, place = slot_row[0], place[0]
    where_row = order[:, None] == jnp.arange(shards, dtype=I32)[None, :]
    turned = lambda a: jnp.sum(
        jnp.where(where_row[:, :, None], a.reshape(1, shards, own_rows), 0), axis=1
    ).reshape(rows)
    slot_row, place = turned(slot_row), turned(place)
    owner = slot_row // slots
    of_block = owner[:, None] == order[None, :]
    step = jnp.sum(jnp.where(of_block, jnp.arange(shards, dtype=I32)[None, :], 0), axis=1)
    arrival = jnp.sum(jnp.where(of_block, ways.arrival()[None, :], 0), axis=1)
    local = slot_row - me * slots
    kinds = jnp.arange(2, dtype=I32)
    in_cols = jnp.arange(slots * 2 * rank, dtype=I32)
    mask_in = (local[:, None] == (in_cols // (2 * rank))[None, :]).astype(F32)
    rank_at = in_cols % rank
    kind_at = in_cols // rank % 2
    row_at = in_cols // (2 * rank) * (2 * half_rank) + kind_at * half_rank + rank_at % half_rank
    depth = slots * 2 * half_rank
    both_cols = jnp.arange(2 * depth, dtype=I32)
    wanted = row_at + jnp.where(rank_at // half_rank == core, 0, depth)
    hit = wanted[:, None] == both_cols[None, :]
    cols = (hit[None] & (kind_at[None, :] == kinds[:, None])[:, :, None]).astype(BF)

    x, low_own = low_in_pairs(token_parts, shrink_in, mask_in)
    low_got = swap(low_own)

    def partial_sums(cap):
        cells = jnp.arange(shards * cap, dtype=I32)
        send_rows = (cells[:, None] == (step * cap + place)[None, :]).astype(BF)
        kind_cell = (arrival * 2 + kinds[:, None]) * cap + place
        kind_cells = jnp.arange(2 * shards * cap, dtype=I32)
        place_rows = (kind_cell[:, :, None] == kind_cells).astype(BF).reshape(2 * rows, -1)
        spots = jnp.arange(cap, dtype=I32)
        picked = (spots[:, None] == place[None, :]) & (owner[None, :] == me)
        pick = picked.astype(BF)
        spot_slot = jnp.sum(jnp.where(picked, local[None, :] + 1, 0), axis=1) - 1
        out_cols = jnp.arange(slots * rank, dtype=I32)
        mask_out = (spot_slot[:, None] == (out_cols // rank)[None, :]).astype(F32)

        made = expand_rows(low_own, low_got, pick, cols, near, far, shards, split)
        held, *made = tied(x, *made)
        expand = expand_down.reshape(slots * rank, width)
        if split == 2:
            beside = lax.ppermute(made[1], "ff", ways.back(0, 1))
            base_there = base_half(there, held, gate_weight, up_weight, half, BF)
            base_there, beside, expand = tied(base_there, beside, expand)
            made = relay(made[0], beside, ways.slow)
            held, *made = tied(held, *made)
            delta = ways.slow_steps(made)
            expand_beside = lax.ppermute(expand, "ff", ways.back(0, 1))
        else:
            base_there = base_half(there, held, gate_weight, up_weight, half, BF)
            delta = ways.spread(made[0].reshape(shards, 2 * cap, half))
            delta = [delta.reshape(2 * shards * cap, half)]
        base_got = swap(base_there)
        base_own = base_half(here, held, gate_weight, up_weight, half, F32)
        if split == 2:
            base_own, expand_beside = tied(base_own, expand_beside)
        hidden, *sent = hidden_half(base_own, base_got, delta, place_rows, send_rows, split)
        hidden_far = swap(hidden)
        shrink = shrink_down.reshape(slots * rank, -1)
        if split == 2:
            beside = lax.ppermute(sent[1], "ff", ways.back(0, 1))
            base, base_sent = down_base(here, hidden, hidden_far, down_weight, (F32, BF))
            base_sent, beside = tied(base_sent, beside)
            base_beside = lax.ppermute(base_sent, "ff", ways.back(0, 1))
            got = ways.slow_steps(relay(sent[0], beside, ways.slow))
        else:
            (base,) = down_base(here, hidden, hidden_far, down_weight, (F32,))
            got = [ways.spread(sent[0].reshape(shards, cap, half)).reshape(shards * cap, half)]
        if split == 2:
            base_beside, *got = tied(base_beside, *got)
        base, *got = tied(base, *got)
        out_own = low_out_pairs(at_here, got, shrink, mask_out)
        out_got = swap(out_own)
        if split == 1:
            parts = add_delta([base], [out_own, out_got], [pick], [expand], shards)
            return list(ways.spread(jnp.stack(parts)))
        out_beside = lax.ppermute(out_own, "ff", ways.back(0, 1))
        across = [
            (2 * f + v, 2 * g + 1 - v) for f, g in ways.back(0, 1) for v in range(2)
        ]
        out_across = lax.ppermute(out_own, ("ff", "var"), across)
        near_rows = rows // 2
        next_owner = order[ways.slow]
        next_pick = (spots[:, None] == place[None, :]) & (owner[None, :] == next_owner)
        parts = add_delta(
            [base, base_beside],
            [out_own, out_got, out_beside, out_across],
            [pick[:, :near_rows], next_pick.astype(BF)[:, :near_rows]],
            [expand, expand_beside],
            ways.slow,
        )
        return ways.slow_steps(parts)

    if most <= USUAL:
        parts = partial_sums(most)
    else:
        parts = lax.cond(
            highest[0] < USUAL, lambda: partial_sums(USUAL), lambda: partial_sums(most)
        )
    return sum(part.astype(F32) for part in parts).astype(BF)


def solution(mesh):
    placed = (
        P(("groups", "ff"), "var"),
        P("var", "ff"),
        P("var", "ff"),
        P("ff", "var"),
        P(("groups", "ff"), None, "var"),
        P(("groups", "ff"), None, "var", None),
        P(("groups", "ff"), None, None),
        P(("groups", "ff"), None, "var"),
        P("groups", None),
        P("groups"),
    )
    return jax.shard_map(
        per_device,
        mesh=mesh,
        in_specs=placed,
        out_specs=P(("groups", "ff"), "var"),
        check_vma=False,
    )
```

```python
import functools

import jax
import jax.numpy as jnp
from jax import lax
from jax.experimental import pallas as pl
from jax.experimental.pallas import tpu as pltpu
from jax.sharding import PartitionSpec as P

MOST = 8
DIRECT = 8
MINE, NEXT, STEP, PLACE = range(4)
USUAL = 16
BF = jnp.bfloat16
F32 = jnp.float32
I32 = jnp.int32
MIB = 1024 * 1024


def dot(a, b):
    return jnp.dot(a, b, preferred_element_type=F32)


def dot_last(a, b):
    return lax.dot_general(a, b, (((1,), (1,)), ((), ())), preferred_element_type=F32)


def params(mib):
    return pltpu.CompilerParams(vmem_limit_bytes=int(mib * MIB))


def cost(flops, moved):
    return pl.CostEstimate(flops=flops, bytes_accessed=moved, transcendentals=0)


SCALARS = pl.BlockSpec(memory_space=pltpu.SMEM)
WHOLE = pl.BlockSpec(memory_space=pltpu.VMEM)
FAR = pl.BlockSpec(memory_space=pltpu.HBM)


def fixed(array):
    zeros = (0,) * array.ndim
    return pl.BlockSpec(array.shape, lambda *_: zeros)


def one_hot(count, cell):
    lines = lax.broadcasted_iota(I32, (count, cell.shape[1]), 0)
    return (lines == cell).astype(F32).astype(BF)


def dot_first(a, b):
    return lax.dot_general(a, b, (((0,), (0,)), ((), ())), preferred_element_type=F32)


class Ways:
    def __init__(self):
        self.shards = lax.axis_size("ff")
        self.fast = 2 if self.shards % 2 == 0 else 1
        self.slow = self.shards // self.fast
        self.direct = self.shards <= DIRECT
        me = lax.axis_index("ff").astype(I32)
        steps = jnp.arange(self.shards, dtype=I32)
        if self.direct:
            slow = (me // self.fast - steps % self.slow) % self.slow
            fast = (me % self.fast - steps // self.slow) % self.fast
            self.order = slow * self.fast + fast
        else:
            self.order = steps

    def arrival(self):
        steps = jnp.arange(self.shards, dtype=I32)
        if not self.direct:
            return steps
        return steps % self.slow * self.fast + steps // self.slow

    def back(self, a, c):
        S, F = self.slow, self.fast
        return [(s * F + f, (s - a) % S * F + (f - c) % F) for s in range(S) for f in range(F)]

    def gather(self, block):
        if not self.direct:
            return list(lax.all_gather(block, "ff"))
        got = [block] + [
            lax.ppermute(block, "ff", self.back(-a, 0)) for a in range(1, self.slow)
        ]
        for c in range(1, self.fast):
            got += [lax.ppermute(part, "ff", self.back(0, -c)) for part in got[: self.slow]]
        return got

    def spread(self, blocks):
        return lax.all_to_all(blocks, "ff", 0, 0, tiled=True)

    def slow_steps(self, blocks):
        got = [blocks[0]] + [None] * (self.slow - 1)
        for a in range(1, self.slow):
            got[(-a) % self.slow] = lax.ppermute(blocks[a], "ff", self.back(a, 0))
        return got


def stage_kernel(
    here_ref, there_ref, x_ref, expand_ref, shrink_ref, kept_ref, near_ref, far_ref, held_ref, sems
):
    half = near_ref.shape[1] // (sems.shape[0] - 1)
    copies = []
    for side, (at_ref, out) in enumerate(((there_ref, far_ref), (here_ref, near_ref))):
        for b in range(sems.shape[0] - 1):
            columns = pl.ds(pl.multiple_of(at_ref[b] * half, half), half)
            put = out.at[:, pl.ds(b * half, half)]
            copies.append(pltpu.make_async_copy(expand_ref.at[:, columns], put, sems.at[b, side]))
    copies.append(pltpu.make_async_copy(shrink_ref, held_ref, sems.at[sems.shape[0] - 1, 0]))
    copies.append(pltpu.make_async_copy(x_ref, kept_ref, sems.at[sems.shape[0] - 1, 1]))
    for copy in copies:
        copy.start()
    for copy in copies:
        copy.wait()


def stage(at_here, at_there, x, expand, shrink):
    depth, width = expand.shape
    shards = at_here.shape[0]
    out = jax.ShapeDtypeStruct((depth, width // 2), BF)
    return pl.pallas_call(
        stage_kernel,
        out_shape=(
            jax.ShapeDtypeStruct(x.shape, BF),
            out,
            out,
            jax.ShapeDtypeStruct(shrink.shape, BF),
        ),
        in_specs=[SCALARS, SCALARS, FAR, FAR, FAR],
        out_specs=(WHOLE,) * 4,
        scratch_shapes=[pltpu.SemaphoreType.DMA((shards + 1, 2))],
        compiler_params=params(51),
        cost_estimate=cost(0, 2 * (2 * expand.size + 2 * shrink.size)),
    )(at_here, at_there, x, expand, shrink)


def low_in_kernel(count, shrink_ref, mask_ref, *refs):
    parts, x_ref, out_ref = refs[:count], refs[count], refs[count + 1]
    x = jnp.concatenate([part[...].astype(F32) for part in parts], axis=0).astype(BF)
    x_ref[...] = x

    @pl.when(pl.program_id(0) == 0)
    def _():
        out_ref[...] = jnp.zeros_like(out_ref)

    out_ref[...] += jnp.where(mask_ref[...] > 0, dot_last(x, shrink_ref[...]), 0.0)


def low_in_pairs(parts, shrink, mask):
    count = len(parts)
    own_rows, width = parts[0].shape
    rows, block = count * own_rows, min(1024, width)
    return pl.pallas_call(
        lambda *refs: low_in_kernel(count, *refs),
        out_shape=(
            jax.ShapeDtypeStruct((rows, width), BF),
            jax.ShapeDtypeStruct(mask.shape, F32),
        ),
        grid=(width // block,),
        in_specs=[pl.BlockSpec((shrink.shape[0], block), lambda n: (0, n)), fixed(mask)]
        + [pl.BlockSpec((own_rows, block), lambda n: (0, n))] * count,
        out_specs=(pl.BlockSpec((rows, block), lambda n: (0, n)), fixed(mask)),
        compiler_params=params(16),
        cost_estimate=cost(2 * rows * width * shrink.shape[0], 2 * shrink.size + 4 * rows * width),
    )(shrink, mask, *parts)


def expand_kernel(
    cap, fast, own_ref, got_ref, marks_ref, cols_ref, near_ref, far_ref, *out_refs
):
    low = (own_ref[...] + got_ref[...]).astype(BF)
    picked = dot(one_hot(cap, marks_ref[MINE : MINE + 1]), low).astype(BF)
    lhs = jnp.concatenate([dot(picked, cols_ref[kind]) for kind in range(2)], axis=0).astype(BF)
    tall = lhs.shape[0]
    half = out_refs[0].shape[1]
    count = near_ref.shape[1] // half
    for b in range(count):
        here = pl.ds(b * half, half)
        both = jnp.concatenate([near_ref[:, here], far_ref[:, here]], axis=0)
        at = b % (count // fast)
        out_refs[b * fast // count][pl.ds(at * tall, tall)] = dot(lhs, both).astype(BF)


def expand_rows(own, got, marks, cols, near, far, shards, cap, fast):
    depth, width = near.shape
    out = jax.ShapeDtypeStruct((2 * cap * shards // fast, width // shards), BF)
    return pl.pallas_call(
        functools.partial(expand_kernel, cap, fast),
        out_shape=(out,) * fast,
        compiler_params=params(16),
        cost_estimate=cost(8 * cap * depth * width, 4 * (depth + cap) * width),
    )(own, got, marks, cols, near, far)


def base_kernel(side_ref, x_ref, gate_ref, up_ref, out_ref, held, sums, sems):
    half = held.shape[2]
    chunks = sems.shape[1]
    depth = held.shape[1] // chunks
    columns = pl.ds(pl.multiple_of(side_ref[0] * half, half), half)
    copies = []
    for c in range(chunks):
        here = pl.ds(c * depth, depth)
        for kind, weight in enumerate((gate_ref, up_ref)):
            copy = pltpu.make_async_copy(
                weight.at[here, columns], held.at[kind, here], sems.at[kind, c]
            )
            copy.start()
            copies.append((kind, here, copy))
    for kind, here, copy in copies:
        copy.wait()
        part = dot(x_ref[:, here], held[kind, here])
        sums[kind] = part if here.start == 0 else sums[kind] + part
    out_ref[...] = sums[...].astype(out_ref.dtype)


def base_half(side, x, gate_weight, up_weight, half, kind):
    rows, width = x.shape
    chunks = max(width // 512, 1)
    return pl.pallas_call(
        base_kernel,
        out_shape=jax.ShapeDtypeStruct((2, rows, half), kind),
        in_specs=[SCALARS, WHOLE, FAR, FAR],
        out_specs=WHOLE,
        scratch_shapes=[
            pltpu.VMEM((2, width, half), BF),
            pltpu.VMEM((2, rows, half), F32),
            pltpu.SemaphoreType.DMA((2, chunks)),
        ],
        compiler_params=params(48),
        cost_estimate=cost(4 * rows * width * half, 4 * width * half + 2 * rows * width),
    )(side, x, gate_weight, up_weight)


def hidden_kernel(cap, count, own_ref, got_ref, marks_ref, arrive_ref, *refs):
    parts, hid_ref, out_refs = refs[:count], refs[count], refs[count + 1 :]
    rows, half = hid_ref.shape
    cells = sum(part.shape[0] for part in parts)
    place = one_hot(cells, arrive_ref[0:1] * cap + arrive_ref[1:2])
    tall = out_refs[0].shape[0]
    leave = marks_ref[STEP : STEP + 1] * cap + marks_ref[PLACE : PLACE + 1]
    send = one_hot(tall * len(out_refs), leave)
    block = min(256, half)
    for first in range(0, half, block):
        here = pl.ds(first, block)
        delta = dot_first(place, jnp.concatenate([part[:, here] for part in parts], axis=0))
        gate = own_ref[0, :, here] + got_ref[0, :, here].astype(F32) + delta[:rows]
        up = own_ref[1, :, here] + got_ref[1, :, here].astype(F32) + delta[rows:]
        hidden = (gate / (1.0 + jnp.exp(-gate)) * up).astype(BF)
        hid_ref[:, here] = hidden
        sent = dot(send, hidden).astype(BF)
        for n, out_ref in enumerate(out_refs):
            out_ref[:, here] = sent[n * tall : (n + 1) * tall]


def hidden_half(own, got, parts, marks, arrive, cap, shards, count):
    rows, half = own.shape[1:]
    cells = shards * cap
    return pl.pallas_call(
        functools.partial(hidden_kernel, cap, len(parts)),
        out_shape=(jax.ShapeDtypeStruct((rows, half), BF),)
        + (jax.ShapeDtypeStruct((cells // count, half), BF),) * count,
        compiler_params=params(40),
        cost_estimate=cost(10 * half * cells * rows, 2 * half * (6 * rows + 3 * cells)),
    )(own, got, marks, arrive, *parts)


def relay_kernel(own_ref, got_ref, *out_refs):
    cap = out_refs[0].shape[0] // 2
    for a, out_ref in enumerate(out_refs):
        here = pl.ds(a * cap, cap)
        out_ref[:cap] = own_ref[here]
        out_ref[cap:] = got_ref[here]


def relay(own, got, count):
    tall, half = own.shape
    return pl.pallas_call(
        relay_kernel,
        out_shape=(jax.ShapeDtypeStruct((2 * tall // count, half), BF),) * count,
        compiler_params=params(16),
        cost_estimate=cost(0, 8 * tall * half),
    )(own, got)


def down_kernel(core_ref, near_ref, far_ref, weight_ref, *refs):
    out_refs, held, sems = refs[:-2], refs[-2], refs[-1]
    chunks = sems.shape[1]
    half, width = held.shape[1:]
    block = width // chunks
    tall = out_refs[0].shape[0]
    copies = []
    for c in range(chunks):
        here = pl.ds(c * block, block)
        for side, at in enumerate((core_ref[0], 1 - core_ref[0])):
            lines = pl.ds(pl.multiple_of(at * half, half), half)
            copy = pltpu.make_async_copy(
                weight_ref.at[lines, here], held.at[side, :, here], sems.at[side, c]
            )
            copy.start()
            copies.append(copy)
    for c in range(chunks):
        here = pl.ds(c * block, block)
        copies[2 * c].wait()
        copies[2 * c + 1].wait()
        total = dot(near_ref[...], held[0, :, here]) + dot(far_ref[...], held[1, :, here])
        for n, out_ref in enumerate(out_refs):
            out_ref[:, here] = total[n * tall : (n + 1) * tall].astype(out_ref.dtype)


def down_base(core, near, far, weight, kinds):
    rows, half = near.shape
    width = weight.shape[1]
    chunks = max(width // 512, 1)
    outs = tuple(jax.ShapeDtypeStruct((rows // len(kinds), width), kind) for kind in kinds)
    return pl.pallas_call(
        down_kernel,
        out_shape=outs,
        in_specs=[SCALARS, WHOLE, WHOLE, FAR],
        out_specs=(WHOLE,) * len(outs),
        scratch_shapes=[
            pltpu.VMEM((2, half, width), BF),
            pltpu.SemaphoreType.DMA((2, chunks)),
        ],
        compiler_params=params(48),
        cost_estimate=cost(4 * rows * half * width, 4 * half * width + 4 * rows * width),
    )(core, near, far, weight)


def low_out_kernel(cap, count, at_ref, marks_ref, slot_ref, shrink_ref, *refs):
    parts, out_ref = refs[:count], refs[count]
    half = parts[0].shape[1]
    blocks = [part[r : r + cap] for r in range(0, parts[0].shape[0], cap) for part in parts]
    pairs = jnp.zeros(out_ref.shape, F32)
    for b, block in enumerate(blocks):
        columns = pl.ds(pl.multiple_of(at_ref[b] * half, half), half)
        pairs += dot_last(block, shrink_ref[:, columns])
    mask = dot(one_hot(cap, marks_ref[MINE : MINE + 1]), slot_ref[...])
    out_ref[...] = jnp.where(mask > 0.5, pairs, 0.0)


def low_out_pairs(at, marks, slot_mask, shrink, parts, cap):
    count = len(parts)
    half = parts[0].shape[1]
    depth = shrink.shape[0]
    return pl.pallas_call(
        functools.partial(low_out_kernel, cap, count),
        out_shape=jax.ShapeDtypeStruct((cap, depth), F32),
        in_specs=[SCALARS] + [WHOLE] * (3 + count),
        compiler_params=params(16),
        cost_estimate=cost(
            2 * cap * depth * at.shape[0] * half, 2 * at.shape[0] * half * (depth + cap)
        ),
    )(at, marks, slot_mask, shrink, *parts)


def add_kernel(owners, *refs):
    base_refs, refs = refs[:owners], refs[owners:]
    low_refs, refs = refs[: 2 * owners], refs[2 * owners :]
    marks_ref, expand_refs, out_refs = refs[0], refs[1 : owners + 1], refs[owners + 1 :]
    rows = base_refs[0].shape[0]
    spreads = []
    for n in range(owners):
        low = (low_refs[2 * n][...] + low_refs[2 * n + 1][...]).astype(BF)
        pick = one_hot(low.shape[0], marks_ref[MINE + n : MINE + n + 1, :rows])
        spreads.append(dot_first(pick, low).astype(BF))
    spread = jnp.concatenate(spreads, axis=1)
    own_rows, width = out_refs[0].shape
    block = min(1024, width)
    for first in range(0, width, block):
        here = pl.ds(first, block)
        expand = jnp.concatenate([ref[:, here] for ref in expand_refs], axis=0)
        total = dot(spread, expand)
        for base_ref in base_refs:
            total += base_ref[:, here].astype(F32)
        for b, out_ref in enumerate(out_refs):
            out_ref[:, here] = total[b * own_rows : (b + 1) * own_rows].astype(BF)


def add_delta(bases, lows, marks, expands, count):
    rows, width = bases[0].shape
    depth = expands[0].shape[0]
    return pl.pallas_call(
        functools.partial(add_kernel, len(bases)),
        out_shape=(jax.ShapeDtypeStruct((rows // count, width), BF),) * count,
        compiler_params=params(32),
        cost_estimate=cost(
            2 * rows * depth * len(bases) * width, width * (6 * rows + 2 * depth) * len(bases)
        ),
    )(*bases, *lows, marks, *expands)


def tied(first, *others):
    return lax.optimization_barrier((first, *others))


def per_device(
    tokens,
    gate_weight,
    up_weight,
    down_weight,
    shrink_gu,
    expand_gu,
    shrink_down,
    expand_down,
    variant_ids,
    variant_slot,
):
    ways = Ways()
    shards, order = ways.shards, ways.order
    me = lax.axis_index("ff").astype(I32)
    core = lax.axis_index("var").astype(I32)
    groups = lax.axis_size("groups")
    own_rows, width = tokens.shape
    rows = own_rows * shards
    slots = shrink_gu.shape[0]
    variants = variant_slot.shape[0]
    rank = shrink_down.shape[1]
    half_rank = expand_gu.shape[2]
    half = gate_weight.shape[1] // 2
    most = min(slots * MOST, rows)
    here = core.reshape(1)
    there = 1 - here
    at_here = 2 * order + core
    at_there = 2 * order + 1 - core
    split = ways.fast if ways.direct else 1
    swap = lambda a: lax.ppermute(a, "var", [(0, 1), (1, 0)])

    token_parts = ways.gather(tokens)
    if ways.direct:
        variant_ids, variant_slot, at_here, at_there, token_parts[ways.slow + 1] = tied(
            variant_ids, variant_slot, at_here, at_there, token_parts[ways.slow + 1]
        )
    named = jnp.concatenate([variant_ids[:, 0], variant_slot]).reshape(1, -1)
    all_named = [named]
    for turn in range(1, groups):
        pairs = [(g, (g + turn) % groups) for g in range(groups)]
        all_named.append(lax.ppermute(named, "groups", pairs))
    all_named = jnp.concatenate(all_named)
    kept, near, far, shrink_in = stage(
        at_here,
        at_there,
        tokens,
        expand_gu.reshape(slots * 2 * half_rank, -1),
        shrink_gu.reshape(slots * 2 * rank, width),
    )
    far = swap(far)
    if ways.direct:
        token_parts[0] = kept

    ids, id_slots = all_named[:, :rows], all_named[:, rows:]
    matches = ids[:, :, None] == jnp.arange(variants, dtype=I32)
    slot_row = jnp.sum(jnp.where(matches, id_slots[:, None, :], 0), axis=2)
    owner = slot_row // slots
    index = jnp.arange(rows, dtype=I32)
    earlier = (owner[:, :, None] == owner[:, None, :]) & (index[None, :] < index[:, None])
    place = jnp.sum(earlier.astype(I32), axis=2)
    highest = jnp.max(place).reshape(1)
    slot_row, place = slot_row[0], place[0]
    where_row = order[:, None] == jnp.arange(shards, dtype=I32)[None, :]
    turned = lambda a: jnp.sum(
        jnp.where(where_row[:, :, None], a.reshape(1, shards, own_rows), 0), axis=1
    ).reshape(rows)
    slot_row, place = turned(slot_row), turned(place)
    owner = slot_row // slots
    of_block = owner[:, None] == order[None, :]
    step = jnp.sum(jnp.where(of_block, jnp.arange(shards, dtype=I32)[None, :], 0), axis=1)
    arrival = jnp.sum(jnp.where(of_block, ways.arrival()[None, :], 0), axis=1)
    local = slot_row - me * slots
    next_owner = order[ways.slow % shards]
    marks = jnp.stack(
        [jnp.where(owner == me, place, -1), jnp.where(owner == next_owner, place, -1), step, place]
    )
    arrive = jnp.stack(
        [jnp.concatenate([2 * arrival, 2 * arrival + 1]), jnp.concatenate([place, place])]
    )
    kinds = jnp.arange(2, dtype=I32)
    in_cols = jnp.arange(slots * 2 * rank, dtype=I32)
    mask_in = (local[:, None] == (in_cols // (2 * rank))[None, :]).astype(F32)
    out_cols = jnp.arange(slots * rank, dtype=I32)
    slot_mask = (local[:, None] == (out_cols // rank)[None, :]).astype(BF)
    rank_at = in_cols % rank
    kind_at = in_cols // rank % 2
    row_at = in_cols // (2 * rank) * (2 * half_rank) + kind_at * half_rank + rank_at % half_rank
    depth = slots * 2 * half_rank
    both_cols = jnp.arange(2 * depth, dtype=I32)
    wanted = row_at + jnp.where(rank_at // half_rank == core, 0, depth)
    hit = wanted[:, None] == both_cols[None, :]
    cols = (hit[None] & (kind_at[None, :] == kinds[:, None])[:, :, None]).astype(BF)

    x, low_own = low_in_pairs(token_parts, shrink_in, mask_in)
    low_got = swap(low_own)

    def partial_sums(cap):
        made = expand_rows(low_own, low_got, marks, cols, near, far, shards, cap, split)
        held, *made = tied(x, *made)
        expand = expand_down.reshape(slots * rank, width)
        if split == 2:
            beside = lax.ppermute(made[1], "ff", ways.back(0, 1))
            base_there = base_half(there, held, gate_weight, up_weight, half, BF)
            base_there, beside, expand = tied(base_there, beside, expand)
            made = relay(made[0], beside, ways.slow)
            held, *made = tied(held, *made)
            delta = ways.slow_steps(made)
            expand_beside = lax.ppermute(expand, "ff", ways.back(0, 1))
        else:
            base_there = base_half(there, held, gate_weight, up_weight, half, BF)
            delta = ways.spread(made[0].reshape(shards, 2 * cap, half))
            delta = [delta.reshape(2 * shards * cap, half)]
        base_got = swap(base_there)
        base_own = base_half(here, held, gate_weight, up_weight, half, F32)
        if split == 2:
            base_own, expand_beside = tied(base_own, expand_beside)
        hidden, *sent = hidden_half(
            base_own, base_got, delta, marks, arrive, cap, shards, split
        )
        hidden_far = swap(hidden)
        shrink = shrink_down.reshape(slots * rank, -1)
        if split == 2:
            beside = lax.ppermute(sent[1], "ff", ways.back(0, 1))
            base, base_sent = down_base(here, hidden, hidden_far, down_weight, (F32, BF))
            base_sent, beside = tied(base_sent, beside)
            base_beside = lax.ppermute(base_sent, "ff", ways.back(0, 1))
            got = ways.slow_steps(relay(sent[0], beside, ways.slow))
        else:
            (base,) = down_base(here, hidden, hidden_far, down_weight, (F32,))
            got = [ways.spread(sent[0].reshape(shards, cap, half)).reshape(shards * cap, half)]
        if split == 2:
            base_beside, *got = tied(base_beside, *got)
        base, *got = tied(base, *got)
        out_own = low_out_pairs(at_here, marks, slot_mask, shrink, got, cap)
        out_got = swap(out_own)
        if split == 1:
            parts = add_delta([base], [out_own, out_got], marks, [expand], shards)
            return list(ways.spread(jnp.stack(parts)))
        out_beside = lax.ppermute(out_own, "ff", ways.back(0, 1))
        across = [
            (2 * f + v, 2 * g + 1 - v) for f, g in ways.back(0, 1) for v in range(2)
        ]
        out_across = lax.ppermute(out_own, ("ff", "var"), across)
        parts = add_delta(
            [base, base_beside],
            [out_own, out_got, out_beside, out_across],
            marks,
            [expand, expand_beside],
            ways.slow,
        )
        return ways.slow_steps(parts)

    if most <= USUAL:
        parts = partial_sums(most)
    else:
        parts = lax.cond(
            highest[0] < USUAL, lambda: partial_sums(USUAL), lambda: partial_sums(most)
        )
    return sum(part.astype(F32) for part in parts).astype(BF)


def solution(mesh):
    placed = (
        P(("groups", "ff"), "var"),
        P("var", "ff"),
        P("var", "ff"),
        P("ff", "var"),
        P(("groups", "ff"), None, "var"),
        P(("groups", "ff"), None, "var", None),
        P(("groups", "ff"), None, None),
        P(("groups", "ff"), None, "var"),
        P("groups", None),
        P("groups"),
    )
    return jax.shard_map(
        per_device,
        mesh=mesh,
        in_specs=placed,
        out_specs=P(("groups", "ff"), "var"),
        check_vma=False,
    )
```

```python
import functools

import jax
import jax.numpy as jnp
from jax import lax
from jax.experimental import pallas as pl
from jax.experimental.pallas import tpu as pltpu
from jax.sharding import PartitionSpec as P

MOST = 8
DIRECT = 8
MINE, NEXT, STEP, PLACE = range(4)
USUAL = 16
BF = jnp.bfloat16
F32 = jnp.float32
I32 = jnp.int32
MIB = 1024 * 1024


def dot(a, b):
    return jnp.dot(a, b, preferred_element_type=F32)


def dot_last(a, b):
    return lax.dot_general(a, b, (((1,), (1,)), ((), ())), preferred_element_type=F32)


def params(mib):
    return pltpu.CompilerParams(vmem_limit_bytes=int(mib * MIB))


def cost(flops, moved):
    return pl.CostEstimate(flops=flops, bytes_accessed=moved, transcendentals=0)


SCALARS = pl.BlockSpec(memory_space=pltpu.SMEM)
WHOLE = pl.BlockSpec(memory_space=pltpu.VMEM)
FAR = pl.BlockSpec(memory_space=pltpu.HBM)


def fixed(array):
    zeros = (0,) * array.ndim
    return pl.BlockSpec(array.shape, lambda *_: zeros)


def one_hot(count, cell):
    lines = lax.broadcasted_iota(I32, (count, cell.shape[1]), 0)
    return (lines == cell).astype(F32).astype(BF)


def dot_first(a, b):
    return lax.dot_general(a, b, (((0,), (0,)), ((), ())), preferred_element_type=F32)


class Ways:
    def __init__(self):
        self.shards = lax.axis_size("ff")
        self.fast = 2 if self.shards % 2 == 0 else 1
        self.slow = self.shards // self.fast
        self.direct = self.shards <= DIRECT
        me = lax.axis_index("ff").astype(I32)
        steps = jnp.arange(self.shards, dtype=I32)
        if self.direct:
            slow = (me // self.fast - steps % self.slow) % self.slow
            fast = (me % self.fast - steps // self.slow) % self.fast
            self.order = slow * self.fast + fast
        else:
            self.order = steps

    def arrival(self):
        steps = jnp.arange(self.shards, dtype=I32)
        if not self.direct:
            return steps
        return steps % self.slow * self.fast + steps // self.slow

    def back(self, a, c):
        S, F = self.slow, self.fast
        return [(s * F + f, (s - a) % S * F + (f - c) % F) for s in range(S) for f in range(F)]

    def gather(self, block, other):
        if not self.direct:
            return list(lax.all_gather(block, "ff")), other
        got = [block] + [
            lax.ppermute(block, "ff", self.back(-a, 0)) for a in range(1, self.slow)
        ]
        other, got[1] = tied(other, got[1])
        for c in range(1, self.fast):
            got += [lax.ppermute(part, "ff", self.back(0, -c)) for part in got[: self.slow]]
        return got, other

    def spread(self, blocks):
        return lax.all_to_all(blocks, "ff", 0, 0, tiled=True)

    def slow_steps(self, blocks):
        got = [blocks[0]] + [None] * (self.slow - 1)
        for a in range(1, self.slow):
            got[(-a) % self.slow] = lax.ppermute(blocks[a], "ff", self.back(a, 0))
        return got


def stage_kernel(*refs):
    count = len(refs) // 2
    sems = refs[2 * count]
    copies = [pltpu.make_async_copy(refs[n], refs[count + n], sems.at[n]) for n in range(count)]
    for copy in copies:
        copy.start()
    for copy in copies:
        copy.wait()


def stage(*arrays):
    return pl.pallas_call(
        stage_kernel,
        out_shape=tuple(jax.ShapeDtypeStruct(array.shape, array.dtype) for array in arrays),
        in_specs=[FAR] * len(arrays),
        out_specs=(WHOLE,) * len(arrays),
        scratch_shapes=[pltpu.SemaphoreType.DMA((len(arrays),))],
        compiler_params=params(52),
        cost_estimate=cost(0, sum(4 * array.size for array in arrays)),
    )(*arrays)


def low_in_kernel(count, shrink_ref, mask_ref, *refs):
    parts, x_ref, out_ref = refs[:count], refs[count], refs[count + 1]
    x = jnp.concatenate([part[...].astype(F32) for part in parts], axis=0).astype(BF)
    x_ref[...] = x

    @pl.when(pl.program_id(0) == 0)
    def _():
        out_ref[...] = jnp.zeros_like(out_ref)

    out_ref[...] += jnp.where(mask_ref[...] > 0, dot_last(x, shrink_ref[...]), 0.0)


def low_in_pairs(parts, shrink, mask):
    count = len(parts)
    own_rows, width = parts[0].shape
    rows, block = count * own_rows, min(1024, width)
    return pl.pallas_call(
        lambda *refs: low_in_kernel(count, *refs),
        out_shape=(
            jax.ShapeDtypeStruct((rows, width), BF),
            jax.ShapeDtypeStruct(mask.shape, F32),
        ),
        grid=(width // block,),
        in_specs=[pl.BlockSpec((shrink.shape[0], block), lambda n: (0, n)), fixed(mask)]
        + [pl.BlockSpec((own_rows, block), lambda n: (0, n))] * count,
        out_specs=(pl.BlockSpec((rows, block), lambda n: (0, n)), fixed(mask)),
        compiler_params=params(16),
        cost_estimate=cost(2 * rows * width * shrink.shape[0], 2 * shrink.size + 4 * rows * width),
    )(shrink, mask, *parts)


def expand_kernel(
    cap, fast, at_ref, own_ref, got_ref, marks_ref, cols_ref, near_ref, far_ref, *out_refs
):
    low = (own_ref[...] + got_ref[...]).astype(BF)
    picked = dot(one_hot(cap, marks_ref[MINE : MINE + 1]), low).astype(BF)
    lhs = jnp.concatenate([dot(picked, cols_ref[kind]) for kind in range(2)], axis=0).astype(BF)
    tall = lhs.shape[0]
    half = out_refs[0].shape[1]
    count = at_ref.shape[0]
    for b in range(count):
        here = pl.ds(pl.multiple_of(at_ref[b] * half, half), half)
        both = jnp.concatenate([near_ref[:, here], far_ref[:, here]], axis=0)
        at = b % (count // fast)
        out_refs[b * fast // count][pl.ds(at * tall, tall)] = dot(lhs, both).astype(BF)


def expand_rows(at, own, got, marks, cols, near, far, cap, fast):
    depth, width = near.shape
    shards = at.shape[0]
    half = width // (2 * shards)
    out = jax.ShapeDtypeStruct((2 * cap * shards // fast, half), BF)
    return pl.pallas_call(
        functools.partial(expand_kernel, cap, fast),
        out_shape=(out,) * fast,
        in_specs=[SCALARS] + [WHOLE] * 6,
        compiler_params=params(16),
        cost_estimate=cost(8 * cap * depth * width, 4 * (depth + cap) * width),
    )(at, own, got, marks, cols, near, far)


def base_kernel(side_ref, x_ref, gate_ref, up_ref, out_ref, held, sums, sems):
    half = held.shape[2]
    chunks = sems.shape[1]
    depth = held.shape[1] // chunks
    columns = pl.ds(pl.multiple_of(side_ref[0] * half, half), half)
    copies = []
    for c in range(chunks):
        here = pl.ds(c * depth, depth)
        for kind, weight in enumerate((gate_ref, up_ref)):
            copy = pltpu.make_async_copy(
                weight.at[here, columns], held.at[kind, here], sems.at[kind, c]
            )
            copy.start()
            copies.append((kind, here, copy))
    for kind, here, copy in copies:
        copy.wait()
        part = dot(x_ref[:, here], held[kind, here])
        sums[kind] = part if here.start == 0 else sums[kind] + part
    out_ref[...] = sums[...].astype(out_ref.dtype)


def base_half(side, x, gate_weight, up_weight, half, kind):
    rows, width = x.shape
    chunks = max(width // 512, 1)
    return pl.pallas_call(
        base_kernel,
        out_shape=jax.ShapeDtypeStruct((2, rows, half), kind),
        in_specs=[SCALARS, WHOLE, FAR, FAR],
        out_specs=WHOLE,
        scratch_shapes=[
            pltpu.VMEM((2, width, half), BF),
            pltpu.VMEM((2, rows, half), F32),
            pltpu.SemaphoreType.DMA((2, chunks)),
        ],
        compiler_params=params(48),
        cost_estimate=cost(4 * rows * width * half, 4 * width * half + 2 * rows * width),
    )(side, x, gate_weight, up_weight)


def hidden_kernel(cap, count, own_ref, got_ref, marks_ref, arrive_ref, *refs):
    parts, hid_ref, out_refs = refs[:count], refs[count], refs[count + 1 :]
    rows, half = hid_ref.shape
    cells = sum(part.shape[0] for part in parts)
    place = one_hot(cells, arrive_ref[0:1] * cap + arrive_ref[1:2])
    tall = out_refs[0].shape[0]
    leave = marks_ref[STEP : STEP + 1] * cap + marks_ref[PLACE : PLACE + 1]
    send = one_hot(tall * len(out_refs), leave)
    block = min(256, half)
    for first in range(0, half, block):
        here = pl.ds(first, block)
        delta = dot_first(place, jnp.concatenate([part[:, here] for part in parts], axis=0))
        gate = own_ref[0, :, here] + got_ref[0, :, here].astype(F32) + delta[:rows]
        up = own_ref[1, :, here] + got_ref[1, :, here].astype(F32) + delta[rows:]
        hidden = (gate / (1.0 + jnp.exp(-gate)) * up).astype(BF)
        hid_ref[:, here] = hidden
        sent = dot(send, hidden).astype(BF)
        for n, out_ref in enumerate(out_refs):
            out_ref[:, here] = sent[n * tall : (n + 1) * tall]


def hidden_half(own, got, parts, marks, arrive, cap, shards, count):
    rows, half = own.shape[1:]
    cells = shards * cap
    return pl.pallas_call(
        functools.partial(hidden_kernel, cap, len(parts)),
        out_shape=(jax.ShapeDtypeStruct((rows, half), BF),)
        + (jax.ShapeDtypeStruct((cells // count, half), BF),) * count,
        compiler_params=params(40),
        cost_estimate=cost(10 * half * cells * rows, 2 * half * (6 * rows + 3 * cells)),
    )(own, got, marks, arrive, *parts)


def relay_kernel(own_ref, got_ref, *out_refs):
    cap = out_refs[0].shape[0] // 2
    for a, out_ref in enumerate(out_refs):
        here = pl.ds(a * cap, cap)
        out_ref[:cap] = own_ref[here]
        out_ref[cap:] = got_ref[here]


def relay(own, got, count):
    tall, half = own.shape
    return pl.pallas_call(
        relay_kernel,
        out_shape=(jax.ShapeDtypeStruct((2 * tall // count, half), BF),) * count,
        compiler_params=params(16),
        cost_estimate=cost(0, 8 * tall * half),
    )(own, got)


def down_kernel(start, core_ref, near_ref, far_ref, weight_ref, *refs):
    out_refs, held, sems = refs[:-2], refs[-2], refs[-1]
    chunks = sems.shape[1]
    half, width = held.shape[1:]
    block = width // chunks
    tall = out_refs[0].shape[0]
    copies = []
    for c in range(chunks):
        here = pl.ds(c * block, block)
        for side, at in enumerate((core_ref[0], 1 - core_ref[0])):
            lines = pl.ds(pl.multiple_of(at * half, half), half)
            copy = pltpu.make_async_copy(
                weight_ref.at[lines, pl.ds(start + c * block, block)],
                held.at[side, :, here],
                sems.at[side, c],
            )
            copy.start()
            copies.append(copy)
    for c in range(chunks):
        here = pl.ds(c * block, block)
        copies[2 * c].wait()
        copies[2 * c + 1].wait()
        total = dot(near_ref[...], held[0, :, here]) + dot(far_ref[...], held[1, :, here])
        for n, out_ref in enumerate(out_refs):
            out_ref[:, here] = total[n * tall : (n + 1) * tall].astype(out_ref.dtype)


def down_base(core, near, far, weight, start, width, kinds):
    rows, half = near.shape
    chunks = max(width // 512, 1)
    outs = tuple(jax.ShapeDtypeStruct((rows // len(kinds), width), kind) for kind in kinds)
    return pl.pallas_call(
        functools.partial(down_kernel, start),
        out_shape=outs,
        in_specs=[SCALARS, WHOLE, WHOLE, FAR],
        out_specs=(WHOLE,) * len(outs),
        scratch_shapes=[
            pltpu.VMEM((2, half, width), BF),
            pltpu.SemaphoreType.DMA((2, chunks)),
        ],
        compiler_params=params(48),
        cost_estimate=cost(4 * rows * half * width, 4 * half * width + 4 * rows * width),
    )(core, near, far, weight)


def low_out_kernel(cap, count, at_ref, marks_ref, slot_ref, shrink_ref, *refs):
    parts, out_ref = refs[:count], refs[count]
    half = parts[0].shape[1]
    blocks = [part[r : r + cap] for r in range(0, parts[0].shape[0], cap) for part in parts]
    pairs = jnp.zeros(out_ref.shape, F32)
    for b, block in enumerate(blocks):
        columns = pl.ds(pl.multiple_of(at_ref[b] * half, half), half)
        pairs += dot_last(block, shrink_ref[:, columns])
    mask = dot(one_hot(cap, marks_ref[MINE : MINE + 1]), slot_ref[...])
    out_ref[...] = jnp.where(mask > 0.5, pairs, 0.0)


def low_out_pairs(at, marks, slot_mask, shrink, parts, cap):
    count = len(parts)
    half = parts[0].shape[1]
    depth = shrink.shape[0]
    return pl.pallas_call(
        functools.partial(low_out_kernel, cap, count),
        out_shape=jax.ShapeDtypeStruct((cap, depth), F32),
        in_specs=[SCALARS] + [WHOLE] * (3 + count),
        compiler_params=params(16),
        cost_estimate=cost(
            2 * cap * depth * at.shape[0] * half, 2 * at.shape[0] * half * (depth + cap)
        ),
    )(at, marks, slot_mask, shrink, *parts)


def add_kernel(owners, sides, *refs):
    base_refs, refs = refs[: owners * sides], refs[owners * sides :]
    low_refs, refs = refs[: 2 * owners], refs[2 * owners :]
    marks_ref, expand_refs, out_refs = refs[0], refs[1 : owners + 1], refs[owners + 1 :]
    rows = base_refs[0].shape[0]
    spreads = []
    for n in range(owners):
        low = (low_refs[2 * n][...] + low_refs[2 * n + 1][...]).astype(BF)
        pick = one_hot(low.shape[0], marks_ref[MINE + n : MINE + n + 1, :rows])
        spreads.append(dot_first(pick, low).astype(BF))
    spread = jnp.concatenate(spreads, axis=1)
    own_rows, width = out_refs[0].shape
    side = width // sides
    block = min(1024, side)
    for first in range(0, width, block):
        here = pl.ds(first, block)
        inside = pl.ds(first % side, block)
        expand = jnp.concatenate([ref[:, here] for ref in expand_refs], axis=0)
        total = dot(spread, expand)
        for base_ref in base_refs[first // side :: sides]:
            total += base_ref[:, inside].astype(F32)
        for b, out_ref in enumerate(out_refs):
            out_ref[:, here] = total[b * own_rows : (b + 1) * own_rows].astype(BF)


def add_delta(bases, lows, marks, expands, count):
    owners = len(expands)
    rows = bases[0].shape[0]
    depth, width = expands[0].shape
    return pl.pallas_call(
        functools.partial(add_kernel, owners, len(bases) // owners),
        out_shape=(jax.ShapeDtypeStruct((rows // count, width), BF),) * count,
        compiler_params=params(32),
        cost_estimate=cost(
            2 * rows * depth * owners * width, width * (6 * rows + 2 * depth) * owners
        ),
    )(*bases, *lows, marks, *expands)


def tied(first, *others):
    return lax.optimization_barrier((first, *others))


def per_device(
    tokens,
    gate_weight,
    up_weight,
    down_weight,
    shrink_gu,
    expand_gu,
    shrink_down,
    expand_down,
    variant_ids,
    variant_slot,
):
    ways = Ways()
    shards, order = ways.shards, ways.order
    me = lax.axis_index("ff").astype(I32)
    core = lax.axis_index("var").astype(I32)
    groups = lax.axis_size("groups")
    own_rows, width = tokens.shape
    rows = own_rows * shards
    slots = shrink_gu.shape[0]
    variants = variant_slot.shape[0]
    rank = shrink_down.shape[1]
    half_rank = expand_gu.shape[2]
    half = gate_weight.shape[1] // 2
    most = min(slots * MOST, rows)
    here = core.reshape(1)
    there = 1 - here
    at_here = 2 * order + core
    split = ways.fast if ways.direct else 1
    swap = lambda a: lax.ppermute(a, "var", [(0, 1), (1, 0)])

    near = expand_gu.reshape(slots * 2 * half_rank, -1)
    token_parts, far = ways.gather(tokens, swap(near))
    shrink_in = shrink_gu.reshape(slots * 2 * rank, width)
    if ways.direct:
        first_hop = ways.slow + 1
        variant_ids, variant_slot, near, shrink_in, token_parts[first_hop] = tied(
            variant_ids, variant_slot, near, shrink_in, token_parts[first_hop]
        )
    all_ids, all_slots = [variant_ids[:, 0]], [variant_slot]
    for turn in range(1, 1 if ways.direct else groups):
        pairs = [(g, (g + turn) % groups) for g in range(groups)]
        all_ids.append(lax.ppermute(all_ids[0], "groups", pairs))
        all_slots.append(lax.ppermute(all_slots[0], "groups", pairs))
    all_ids, all_slots = jnp.stack(all_ids), jnp.stack(all_slots)
    token_parts[0], near, shrink_in = stage(token_parts[0], near, shrink_in)

    matches = all_ids[:, :, None] == jnp.arange(variants, dtype=I32)
    slot_row = jnp.sum(jnp.where(matches, all_slots[:, None, :], 0), axis=2)
    owner = slot_row // slots
    index = jnp.arange(rows, dtype=I32)
    earlier = (owner[:, :, None] == owner[:, None, :]) & (index[None, :] < index[:, None])
    place = jnp.sum(earlier.astype(I32), axis=2)
    highest = jnp.max(place).reshape(1)
    slot_row, place = slot_row[0], place[0]
    where_row = order[:, None] == jnp.arange(shards, dtype=I32)[None, :]
    turned = lambda a: jnp.sum(
        jnp.where(where_row[:, :, None], a.reshape(1, shards, own_rows), 0), axis=1
    ).reshape(rows)
    slot_row, place = turned(slot_row), turned(place)
    owner = slot_row // slots
    of_block = owner[:, None] == order[None, :]
    step = jnp.sum(jnp.where(of_block, jnp.arange(shards, dtype=I32)[None, :], 0), axis=1)
    arrival = jnp.sum(jnp.where(of_block, ways.arrival()[None, :], 0), axis=1)
    local = slot_row - me * slots
    next_owner = order[ways.slow % shards]
    marks = jnp.stack(
        [jnp.where(owner == me, place, -1), jnp.where(owner == next_owner, place, -1), step, place]
    )
    arrive = jnp.stack(
        [jnp.concatenate([2 * arrival, 2 * arrival + 1]), jnp.concatenate([place, place])]
    )
    kinds = jnp.arange(2, dtype=I32)
    in_cols = jnp.arange(slots * 2 * rank, dtype=I32)
    mask_in = (local[:, None] == (in_cols // (2 * rank))[None, :]).astype(F32)
    out_cols = jnp.arange(slots * rank, dtype=I32)
    slot_mask = (local[:, None] == (out_cols // rank)[None, :]).astype(BF)
    rank_at = in_cols % rank
    kind_at = in_cols // rank % 2
    row_at = in_cols // (2 * rank) * (2 * half_rank) + kind_at * half_rank + rank_at % half_rank
    depth = slots * 2 * half_rank
    both_cols = jnp.arange(2 * depth, dtype=I32)
    wanted = row_at + jnp.where(rank_at // half_rank == core, 0, depth)
    hit = wanted[:, None] == both_cols[None, :]
    cols = (hit[None] & (kind_at[None, :] == kinds[:, None])[:, :, None]).astype(BF)

    x, low_own = low_in_pairs(token_parts, shrink_in, mask_in)
    low_got = swap(low_own)

    def partial_sums(cap):
        made = expand_rows(at_here, low_own, low_got, marks, cols, near, far, cap, split)
        held, *made = tied(x, *made)
        expand = expand_down.reshape(slots * rank, width)
        if split == 2:
            beside = lax.ppermute(made[1], "ff", ways.back(0, 1))
            base_there = base_half(there, held, gate_weight, up_weight, half, BF)
            base_there, beside, expand = tied(base_there, beside, expand)
            made = relay(made[0], beside, ways.slow)
            held, *made = tied(held, *made)
            delta = ways.slow_steps(made)
            expand_beside = lax.ppermute(expand, "ff", ways.back(0, 1))
        else:
            base_there = base_half(there, held, gate_weight, up_weight, half, BF)
            delta = ways.spread(made[0].reshape(shards, 2 * cap, half))
            delta = [delta.reshape(2 * shards * cap, half)]
        base_got = swap(base_there)
        base_own = base_half(here, held, gate_weight, up_weight, half, F32)
        if split == 2:
            base_own, expand_beside = tied(base_own, expand_beside)
        hidden, *sent = hidden_half(
            base_own, base_got, delta, marks, arrive, cap, shards, split
        )
        hidden_far = swap(hidden)
        shrink = shrink_down.reshape(slots * rank, -1)
        down = functools.partial(down_base, here, hidden, hidden_far, down_weight, 0, width)
        if split == 2:
            beside = lax.ppermute(sent[1], "ff", ways.back(0, 1))
            base, base_sent = down((F32, BF))
            base_sent, beside = tied(base_sent, beside)
            base_beside = lax.ppermute(base_sent, "ff", ways.back(0, 1))
            got = ways.slow_steps(relay(sent[0], beside, ways.slow))
            base_beside, *got = tied(base_beside, *got)
            bases = [base, base_beside]
        else:
            bases = list(down((F32,)))
            got = [ways.spread(sent[0].reshape(shards, cap, half)).reshape(shards * cap, half)]
        bases[0], *got = tied(bases[0], *got)
        out_own = low_out_pairs(at_here, marks, slot_mask, shrink, got, cap)
        out_got = swap(out_own)
        if split == 1:
            parts = add_delta(bases, [out_own, out_got], marks, [expand], shards)
            return list(ways.spread(jnp.stack(parts)))
        out_beside = lax.ppermute(out_own, "ff", ways.back(0, 1))
        across = [
            (2 * f + v, 2 * g + 1 - v) for f, g in ways.back(0, 1) for v in range(2)
        ]
        out_across = lax.ppermute(out_own, ("ff", "var"), across)
        parts = add_delta(
            bases,
            [out_own, out_got, out_beside, out_across],
            marks,
            [expand, expand_beside],
            ways.slow,
        )
        return ways.slow_steps(parts)

    if most <= USUAL:
        parts = partial_sums(most)
    else:
        parts = lax.cond(
            highest[0] < USUAL, lambda: partial_sums(USUAL), lambda: partial_sums(most)
        )
    return sum(part.astype(F32) for part in parts).astype(BF)


def solution(mesh):
    placed = (
        P(("groups", "ff"), "var"),
        P("var", "ff"),
        P("var", "ff"),
        P("ff", "var"),
        P(("groups", "ff"), None, "var"),
        P(("groups", "ff"), None, "var", None),
        P(("groups", "ff"), None, None),
        P(("groups", "ff"), None, "var"),
        P("groups", None),
        P("groups"),
    )
    return jax.shard_map(
        per_device,
        mesh=mesh,
        in_specs=placed,
        out_specs=P(("groups", "ff"), "var"),
        check_vma=False,
    )
```

```python
import functools

import jax
import jax.numpy as jnp
from jax import lax
from jax.experimental import pallas as pl
from jax.experimental.pallas import tpu as pltpu
from jax.sharding import PartitionSpec as P

MOST = 8
DIRECT = 8
MINE, NEXT, STEP, PLACE = range(4)
USUAL = 16
BF = jnp.bfloat16
F32 = jnp.float32
I32 = jnp.int32
MIB = 1024 * 1024


def dot(a, b):
    return jnp.dot(a, b, preferred_element_type=F32)


def dot_last(a, b):
    return lax.dot_general(a, b, (((1,), (1,)), ((), ())), preferred_element_type=F32)


def params(mib):
    return pltpu.CompilerParams(vmem_limit_bytes=int(mib * MIB))


def cost(flops, moved):
    return pl.CostEstimate(flops=flops, bytes_accessed=moved, transcendentals=0)


SCALARS = pl.BlockSpec(memory_space=pltpu.SMEM)
WHOLE = pl.BlockSpec(memory_space=pltpu.VMEM)
FAR = pl.BlockSpec(memory_space=pltpu.HBM)


def fixed(array):
    zeros = (0,) * array.ndim
    return pl.BlockSpec(array.shape, lambda *_: zeros)


def one_hot(count, cell):
    lines = lax.broadcasted_iota(I32, (count, cell.shape[1]), 0)
    return (lines == cell).astype(F32).astype(BF)


def dot_first(a, b):
    return lax.dot_general(a, b, (((0,), (0,)), ((), ())), preferred_element_type=F32)


class Ways:
    def __init__(self):
        self.shards = lax.axis_size("ff")
        self.fast = 2 if self.shards % 2 == 0 else 1
        self.slow = self.shards // self.fast
        self.direct = self.shards <= DIRECT
        me = lax.axis_index("ff").astype(I32)
        steps = jnp.arange(self.shards, dtype=I32)
        if self.direct:
            slow = (me // self.fast - steps % self.slow) % self.slow
            fast = (me % self.fast - steps // self.slow) % self.fast
            self.order = slow * self.fast + fast
        else:
            self.order = steps

    def arrival(self):
        steps = jnp.arange(self.shards, dtype=I32)
        if not self.direct:
            return steps
        return steps % self.slow * self.fast + steps // self.slow

    def back(self, a, c):
        S, F = self.slow, self.fast
        return [(s * F + f, (s - a) % S * F + (f - c) % F) for s in range(S) for f in range(F)]

    def gather(self, block, other):
        if not self.direct:
            return list(lax.all_gather(block, "ff")), other
        got = [block] + [
            lax.ppermute(block, "ff", self.back(-a, 0)) for a in range(1, self.slow)
        ]
        other, got[1] = tied(other, got[1])
        for c in range(1, self.fast):
            got += [lax.ppermute(part, "ff", self.back(0, -c)) for part in got[: self.slow]]
        return got, other

    def spread(self, blocks):
        return lax.all_to_all(blocks, "ff", 0, 0, tiled=True)

    def slow_steps(self, blocks):
        got = [blocks[0]] + [None] * (self.slow - 1)
        for a in range(1, self.slow):
            got[(-a) % self.slow] = lax.ppermute(blocks[a], "ff", self.back(a, 0))
        return got


def stage_kernel(*refs):
    count = len(refs) // 2
    sems = refs[2 * count]
    copies = [pltpu.make_async_copy(refs[n], refs[count + n], sems.at[n]) for n in range(count)]
    for copy in copies:
        copy.start()
    for copy in copies:
        copy.wait()


def stage(*arrays):
    return pl.pallas_call(
        stage_kernel,
        out_shape=tuple(jax.ShapeDtypeStruct(array.shape, array.dtype) for array in arrays),
        in_specs=[FAR] * len(arrays),
        out_specs=(WHOLE,) * len(arrays),
        scratch_shapes=[pltpu.SemaphoreType.DMA((len(arrays),))],
        compiler_params=params(52),
        cost_estimate=cost(0, sum(4 * array.size for array in arrays)),
    )(*arrays)


def low_in_kernel(count, shrink_ref, mask_ref, *refs):
    parts, x_ref, out_ref = refs[:count], refs[count], refs[count + 1]
    x = jnp.concatenate([part[...].astype(F32) for part in parts], axis=0).astype(BF)
    x_ref[...] = x

    @pl.when(pl.program_id(0) == 0)
    def _():
        out_ref[...] = jnp.zeros_like(out_ref)

    out_ref[...] += jnp.where(mask_ref[...] > 0, dot_last(x, shrink_ref[...]), 0.0)


def low_in_pairs(parts, shrink, mask):
    count = len(parts)
    own_rows, width = parts[0].shape
    rows, block = count * own_rows, min(1024, width)
    return pl.pallas_call(
        lambda *refs: low_in_kernel(count, *refs),
        out_shape=(
            jax.ShapeDtypeStruct((rows, width), BF),
            jax.ShapeDtypeStruct(mask.shape, F32),
        ),
        grid=(width // block,),
        in_specs=[pl.BlockSpec((shrink.shape[0], block), lambda n: (0, n)), fixed(mask)]
        + [pl.BlockSpec((own_rows, block), lambda n: (0, n))] * count,
        out_specs=(pl.BlockSpec((rows, block), lambda n: (0, n)), fixed(mask)),
        compiler_params=params(16),
        cost_estimate=cost(2 * rows * width * shrink.shape[0], 2 * shrink.size + 4 * rows * width),
    )(shrink, mask, *parts)


def expand_kernel(
    cap,
    fast,
    at_ref,
    own_ref,
    got_ref,
    marks_ref,
    cols_ref,
    far_ref,
    near_ref,
    *refs,
):
    out_refs, held, sems = refs[:-2], refs[-2], refs[-1]
    half = out_refs[0].shape[1]
    count = at_ref.shape[0]
    columns = [pl.ds(pl.multiple_of(at_ref[b] * half, half), half) for b in range(count)]
    copies = []
    for b in range(count):
        put = held.at[:, pl.ds(b * half, half)]
        copies.append(pltpu.make_async_copy(near_ref.at[:, columns[b]], put, sems.at[b]))
        copies[b].start()
    low = (own_ref[...] + got_ref[...]).astype(BF)
    picked = dot(one_hot(cap, marks_ref[MINE : MINE + 1]), low).astype(BF)
    lhs = jnp.concatenate([dot(picked, cols_ref[kind]) for kind in range(2)], axis=0).astype(BF)
    tall = lhs.shape[0]
    for b in range(count):
        copies[b].wait()
        both = jnp.concatenate([held[:, pl.ds(b * half, half)], far_ref[:, columns[b]]], axis=0)
        at = b % (count // fast)
        out_refs[b * fast // count][pl.ds(at * tall, tall)] = dot(lhs, both).astype(BF)


def expand_rows(at, own, got, marks, cols, near, far, cap, fast):
    depth, width = near.shape
    shards = at.shape[0]
    half = width // (2 * shards)
    out = jax.ShapeDtypeStruct((2 * cap * shards // fast, half), BF)
    return pl.pallas_call(
        functools.partial(expand_kernel, cap, fast),
        out_shape=(out,) * fast,
        in_specs=[SCALARS] + [WHOLE] * 5 + [FAR],
        scratch_shapes=[
            pltpu.VMEM((depth, width // 2), BF),
            pltpu.SemaphoreType.DMA((shards,)),
        ],
        compiler_params=params(52),
        cost_estimate=cost(8 * cap * depth * width, 4 * (depth + cap) * width),
    )(at, own, got, marks, cols, far, near)


def base_kernel(side_ref, x_ref, gate_ref, up_ref, out_ref, held, sums, sems):
    half = held.shape[2]
    chunks = sems.shape[1]
    depth = held.shape[1] // chunks
    columns = pl.ds(pl.multiple_of(side_ref[0] * half, half), half)
    copies = []
    for c in range(chunks):
        here = pl.ds(c * depth, depth)
        for kind, weight in enumerate((gate_ref, up_ref)):
            copy = pltpu.make_async_copy(
                weight.at[here, columns], held.at[kind, here], sems.at[kind, c]
            )
            copy.start()
            copies.append((kind, here, copy))
    for kind, here, copy in copies:
        copy.wait()
        part = dot(x_ref[:, here], held[kind, here])
        sums[kind] = part if here.start == 0 else sums[kind] + part
    out_ref[...] = sums[...].astype(out_ref.dtype)


def base_half(side, x, gate_weight, up_weight, half, kind):
    rows, width = x.shape
    chunks = max(width // 512, 1)
    return pl.pallas_call(
        base_kernel,
        out_shape=jax.ShapeDtypeStruct((2, rows, half), kind),
        in_specs=[SCALARS, WHOLE, FAR, FAR],
        out_specs=WHOLE,
        scratch_shapes=[
            pltpu.VMEM((2, width, half), BF),
            pltpu.VMEM((2, rows, half), F32),
            pltpu.SemaphoreType.DMA((2, chunks)),
        ],
        compiler_params=params(48),
        cost_estimate=cost(4 * rows * width * half, 4 * width * half + 2 * rows * width),
    )(side, x, gate_weight, up_weight)


def hidden_kernel(cap, count, own_ref, got_ref, marks_ref, arrive_ref, *refs):
    parts, hid_ref, out_refs = refs[:count], refs[count], refs[count + 1 :]
    rows, half = hid_ref.shape
    cells = sum(part.shape[0] for part in parts)
    place = one_hot(cells, arrive_ref[0:1] * cap + arrive_ref[1:2])
    tall = out_refs[0].shape[0]
    leave = marks_ref[STEP : STEP + 1] * cap + marks_ref[PLACE : PLACE + 1]
    send = one_hot(tall * len(out_refs), leave)
    block = min(256, half)
    for first in range(0, half, block):
        here = pl.ds(first, block)
        delta = dot_first(place, jnp.concatenate([part[:, here] for part in parts], axis=0))
        gate = own_ref[0, :, here] + got_ref[0, :, here].astype(F32) + delta[:rows]
        up = own_ref[1, :, here] + got_ref[1, :, here].astype(F32) + delta[rows:]
        hidden = (gate / (1.0 + jnp.exp(-gate)) * up).astype(BF)
        hid_ref[:, here] = hidden
        sent = dot(send, hidden).astype(BF)
        for n, out_ref in enumerate(out_refs):
            out_ref[:, here] = sent[n * tall : (n + 1) * tall]


def hidden_half(own, got, parts, marks, arrive, cap, shards, count):
    rows, half = own.shape[1:]
    cells = shards * cap
    return pl.pallas_call(
        functools.partial(hidden_kernel, cap, len(parts)),
        out_shape=(jax.ShapeDtypeStruct((rows, half), BF),)
        + (jax.ShapeDtypeStruct((cells // count, half), BF),) * count,
        compiler_params=params(40),
        cost_estimate=cost(10 * half * cells * rows, 2 * half * (6 * rows + 3 * cells)),
    )(own, got, marks, arrive, *parts)


def relay_kernel(own_ref, got_ref, *out_refs):
    cap = out_refs[0].shape[0] // 2
    for a, out_ref in enumerate(out_refs):
        here = pl.ds(a * cap, cap)
        out_ref[:cap] = own_ref[here]
        out_ref[cap:] = got_ref[here]


def relay(own, got, count):
    tall, half = own.shape
    return pl.pallas_call(
        relay_kernel,
        out_shape=(jax.ShapeDtypeStruct((2 * tall // count, half), BF),) * count,
        compiler_params=params(16),
        cost_estimate=cost(0, 8 * tall * half),
    )(own, got)


def down_kernel(start, core_ref, near_ref, far_ref, weight_ref, *refs):
    out_refs, held, sems = refs[:-2], refs[-2], refs[-1]
    chunks = sems.shape[1]
    half, width = held.shape[1:]
    block = width // chunks
    tall = out_refs[0].shape[0]
    copies = []
    for c in range(chunks):
        here = pl.ds(c * block, block)
        for side, at in enumerate((core_ref[0], 1 - core_ref[0])):
            lines = pl.ds(pl.multiple_of(at * half, half), half)
            copy = pltpu.make_async_copy(
                weight_ref.at[lines, pl.ds(start + c * block, block)],
                held.at[side, :, here],
                sems.at[side, c],
            )
            copy.start()
            copies.append(copy)
    for c in range(chunks):
        here = pl.ds(c * block, block)
        copies[2 * c].wait()
        copies[2 * c + 1].wait()
        total = dot(near_ref[...], held[0, :, here]) + dot(far_ref[...], held[1, :, here])
        for n, out_ref in enumerate(out_refs):
            out_ref[:, here] = total[n * tall : (n + 1) * tall].astype(out_ref.dtype)


def down_base(core, near, far, weight, start, width, kinds):
    rows, half = near.shape
    chunks = max(width // 512, 1)
    outs = tuple(jax.ShapeDtypeStruct((rows // len(kinds), width), kind) for kind in kinds)
    return pl.pallas_call(
        functools.partial(down_kernel, start),
        out_shape=outs,
        in_specs=[SCALARS, WHOLE, WHOLE, FAR],
        out_specs=(WHOLE,) * len(outs),
        scratch_shapes=[
            pltpu.VMEM((2, half, width), BF),
            pltpu.SemaphoreType.DMA((2, chunks)),
        ],
        compiler_params=params(48),
        cost_estimate=cost(4 * rows * half * width, 4 * half * width + 4 * rows * width),
    )(core, near, far, weight)


def low_out_kernel(cap, count, at_ref, marks_ref, slot_ref, shrink_ref, *refs):
    parts, out_ref = refs[:count], refs[count]
    half = parts[0].shape[1]
    blocks = [part[r : r + cap] for r in range(0, parts[0].shape[0], cap) for part in parts]
    pairs = jnp.zeros(out_ref.shape, F32)
    for b, block in enumerate(blocks):
        columns = pl.ds(pl.multiple_of(at_ref[b] * half, half), half)
        pairs += dot_last(block, shrink_ref[:, columns])
    mask = dot(one_hot(cap, marks_ref[MINE : MINE + 1]), slot_ref[...])
    out_ref[...] = jnp.where(mask > 0.5, pairs, 0.0)


def low_out_pairs(at, marks, slot_mask, shrink, parts, cap):
    count = len(parts)
    half = parts[0].shape[1]
    depth = shrink.shape[0]
    return pl.pallas_call(
        functools.partial(low_out_kernel, cap, count),
        out_shape=jax.ShapeDtypeStruct((cap, depth), F32),
        in_specs=[SCALARS] + [WHOLE] * (3 + count),
        compiler_params=params(16),
        cost_estimate=cost(
            2 * cap * depth * at.shape[0] * half, 2 * at.shape[0] * half * (depth + cap)
        ),
    )(at, marks, slot_mask, shrink, *parts)


def add_kernel(owners, sides, *refs):
    base_refs, refs = refs[: owners * sides], refs[owners * sides :]
    low_refs, refs = refs[: 2 * owners], refs[2 * owners :]
    marks_ref, expand_refs, out_refs = refs[0], refs[1 : owners + 1], refs[owners + 1 :]
    rows = base_refs[0].shape[0]
    spreads = []
    for n in range(owners):
        low = (low_refs[2 * n][...] + low_refs[2 * n + 1][...]).astype(BF)
        pick = one_hot(low.shape[0], marks_ref[MINE + n : MINE + n + 1, :rows])
        spreads.append(dot_first(pick, low).astype(BF))
    spread = jnp.concatenate(spreads, axis=1)
    own_rows, width = out_refs[0].shape
    side = width // sides
    block = min(1024, side)
    for first in range(0, width, block):
        here = pl.ds(first, block)
        inside = pl.ds(first % side, block)
        expand = jnp.concatenate([ref[:, here] for ref in expand_refs], axis=0)
        total = dot(spread, expand)
        for base_ref in base_refs[first // side :: sides]:
            total += base_ref[:, inside].astype(F32)
        for b, out_ref in enumerate(out_refs):
            out_ref[:, here] = total[b * own_rows : (b + 1) * own_rows].astype(BF)


def add_delta(bases, lows, marks, expands, count):
    owners = len(expands)
    rows = bases[0].shape[0]
    depth, width = expands[0].shape
    return pl.pallas_call(
        functools.partial(add_kernel, owners, len(bases) // owners),
        out_shape=(jax.ShapeDtypeStruct((rows // count, width), BF),) * count,
        compiler_params=params(32),
        cost_estimate=cost(
            2 * rows * depth * owners * width, width * (6 * rows + 2 * depth) * owners
        ),
    )(*bases, *lows, marks, *expands)


def tied(first, *others):
    return lax.optimization_barrier((first, *others))


def per_device(
    tokens,
    gate_weight,
    up_weight,
    down_weight,
    shrink_gu,
    expand_gu,
    shrink_down,
    expand_down,
    variant_ids,
    variant_slot,
):
    ways = Ways()
    shards, order = ways.shards, ways.order
    me = lax.axis_index("ff").astype(I32)
    core = lax.axis_index("var").astype(I32)
    groups = lax.axis_size("groups")
    own_rows, width = tokens.shape
    rows = own_rows * shards
    slots = shrink_gu.shape[0]
    variants = variant_slot.shape[0]
    rank = shrink_down.shape[1]
    half_rank = expand_gu.shape[2]
    half = gate_weight.shape[1] // 2
    most = min(slots * MOST, rows)
    here = core.reshape(1)
    there = 1 - here
    at_here = 2 * order + core
    split = ways.fast if ways.direct else 1
    swap = lambda a: lax.ppermute(a, "var", [(0, 1), (1, 0)])

    near = expand_gu.reshape(slots * 2 * half_rank, -1)
    token_parts, far = ways.gather(tokens, swap(near))
    shrink_in = shrink_gu.reshape(slots * 2 * rank, width)
    if ways.direct:
        first_hop = ways.slow + 1
        variant_ids, variant_slot, shrink_in, token_parts[first_hop] = tied(
            variant_ids, variant_slot, shrink_in, token_parts[first_hop]
        )
    all_ids, all_slots = [variant_ids[:, 0]], [variant_slot]
    for turn in range(1, 1 if ways.direct else groups):
        pairs = [(g, (g + turn) % groups) for g in range(groups)]
        all_ids.append(lax.ppermute(all_ids[0], "groups", pairs))
        all_slots.append(lax.ppermute(all_slots[0], "groups", pairs))
    all_ids, all_slots = jnp.stack(all_ids), jnp.stack(all_slots)
    token_parts[0], shrink_in = stage(token_parts[0], shrink_in)

    matches = all_ids[:, :, None] == jnp.arange(variants, dtype=I32)
    slot_row = jnp.sum(jnp.where(matches, all_slots[:, None, :], 0), axis=2)
    owner = slot_row // slots
    index = jnp.arange(rows, dtype=I32)
    earlier = (owner[:, :, None] == owner[:, None, :]) & (index[None, :] < index[:, None])
    place = jnp.sum(earlier.astype(I32), axis=2)
    highest = jnp.max(place).reshape(1)
    slot_row, place = slot_row[0], place[0]
    where_row = order[:, None] == jnp.arange(shards, dtype=I32)[None, :]
    turned = lambda a: jnp.sum(
        jnp.where(where_row[:, :, None], a.reshape(1, shards, own_rows), 0), axis=1
    ).reshape(rows)
    slot_row, place = turned(slot_row), turned(place)
    owner = slot_row // slots
    of_block = owner[:, None] == order[None, :]
    step = jnp.sum(jnp.where(of_block, jnp.arange(shards, dtype=I32)[None, :], 0), axis=1)
    arrival = jnp.sum(jnp.where(of_block, ways.arrival()[None, :], 0), axis=1)
    local = slot_row - me * slots
    next_owner = order[ways.slow % shards]
    marks = jnp.stack(
        [jnp.where(owner == me, place, -1), jnp.where(owner == next_owner, place, -1), step, place]
    )
    arrive = jnp.stack(
        [jnp.concatenate([2 * arrival, 2 * arrival + 1]), jnp.concatenate([place, place])]
    )
    kinds = jnp.arange(2, dtype=I32)
    in_cols = jnp.arange(slots * 2 * rank, dtype=I32)
    mask_in = (local[:, None] == (in_cols // (2 * rank))[None, :]).astype(F32)
    out_cols = jnp.arange(slots * rank, dtype=I32)
    slot_mask = (local[:, None] == (out_cols // rank)[None, :]).astype(BF)
    rank_at = in_cols % rank
    kind_at = in_cols // rank % 2
    row_at = in_cols // (2 * rank) * (2 * half_rank) + kind_at * half_rank + rank_at % half_rank
    depth = slots * 2 * half_rank
    both_cols = jnp.arange(2 * depth, dtype=I32)
    wanted = row_at + jnp.where(rank_at // half_rank == core, 0, depth)
    hit = wanted[:, None] == both_cols[None, :]
    cols = (hit[None] & (kind_at[None, :] == kinds[:, None])[:, :, None]).astype(BF)

    x, low_own = low_in_pairs(token_parts, shrink_in, mask_in)
    low_got = swap(low_own)

    def partial_sums(cap):
        made = expand_rows(at_here, low_own, low_got, marks, cols, near, far, cap, split)
        held, *made = tied(x, *made)
        expand = expand_down.reshape(slots * rank, width)
        if split == 2:
            beside = lax.ppermute(made[1], "ff", ways.back(0, 1))
            base_there = base_half(there, held, gate_weight, up_weight, half, BF)
            base_there, beside, expand = tied(base_there, beside, expand)
            made = relay(made[0], beside, ways.slow)
            held, *made = tied(held, *made)
            delta = ways.slow_steps(made)
            expand_beside = lax.ppermute(expand, "ff", ways.back(0, 1))
        else:
            base_there = base_half(there, held, gate_weight, up_weight, half, BF)
            delta = ways.spread(made[0].reshape(shards, 2 * cap, half))
            delta = [delta.reshape(2 * shards * cap, half)]
        base_got = swap(base_there)
        base_own = base_half(here, held, gate_weight, up_weight, half, F32)
        if split == 2:
            base_own, expand_beside = tied(base_own, expand_beside)
        hidden, *sent = hidden_half(
            base_own, base_got, delta, marks, arrive, cap, shards, split
        )
        hidden_far = swap(hidden)
        shrink = shrink_down.reshape(slots * rank, -1)
        side = width // 2
        down = functools.partial(down_base, here, hidden, hidden_far, down_weight)
        if split == 2:
            beside = lax.ppermute(sent[1], "ff", ways.back(0, 1))
            left, left_sent = down(0, side, (F32, BF))
            left_sent, beside = tied(left_sent, beside)
            left_beside = lax.ppermute(left_sent, "ff", ways.back(0, 1))
            sent = relay(sent[0], beside, ways.slow)
            hidden, *sent = tied(hidden, *sent)
            down = functools.partial(down_base, here, hidden, hidden_far, down_weight)
            got = ways.slow_steps(sent)
            right, right_sent = down(side, side, (F32, BF))
            right_sent, left_beside, *got = tied(right_sent, left_beside, *got)
            right_beside = lax.ppermute(right_sent, "ff", ways.back(0, 1))
            bases = [left, right, left_beside, right_beside]
        else:
            bases = [down(0, side, (F32,))[0], down(side, side, (F32,))[0]]
            got = [ways.spread(sent[0].reshape(shards, cap, half)).reshape(shards * cap, half)]
        bases[1], *got = tied(bases[1], *got)
        out_own = low_out_pairs(at_here, marks, slot_mask, shrink, got, cap)
        out_got = swap(out_own)
        if split == 1:
            parts = add_delta(bases, [out_own, out_got], marks, [expand], shards)
            return list(ways.spread(jnp.stack(parts)))
        out_beside = lax.ppermute(out_own, "ff", ways.back(0, 1))
        across = [
            (2 * f + v, 2 * g + 1 - v) for f, g in ways.back(0, 1) for v in range(2)
        ]
        out_across = lax.ppermute(out_own, ("ff", "var"), across)
        parts = add_delta(
            bases,
            [out_own, out_got, out_beside, out_across],
            marks,
            [expand, expand_beside],
            ways.slow,
        )
        return ways.slow_steps(parts)

    if most <= USUAL:
        parts = partial_sums(most)
    else:
        parts = lax.cond(
            highest[0] < USUAL, lambda: partial_sums(USUAL), lambda: partial_sums(most)
        )
    return sum(part.astype(F32) for part in parts).astype(BF)


def solution(mesh):
    placed = (
        P(("groups", "ff"), "var"),
        P("var", "ff"),
        P("var", "ff"),
        P("ff", "var"),
        P(("groups", "ff"), None, "var"),
        P(("groups", "ff"), None, "var", None),
        P(("groups", "ff"), None, None),
        P(("groups", "ff"), None, "var"),
        P("groups", None),
        P("groups"),
    )
    return jax.shard_map(
        per_device,
        mesh=mesh,
        in_specs=placed,
        out_specs=P(("groups", "ff"), "var"),
        check_vma=False,
    )
```

```python
import functools

import jax
import jax.numpy as jnp
from jax import lax
from jax.experimental import pallas as pl
from jax.experimental.pallas import tpu as pltpu
from jax.sharding import PartitionSpec as P

MOST = 8
DIRECT = 8
MINE, NEXT, STEP, PLACE, ARRIVE, PACKED = range(6)
USUAL = 16
USUAL_PAIR = 24
BF = jnp.bfloat16
F32 = jnp.float32
I32 = jnp.int32
MIB = 1024 * 1024


def dot(a, b):
    return jnp.dot(a, b, preferred_element_type=F32)


def dot_last(a, b):
    return lax.dot_general(a, b, (((1,), (1,)), ((), ())), preferred_element_type=F32)


def params(mib):
    return pltpu.CompilerParams(vmem_limit_bytes=int(mib * MIB))


def cost(flops, moved):
    return pl.CostEstimate(flops=flops, bytes_accessed=moved, transcendentals=0)


SCALARS = pl.BlockSpec(memory_space=pltpu.SMEM)
WHOLE = pl.BlockSpec(memory_space=pltpu.VMEM)
FAR = pl.BlockSpec(memory_space=pltpu.HBM)


def fixed(array):
    zeros = (0,) * array.ndim
    return pl.BlockSpec(array.shape, lambda *_: zeros)


def one_hot(count, cell):
    lines = lax.broadcasted_iota(I32, (count, cell.shape[1]), 0)
    return (lines == cell).astype(F32).astype(BF)


def dot_first(a, b):
    return lax.dot_general(a, b, (((0,), (0,)), ((), ())), preferred_element_type=F32)


class Ways:
    def __init__(self):
        self.shards = lax.axis_size("ff")
        self.fast = 2 if self.shards % 2 == 0 else 1
        self.slow = self.shards // self.fast
        self.direct = self.shards <= DIRECT
        me = lax.axis_index("ff").astype(I32)
        steps = jnp.arange(self.shards, dtype=I32)
        if self.direct:
            slow = (me // self.fast - steps % self.slow) % self.slow
            fast = (me % self.fast - steps // self.slow) % self.fast
            self.order = slow * self.fast + fast
        else:
            self.order = steps

    def back(self, a, c):
        S, F = self.slow, self.fast
        return [(s * F + f, (s - a) % S * F + (f - c) % F) for s in range(S) for f in range(F)]

    def gather(self, block, other):
        if not self.direct:
            return list(lax.all_gather(block, "ff")), other
        got = [block] + [
            lax.ppermute(block, "ff", self.back(-a, 0)) for a in range(1, self.slow)
        ]
        other, got[1] = tied(other, got[1])
        for c in range(1, self.fast):
            got += [lax.ppermute(part, "ff", self.back(0, -c)) for part in got[: self.slow]]
        return got, other

    def spread(self, blocks):
        return lax.all_to_all(blocks, "ff", 0, 0, tiled=True)

    def slow_steps(self, blocks):
        got = [blocks[0]] + [None] * (self.slow - 1)
        for a in range(1, self.slow):
            got[(-a) % self.slow] = lax.ppermute(blocks[a], "ff", self.back(a, 0))
        return got


def tables_kernel(
    ways,
    slots,
    order_ref,
    me_ref,
    ids_ref,
    slot_ref,
    x_ref,
    shrink_ref,
    marks_ref,
    in_ref,
    out_ref,
    facts_ref,
    kept_ref,
    held_ref,
    sems,
):
    copies = [
        pltpu.make_async_copy(x_ref, kept_ref, sems.at[0]),
        pltpu.make_async_copy(shrink_ref, held_ref, sems.at[1]),
    ]
    for copy in copies:
        copy.start()
    rows, variants = ids_ref.shape[0], slot_ref.shape[1]
    shards = order_ref.shape[0]
    own_rows = rows // shards
    me = me_ref[0].astype(F32)
    order = [order_ref[b].astype(F32) for b in range(shards)]
    count = lambda shape, axis: lax.broadcasted_iota(I32, shape, axis).astype(F32)
    across = lambda a: jnp.sum(a, axis=1, keepdims=True)
    along = lambda a: jnp.sum(a, axis=0, keepdims=True)
    line, lane = count((rows, rows), 0), count((rows, rows), 1)
    matches = ids_ref[...].astype(F32) == count((rows, variants), 1)
    slot = across(jnp.where(matches, slot_ref[...].astype(F32), 0.0))
    owner = across((slot >= (count((rows, shards), 1) + 1.0) * slots).astype(F32))
    owner_along = along(jnp.where(line == lane, owner, 0.0))
    same = owner == owner_along
    place = across((same & (lane < line)).astype(F32))
    paired = ways.direct and ways.fast == 2
    beside = jnp.zeros_like(place)
    if paired:
        odd = across((owner == 2.0 * count((rows, shards), 1) + 1.0).astype(F32))
        beside = across((owner + 1.0 - 2.0 * odd == owner_along).astype(F32))
    facts_ref[0] = jnp.max(place).astype(I32)
    facts_ref[1] = jnp.max(across(same.astype(F32)) + beside).astype(I32)
    facts_ref[2] = jnp.sum((owner == me).astype(F32)).astype(I32)
    facts_ref[3] = jnp.sum((owner == order[ways.slow % shards]).astype(F32)).astype(I32)
    row_along, row_down = count((1, rows), 1), count((rows, 1), 0)
    at_along, at_down = row_along, row_down
    for b in range(shards):
        shift = (order[b] - b) * own_rows
        low, high = b * own_rows, (b + 1) * own_rows
        at_along = jnp.where((row_along >= low) & (row_along < high), row_along + shift, at_along)
        at_down = jnp.where((row_down >= low) & (row_down < high), row_down + shift, at_down)
    turned = lambda a: along(jnp.where(line == at_along, a, 0.0))
    slot_along = along(jnp.where(line == lane, slot, 0.0))
    slot = across(jnp.where(lane == at_down, slot_along, 0.0))
    owner, place, beside = turned(owner), turned(place), turned(beside)
    step = jnp.zeros_like(owner)
    arrive, packed = step, place
    for b in range(shards):
        hit = owner == order[b]
        step = jnp.where(hit, float(b), step)
        arrive = jnp.where(hit, float(b % ways.slow if paired else b), arrive)
        if paired and b >= ways.slow:
            packed = jnp.where(hit, place + beside, packed)
    lines = {
        MINE: jnp.where(owner == me, place, -1.0),
        NEXT: jnp.where(owner == order[ways.slow % shards], place, -1.0),
        STEP: step,
        PLACE: place,
        ARRIVE: arrive,
        PACKED: packed,
    }
    for n, values in lines.items():
        marks_ref[n : n + 1] = values.astype(I32)
    local = slot - me * slots
    for ref in (in_ref, out_ref):
        wide = ref.shape[1] // slots
        column = count(ref.shape, 1)
        inside = (column >= local * wide) & (column < (local + 1.0) * wide)
        ref[...] = inside.astype(F32).astype(ref.dtype)
    for copy in copies:
        copy.wait()


def tables(ways, me, ids, variant_slot, x, shrink, slots, rank):
    rows = ids.shape[0]
    return pl.pallas_call(
        functools.partial(tables_kernel, ways, slots),
        out_shape=(
            jax.ShapeDtypeStruct((8, rows), I32),
            jax.ShapeDtypeStruct((rows, slots * 2 * rank), F32),
            jax.ShapeDtypeStruct((rows, slots * rank), BF),
            jax.ShapeDtypeStruct((4,), I32),
            jax.ShapeDtypeStruct(x.shape, BF),
            jax.ShapeDtypeStruct(shrink.shape, BF),
        ),
        in_specs=[SCALARS, SCALARS, WHOLE, WHOLE, FAR, FAR],
        out_specs=(WHOLE, WHOLE, WHOLE, SCALARS, WHOLE, WHOLE),
        scratch_shapes=[pltpu.SemaphoreType.DMA((2,))],
        compiler_params=params(52),
        cost_estimate=cost(0, 4 * x.size + 4 * shrink.size),
    )(ways.order, me, ids, variant_slot, x, shrink)


def low_in_kernel(count, shrink_ref, mask_ref, *refs):
    parts, x_ref, out_ref = refs[:count], refs[count], refs[count + 1]
    x = jnp.concatenate([part[...].astype(F32) for part in parts], axis=0).astype(BF)
    x_ref[...] = x

    @pl.when(pl.program_id(0) == 0)
    def _():
        out_ref[...] = jnp.zeros_like(out_ref)

    out_ref[...] += jnp.where(mask_ref[...] > 0, dot_last(x, shrink_ref[...]), 0.0)


def low_in_pairs(parts, shrink, mask):
    count = len(parts)
    own_rows, width = parts[0].shape
    rows, block = count * own_rows, min(1024, width)
    return pl.pallas_call(
        lambda *refs: low_in_kernel(count, *refs),
        out_shape=(
            jax.ShapeDtypeStruct((rows, width), BF),
            jax.ShapeDtypeStruct(mask.shape, F32),
        ),
        grid=(width // block,),
        in_specs=[pl.BlockSpec((shrink.shape[0], block), lambda n: (0, n)), fixed(mask)]
        + [pl.BlockSpec((own_rows, block), lambda n: (0, n))] * count,
        out_specs=(pl.BlockSpec((rows, block), lambda n: (0, n)), fixed(mask)),
        compiler_params=params(16),
        cost_estimate=cost(2 * rows * width * shrink.shape[0], 2 * shrink.size + 4 * rows * width),
    )(shrink, mask, *parts)


def expand_kernel(
    cap,
    fast,
    at_ref,
    own_ref,
    got_ref,
    marks_ref,
    cols_ref,
    far_ref,
    near_ref,
    *refs,
):
    out_refs, held, sems = refs[:-2], refs[-2], refs[-1]
    half = out_refs[0].shape[1]
    count = at_ref.shape[0]
    columns = [pl.ds(pl.multiple_of(at_ref[b] * half, half), half) for b in range(count)]
    copies = []
    for b in range(count):
        put = held.at[:, pl.ds(b * half, half)]
        copies.append(pltpu.make_async_copy(near_ref.at[:, columns[b]], put, sems.at[b]))
        copies[b].start()
    low = (own_ref[...] + got_ref[...]).astype(BF)
    picked = dot(one_hot(cap, marks_ref[MINE : MINE + 1]), low).astype(BF)
    lhs = jnp.concatenate([dot(picked, cols_ref[kind]) for kind in range(2)], axis=0).astype(BF)
    tall = lhs.shape[0]
    for b in range(count):
        copies[b].wait()
        both = jnp.concatenate([held[:, pl.ds(b * half, half)], far_ref[:, columns[b]]], axis=0)
        at = b % (count // fast)
        out_refs[b * fast // count][pl.ds(at * tall, tall)] = dot(lhs, both).astype(BF)


def expand_rows(at, own, got, marks, cols, near, far, cap, fast):
    depth, width = near.shape
    shards = at.shape[0]
    half = width // (2 * shards)
    out = jax.ShapeDtypeStruct((2 * cap * shards // fast, half), BF)
    return pl.pallas_call(
        functools.partial(expand_kernel, cap, fast),
        out_shape=(out,) * fast,
        in_specs=[SCALARS] + [WHOLE] * 5 + [FAR],
        scratch_shapes=[
            pltpu.VMEM((depth, width // 2), BF),
            pltpu.SemaphoreType.DMA((shards,)),
        ],
        compiler_params=params(52),
        cost_estimate=cost(8 * cap * depth * width, 4 * (depth + cap) * width),
    )(at, own, got, marks, cols, far, near)


def base_kernel(side_ref, x_ref, gate_ref, up_ref, out_ref, held, sums, sems):
    half = held.shape[2]
    chunks = sems.shape[1]
    depth = held.shape[1] // chunks
    columns = pl.ds(pl.multiple_of(side_ref[0] * half, half), half)
    copies = []
    for c in range(chunks):
        here = pl.ds(c * depth, depth)
        for kind, weight in enumerate((gate_ref, up_ref)):
            copy = pltpu.make_async_copy(
                weight.at[here, columns], held.at[kind, here], sems.at[kind, c]
            )
            copy.start()
            copies.append((kind, here, copy))
    for kind, here, copy in copies:
        copy.wait()
        part = dot(x_ref[:, here], held[kind, here])
        sums[kind] = part if here.start == 0 else sums[kind] + part
    out_ref[...] = sums[...].astype(out_ref.dtype)


def base_half(side, x, gate_weight, up_weight, half, kind):
    rows, width = x.shape
    chunks = max(width // 512, 1)
    return pl.pallas_call(
        base_kernel,
        out_shape=jax.ShapeDtypeStruct((2, rows, half), kind),
        in_specs=[SCALARS, WHOLE, FAR, FAR],
        out_specs=WHOLE,
        scratch_shapes=[
            pltpu.VMEM((2, width, half), BF),
            pltpu.VMEM((2, rows, half), F32),
            pltpu.SemaphoreType.DMA((2, chunks)),
        ],
        compiler_params=params(48),
        cost_estimate=cost(4 * rows * width * half, 4 * width * half + 2 * rows * width),
    )(side, x, gate_weight, up_weight)


def hidden_kernel(cap, room, count, own_ref, got_ref, marks_ref, *refs):
    parts, hid_ref, out_refs = refs[:count], refs[count], refs[count + 1 :]
    half = hid_ref.shape[1]
    cells = sum(part.shape[0] for part in parts)
    first_cell = marks_ref[ARRIVE : ARRIVE + 1] * (2 * room) + marks_ref[PACKED : PACKED + 1]
    places = [one_hot(cells, first_cell + kind * room) for kind in range(2)]
    tall = out_refs[0].shape[0]
    leave = marks_ref[STEP : STEP + 1] * cap + marks_ref[PLACE : PLACE + 1]
    send = one_hot(tall * len(out_refs), leave)
    block = min(256, half)
    for first in range(0, half, block):
        here = pl.ds(first, block)
        delta = jnp.concatenate([part[:, here] for part in parts], axis=0)
        gate, up = [
            own_ref[kind, :, here]
            + got_ref[kind, :, here].astype(F32)
            + dot_first(places[kind], delta)
            for kind in range(2)
        ]
        hidden = (gate / (1.0 + jnp.exp(-gate)) * up).astype(BF)
        hid_ref[:, here] = hidden
        sent = dot(send, hidden).astype(BF)
        for n, out_ref in enumerate(out_refs):
            out_ref[:, here] = sent[n * tall : (n + 1) * tall]


def hidden_half(own, got, parts, marks, cap, room, shards, count):
    rows, half = own.shape[1:]
    cells = shards * cap
    return pl.pallas_call(
        functools.partial(hidden_kernel, cap, room, len(parts)),
        out_shape=(jax.ShapeDtypeStruct((rows, half), BF),)
        + (jax.ShapeDtypeStruct((cells // count, half), BF),) * count,
        compiler_params=params(40),
        cost_estimate=cost(10 * half * cells * rows, 2 * half * (6 * rows + 3 * cells)),
    )(own, got, marks, *parts)


def pack_kernel(cap, facts_ref, own_ref, got_ref, *out_refs):
    column = lax.broadcasted_iota(I32, (1, 4 * cap), 1)
    from_got = column >= 2 * cap
    column = column - jnp.where(from_got, 2 * cap, 0)
    kind = jnp.where(column >= cap, 1, 0)
    row = column - kind * cap
    live = row < jnp.where(from_got, facts_ref[3], facts_ref[2])
    row = row + jnp.where(from_got, facts_ref[2], 0)
    room = out_refs[0].shape[0] // 2
    packing = one_hot(2 * room, jnp.where(live, row + kind * room, -1))
    for a, out_ref in enumerate(out_refs):
        here = pl.ds(a * 2 * cap, 2 * cap)
        both = jnp.concatenate([own_ref[here], got_ref[here]], axis=0)
        out_ref[...] = dot(packing, both).astype(BF)


def pack(facts, own, got, cap, room, count):
    half = own.shape[1]
    return pl.pallas_call(
        functools.partial(pack_kernel, cap),
        out_shape=(jax.ShapeDtypeStruct((2 * room, half), BF),) * count,
        in_specs=[SCALARS, WHOLE, WHOLE],
        compiler_params=params(16),
        cost_estimate=cost(0, 8 * own.size),
    )(facts, own, got)


def relay_kernel(own_ref, got_ref, *out_refs):
    cap = out_refs[0].shape[0] // 2
    for a, out_ref in enumerate(out_refs):
        here = pl.ds(a * cap, cap)
        out_ref[:cap] = own_ref[here]
        out_ref[cap:] = got_ref[here]


def relay(own, got, count):
    tall, half = own.shape
    return pl.pallas_call(
        relay_kernel,
        out_shape=(jax.ShapeDtypeStruct((2 * tall // count, half), BF),) * count,
        compiler_params=params(16),
        cost_estimate=cost(0, 8 * tall * half),
    )(own, got)


def down_kernel(start, core_ref, near_ref, far_ref, weight_ref, *refs):
    out_refs, held, sems = refs[:-2], refs[-2], refs[-1]
    chunks = sems.shape[1]
    half, width = held.shape[1:]
    block = width // chunks
    tall = out_refs[0].shape[0]
    copies = []
    for c in range(chunks):
        here = pl.ds(c * block, block)
        for side, at in enumerate((core_ref[0], 1 - core_ref[0])):
            lines = pl.ds(pl.multiple_of(at * half, half), half)
            copy = pltpu.make_async_copy(
                weight_ref.at[lines, pl.ds(start + c * block, block)],
                held.at[side, :, here],
                sems.at[side, c],
            )
            copy.start()
            copies.append(copy)
    for c in range(chunks):
        here = pl.ds(c * block, block)
        copies[2 * c].wait()
        copies[2 * c + 1].wait()
        total = dot(near_ref[...], held[0, :, here]) + dot(far_ref[...], held[1, :, here])
        for n, out_ref in enumerate(out_refs):
            out_ref[:, here] = total[n * tall : (n + 1) * tall].astype(out_ref.dtype)


def down_base(core, near, far, weight, start, width, kinds):
    rows, half = near.shape
    chunks = max(width // 512, 1)
    outs = tuple(jax.ShapeDtypeStruct((rows // len(kinds), width), kind) for kind in kinds)
    return pl.pallas_call(
        functools.partial(down_kernel, start),
        out_shape=outs,
        in_specs=[SCALARS, WHOLE, WHOLE, FAR],
        out_specs=(WHOLE,) * len(outs),
        scratch_shapes=[
            pltpu.VMEM((2, half, width), BF),
            pltpu.SemaphoreType.DMA((2, chunks)),
        ],
        compiler_params=params(48),
        cost_estimate=cost(4 * rows * half * width, 4 * half * width + 4 * rows * width),
    )(core, near, far, weight)


def low_out_kernel(cap, count, at_ref, marks_ref, slot_ref, shrink_ref, *refs):
    parts, out_ref = refs[:count], refs[count]
    half = parts[0].shape[1]
    blocks = [part[r : r + cap] for r in range(0, parts[0].shape[0], cap) for part in parts]
    pairs = jnp.zeros(out_ref.shape, F32)
    for b, block in enumerate(blocks):
        columns = pl.ds(pl.multiple_of(at_ref[b] * half, half), half)
        pairs += dot_last(block, shrink_ref[:, columns])
    mask = dot(one_hot(cap, marks_ref[MINE : MINE + 1]), slot_ref[...])
    out_ref[...] = jnp.where(mask > 0.5, pairs, 0.0)


def low_out_pairs(at, marks, slot_mask, shrink, parts, cap):
    count = len(parts)
    half = parts[0].shape[1]
    depth = shrink.shape[0]
    return pl.pallas_call(
        functools.partial(low_out_kernel, cap, count),
        out_shape=jax.ShapeDtypeStruct((cap, depth), F32),
        in_specs=[SCALARS] + [WHOLE] * (3 + count),
        compiler_params=params(16),
        cost_estimate=cost(
            2 * cap * depth * at.shape[0] * half, 2 * at.shape[0] * half * (depth + cap)
        ),
    )(at, marks, slot_mask, shrink, *parts)


def add_kernel(owners, sides, *refs):
    base_refs, refs = refs[: owners * sides], refs[owners * sides :]
    low_refs, refs = refs[: 2 * owners], refs[2 * owners :]
    marks_ref, expand_refs, out_refs = refs[0], refs[1 : owners + 1], refs[owners + 1 :]
    rows = base_refs[0].shape[0]
    spreads = []
    for n in range(owners):
        low = (low_refs[2 * n][...] + low_refs[2 * n + 1][...]).astype(BF)
        pick = one_hot(low.shape[0], marks_ref[MINE + n : MINE + n + 1, :rows])
        spreads.append(dot_first(pick, low).astype(BF))
    spread = jnp.concatenate(spreads, axis=1)
    own_rows, width = out_refs[0].shape
    side = width // sides
    block = min(1024, side)
    for first in range(0, width, block):
        here = pl.ds(first, block)
        inside = pl.ds(first % side, block)
        expand = jnp.concatenate([ref[:, here] for ref in expand_refs], axis=0)
        total = dot(spread, expand)
        for base_ref in base_refs[first // side :: sides]:
            total += base_ref[:, inside].astype(F32)
        for b, out_ref in enumerate(out_refs):
            out_ref[:, here] = total[b * own_rows : (b + 1) * own_rows].astype(BF)


def add_delta(bases, lows, marks, expands, count):
    owners = len(expands)
    rows = bases[0].shape[0]
    depth, width = expands[0].shape
    return pl.pallas_call(
        functools.partial(add_kernel, owners, len(bases) // owners),
        out_shape=(jax.ShapeDtypeStruct((rows // count, width), BF),) * count,
        compiler_params=params(32),
        cost_estimate=cost(
            2 * rows * depth * owners * width, width * (6 * rows + 2 * depth) * owners
        ),
    )(*bases, *lows, marks, *expands)


def tied(first, *others):
    return lax.optimization_barrier((first, *others))


def per_device(
    tokens,
    gate_weight,
    up_weight,
    down_weight,
    shrink_gu,
    expand_gu,
    shrink_down,
    expand_down,
    variant_ids,
    variant_slot,
):
    ways = Ways()
    shards, order = ways.shards, ways.order
    me = lax.axis_index("ff").astype(I32)
    core = lax.axis_index("var").astype(I32)
    groups = lax.axis_size("groups")
    own_rows, width = tokens.shape
    rows = own_rows * shards
    slots = shrink_gu.shape[0]
    variants = variant_slot.shape[0]
    rank = shrink_down.shape[1]
    half_rank = expand_gu.shape[2]
    half = gate_weight.shape[1] // 2
    most = min(slots * MOST, rows)
    here = core.reshape(1)
    there = 1 - here
    at_here = 2 * order + core
    split = ways.fast if ways.direct else 1
    swap = lambda a: lax.ppermute(a, "var", [(0, 1), (1, 0)])

    near = expand_gu.reshape(slots * 2 * half_rank, -1)
    token_parts, far = ways.gather(tokens, swap(near))
    shrink_in = shrink_gu.reshape(slots * 2 * rank, width)
    if ways.direct:
        first_hop = ways.slow + 1
        variant_ids, variant_slot, shrink_in, token_parts[first_hop] = tied(
            variant_ids, variant_slot, shrink_in, token_parts[first_hop]
        )
    marks, mask_in, slot_mask, facts, token_parts[0], shrink_in = tables(
        ways,
        me.reshape(1),
        variant_ids,
        variant_slot.reshape(1, variants),
        token_parts[0],
        shrink_in,
        slots,
        rank,
    )
    most_facts = facts
    for turn in range(1, 1 if ways.direct else groups):
        pairs = [(g, (g + turn) % groups) for g in range(groups)]
        most_facts = jnp.maximum(most_facts, lax.ppermute(facts, "groups", pairs))
    kinds = jnp.arange(2, dtype=I32)
    in_cols = jnp.arange(slots * 2 * rank, dtype=I32)
    rank_at = in_cols % rank
    kind_at = in_cols // rank % 2
    row_at = in_cols // (2 * rank) * (2 * half_rank) + kind_at * half_rank + rank_at % half_rank
    depth = slots * 2 * half_rank
    both_cols = jnp.arange(2 * depth, dtype=I32)
    wanted = row_at + jnp.where(rank_at // half_rank == core, 0, depth)
    hit = wanted[:, None] == both_cols[None, :]
    cols = (hit[None] & (kind_at[None, :] == kinds[:, None])[:, :, None]).astype(BF)

    x, low_own = low_in_pairs(token_parts, shrink_in, mask_in)
    low_got = swap(low_own)

    def partial_sums(cap, room):
        made = expand_rows(at_here, low_own, low_got, marks, cols, near, far, cap, split)
        held, *made = tied(x, *made)
        expand = expand_down.reshape(slots * rank, width)
        if split == 2:
            beside = lax.ppermute(made[1], "ff", ways.back(0, 1))
            base_there = base_half(there, held, gate_weight, up_weight, half, BF)
            base_there, beside, expand = tied(base_there, beside, expand)
            made = pack(facts, made[0], beside, cap, room, ways.slow)
            held, *made = tied(held, *made)
            delta = ways.slow_steps(made)
            expand_beside = lax.ppermute(expand, "ff", ways.back(0, 1))
        else:
            base_there = base_half(there, held, gate_weight, up_weight, half, BF)
            delta = ways.spread(made[0].reshape(shards, 2 * cap, half))
            delta = [delta.reshape(2 * shards * cap, half)]
        base_got = swap(base_there)
        base_own = base_half(here, held, gate_weight, up_weight, half, F32)
        if split == 2:
            base_own, expand_beside = tied(base_own, expand_beside)
        hidden, *sent = hidden_half(
            base_own, base_got, delta, marks, cap, room, shards, split
        )
        hidden_far = swap(hidden)
        shrink = shrink_down.reshape(slots * rank, -1)
        side = width // 2
        down = functools.partial(down_base, here, hidden, hidden_far, down_weight)
        if split == 2:
            beside = lax.ppermute(sent[1], "ff", ways.back(0, 1))
            left, left_sent = down(0, side, (F32, BF))
            left_sent, beside = tied(left_sent, beside)
            left_beside = lax.ppermute(left_sent, "ff", ways.back(0, 1))
            sent = relay(sent[0], beside, ways.slow)
            hidden, *sent = tied(hidden, *sent)
            down = functools.partial(down_base, here, hidden, hidden_far, down_weight)
            got = ways.slow_steps(sent)
            right, right_sent = down(side, side, (F32, BF))
            right_sent, left_beside, *got = tied(right_sent, left_beside, *got)
            right_beside = lax.ppermute(right_sent, "ff", ways.back(0, 1))
            bases = [left, right, left_beside, right_beside]
        else:
            bases = [down(0, side, (F32,))[0], down(side, side, (F32,))[0]]
            got = [ways.spread(sent[0].reshape(shards, cap, half)).reshape(shards * cap, half)]
        bases[1], *got = tied(bases[1], *got)
        out_own = low_out_pairs(at_here, marks, slot_mask, shrink, got, cap)
        out_got = swap(out_own)
        if split == 1:
            parts = add_delta(bases, [out_own, out_got], marks, [expand], shards)
            return list(ways.spread(jnp.stack(parts)))
        out_beside = lax.ppermute(out_own, "ff", ways.back(0, 1))
        across = [
            (2 * f + v, 2 * g + 1 - v) for f, g in ways.back(0, 1) for v in range(2)
        ]
        out_across = lax.ppermute(out_own, ("ff", "var"), across)
        parts = add_delta(
            bases,
            [out_own, out_got, out_beside, out_across],
            marks,
            [expand, expand_beside],
            ways.slow,
        )
        return ways.slow_steps(parts)

    most_room = 2 * most if split == 2 else most
    if most <= USUAL:
        parts = partial_sums(most, most_room)
    else:
        usual = most_facts[0] < USUAL
        if split == 2:
            usual = usual & (most_facts[1] <= USUAL_PAIR)
        parts = lax.cond(
            usual,
            lambda: partial_sums(USUAL, USUAL_PAIR if split == 2 else USUAL),
            lambda: partial_sums(most, most_room),
        )
    return sum(part.astype(F32) for part in parts).astype(BF)


def solution(mesh):
    placed = (
        P(("groups", "ff"), "var"),
        P("var", "ff"),
        P("var", "ff"),
        P("ff", "var"),
        P(("groups", "ff"), None, "var"),
        P(("groups", "ff"), None, "var", None),
        P(("groups", "ff"), None, None),
        P(("groups", "ff"), None, "var"),
        P("groups", None),
        P("groups"),
    )
    return jax.shard_map(
        per_device,
        mesh=mesh,
        in_specs=placed,
        out_specs=P(("groups", "ff"), "var"),
        check_vma=False,
    )
```

```python
import functools

import jax
import jax.numpy as jnp
from jax import lax
from jax.experimental import pallas as pl
from jax.experimental.pallas import tpu as pltpu
from jax.sharding import PartitionSpec as P

MOST = 8
DIRECT = 8
MINE, NEXT, STEP, PLACE, ARRIVE, PACKED = range(6)
USUAL = 16
USUAL_PAIR = 24
BF = jnp.bfloat16
F32 = jnp.float32
I32 = jnp.int32
MIB = 1024 * 1024


def dot(a, b):
    return jnp.dot(a, b, preferred_element_type=F32)


def dot_last(a, b):
    return lax.dot_general(a, b, (((1,), (1,)), ((), ())), preferred_element_type=F32)


def params(mib):
    return pltpu.CompilerParams(vmem_limit_bytes=int(mib * MIB))


def cost(flops, moved):
    return pl.CostEstimate(flops=flops, bytes_accessed=moved, transcendentals=0)


SCALARS = pl.BlockSpec(memory_space=pltpu.SMEM)
WHOLE = pl.BlockSpec(memory_space=pltpu.VMEM)
FAR = pl.BlockSpec(memory_space=pltpu.HBM)


def fixed(array):
    zeros = (0,) * array.ndim
    return pl.BlockSpec(array.shape, lambda *_: zeros)


def one_hot(count, cell):
    lines = lax.broadcasted_iota(I32, (count, cell.shape[1]), 0)
    return (lines == cell).astype(F32).astype(BF)


def dot_first(a, b):
    return lax.dot_general(a, b, (((0,), (0,)), ((), ())), preferred_element_type=F32)


class Ways:
    def __init__(self):
        self.shards = lax.axis_size("ff")
        self.fast = 2 if self.shards % 2 == 0 else 1
        self.slow = self.shards // self.fast
        self.direct = self.shards <= DIRECT
        me = lax.axis_index("ff").astype(I32)
        steps = jnp.arange(self.shards, dtype=I32)
        if self.direct:
            slow = (me // self.fast - steps % self.slow) % self.slow
            fast = (me % self.fast - steps // self.slow) % self.fast
            self.order = slow * self.fast + fast
        else:
            self.order = steps

    def back(self, a, c):
        S, F = self.slow, self.fast
        return [(s * F + f, (s - a) % S * F + (f - c) % F) for s in range(S) for f in range(F)]

    def gather(self, block, other):
        if not self.direct:
            return list(lax.all_gather(block, "ff")), other
        got = [block] + [
            lax.ppermute(block, "ff", self.back(-a, 0)) for a in range(1, self.slow)
        ]
        other, got[1] = tied(other, got[1])
        for c in range(1, self.fast):
            got += [lax.ppermute(part, "ff", self.back(0, -c)) for part in got[: self.slow]]
        return got, other

    def spread(self, blocks):
        return lax.all_to_all(blocks, "ff", 0, 0, tiled=True)

    def slow_steps(self, blocks):
        got = [blocks[0]] + [None] * (self.slow - 1)
        for a in range(1, self.slow):
            got[(-a) % self.slow] = lax.ppermute(blocks[a], "ff", self.back(a, 0))
        return got


def tables_kernel(
    ways,
    slots,
    order_ref,
    me_ref,
    ids_ref,
    slot_ref,
    x_ref,
    shrink_ref,
    marks_ref,
    in_ref,
    out_ref,
    facts_ref,
    kept_ref,
    held_ref,
    sems,
):
    copies = [
        pltpu.make_async_copy(x_ref, kept_ref, sems.at[0]),
        pltpu.make_async_copy(shrink_ref, held_ref, sems.at[1]),
    ]
    for copy in copies:
        copy.start()
    rows, variants = ids_ref.shape[0], slot_ref.shape[1]
    shards = order_ref.shape[0]
    own_rows = rows // shards
    me = me_ref[0].astype(F32)
    order = [order_ref[b].astype(F32) for b in range(shards)]
    count = lambda shape, axis: lax.broadcasted_iota(I32, shape, axis).astype(F32)
    across = lambda a: jnp.sum(a, axis=1, keepdims=True)
    along = lambda a: jnp.sum(a, axis=0, keepdims=True)
    line, lane = count((rows, rows), 0), count((rows, rows), 1)
    matches = ids_ref[...].astype(F32) == count((rows, variants), 1)
    slot = across(jnp.where(matches, slot_ref[...].astype(F32), 0.0))
    owner = across((slot >= (count((rows, shards), 1) + 1.0) * slots).astype(F32))
    owner_along = along(jnp.where(line == lane, owner, 0.0))
    same = owner == owner_along
    place = across((same & (lane < line)).astype(F32))
    paired = ways.direct and ways.fast == 2
    beside = pair = jnp.zeros_like(place)
    if paired:
        odd = across((owner == 2.0 * count((rows, shards), 1) + 1.0).astype(F32))
        beside = across((owner + 1.0 - 2.0 * odd == owner_along).astype(F32))
        pair = across(same.astype(F32)) + beside
    facts_ref[0] = jnp.where(
        (jnp.max(place) < USUAL) & (jnp.max(pair) <= USUAL_PAIR), 0, 1
    )
    facts_ref[1] = jnp.sum((owner == me).astype(F32)).astype(I32)
    facts_ref[2] = jnp.sum((owner == order[ways.slow % shards]).astype(F32)).astype(I32)
    row_along, row_down = count((1, rows), 1), count((rows, 1), 0)
    at_along, at_down = row_along, row_down
    for b in range(shards):
        shift = (order[b] - b) * own_rows
        low, high = b * own_rows, (b + 1) * own_rows
        at_along = jnp.where((row_along >= low) & (row_along < high), row_along + shift, at_along)
        at_down = jnp.where((row_down >= low) & (row_down < high), row_down + shift, at_down)
    turned = lambda a: along(jnp.where(line == at_along, a, 0.0))
    slot_along = along(jnp.where(line == lane, slot, 0.0))
    slot = across(jnp.where(lane == at_down, slot_along, 0.0))
    owner, place, beside = turned(owner), turned(place), turned(beside)
    step = jnp.zeros_like(owner)
    arrive, packed = step, place
    for b in range(shards):
        hit = owner == order[b]
        step = jnp.where(hit, float(b), step)
        arrive = jnp.where(hit, float(b % ways.slow if paired else b), arrive)
        if paired and b >= ways.slow:
            packed = jnp.where(hit, place + beside, packed)
    lines = {
        MINE: jnp.where(owner == me, place, -1.0),
        NEXT: jnp.where(owner == order[ways.slow % shards], place, -1.0),
        STEP: step,
        PLACE: place,
        ARRIVE: arrive,
        PACKED: packed,
    }
    for n, values in lines.items():
        marks_ref[n : n + 1] = values.astype(I32)
    local = slot - me * slots
    for ref in (in_ref, out_ref):
        wide = ref.shape[1] // slots
        column = count(ref.shape, 1)
        inside = (column >= local * wide) & (column < (local + 1.0) * wide)
        ref[...] = inside.astype(F32).astype(ref.dtype)
    for copy in copies:
        copy.wait()


def tables(ways, me, ids, variant_slot, x, shrink, slots, rank):
    rows = ids.shape[0]
    return pl.pallas_call(
        functools.partial(tables_kernel, ways, slots),
        out_shape=(
            jax.ShapeDtypeStruct((8, rows), I32),
            jax.ShapeDtypeStruct((rows, slots * 2 * rank), F32),
            jax.ShapeDtypeStruct((rows, slots * rank), BF),
            jax.ShapeDtypeStruct((3,), I32),
            jax.ShapeDtypeStruct(x.shape, BF),
            jax.ShapeDtypeStruct(shrink.shape, BF),
        ),
        in_specs=[SCALARS, SCALARS, WHOLE, WHOLE, FAR, FAR],
        out_specs=(WHOLE, WHOLE, WHOLE, SCALARS, WHOLE, WHOLE),
        scratch_shapes=[pltpu.SemaphoreType.DMA((2,))],
        compiler_params=params(52),
        cost_estimate=cost(0, 4 * x.size + 4 * shrink.size),
    )(ways.order, me, ids, variant_slot, x, shrink)


def low_in_kernel(count, shrink_ref, mask_ref, *refs):
    parts, x_ref, out_ref = refs[:count], refs[count], refs[count + 1]
    x = jnp.concatenate([part[...].astype(F32) for part in parts], axis=0).astype(BF)
    x_ref[...] = x

    @pl.when(pl.program_id(0) == 0)
    def _():
        out_ref[...] = jnp.zeros_like(out_ref)

    out_ref[...] += jnp.where(mask_ref[...] > 0, dot_last(x, shrink_ref[...]), 0.0)


def low_in_pairs(parts, shrink, mask):
    count = len(parts)
    own_rows, width = parts[0].shape
    rows, block = count * own_rows, min(1024, width)
    return pl.pallas_call(
        lambda *refs: low_in_kernel(count, *refs),
        out_shape=(
            jax.ShapeDtypeStruct((rows, width), BF),
            jax.ShapeDtypeStruct(mask.shape, F32),
        ),
        grid=(width // block,),
        in_specs=[pl.BlockSpec((shrink.shape[0], block), lambda n: (0, n)), fixed(mask)]
        + [pl.BlockSpec((own_rows, block), lambda n: (0, n))] * count,
        out_specs=(pl.BlockSpec((rows, block), lambda n: (0, n)), fixed(mask)),
        compiler_params=params(16),
        cost_estimate=cost(2 * rows * width * shrink.shape[0], 2 * shrink.size + 4 * rows * width),
    )(shrink, mask, *parts)


def expand_kernel(
    cap,
    fast,
    at_ref,
    own_ref,
    got_ref,
    marks_ref,
    cols_ref,
    far_ref,
    near_ref,
    *refs,
):
    out_refs, held, sems = refs[:-2], refs[-2], refs[-1]
    half = out_refs[0].shape[1]
    count = at_ref.shape[0]
    columns = [pl.ds(pl.multiple_of(at_ref[b] * half, half), half) for b in range(count)]
    copies = []
    for b in range(count):
        put = held.at[:, pl.ds(b * half, half)]
        copies.append(pltpu.make_async_copy(near_ref.at[:, columns[b]], put, sems.at[b]))
        copies[b].start()
    low = (own_ref[...] + got_ref[...]).astype(BF)
    picked = dot(one_hot(cap, marks_ref[MINE : MINE + 1]), low).astype(BF)
    lhs = jnp.concatenate([dot(picked, cols_ref[kind]) for kind in range(2)], axis=0).astype(BF)
    tall = lhs.shape[0]
    for b in range(count):
        copies[b].wait()
        both = jnp.concatenate([held[:, pl.ds(b * half, half)], far_ref[:, columns[b]]], axis=0)
        at = b % (count // fast)
        out_refs[b * fast // count][pl.ds(at * tall, tall)] = dot(lhs, both).astype(BF)


def expand_rows(at, own, got, marks, cols, near, far, cap, fast):
    depth, width = near.shape
    shards = at.shape[0]
    half = width // (2 * shards)
    out = jax.ShapeDtypeStruct((2 * cap * shards // fast, half), BF)
    return pl.pallas_call(
        functools.partial(expand_kernel, cap, fast),
        out_shape=(out,) * fast,
        in_specs=[SCALARS] + [WHOLE] * 5 + [FAR],
        scratch_shapes=[
            pltpu.VMEM((depth, width // 2), BF),
            pltpu.SemaphoreType.DMA((shards,)),
        ],
        compiler_params=params(52),
        cost_estimate=cost(8 * cap * depth * width, 4 * (depth + cap) * width),
    )(at, own, got, marks, cols, far, near)


def base_kernel(side_ref, x_ref, gate_ref, up_ref, out_ref, held, sums, sems):
    half = held.shape[2]
    chunks = sems.shape[1]
    depth = held.shape[1] // chunks
    columns = pl.ds(pl.multiple_of(side_ref[0] * half, half), half)
    copies = []
    for c in range(chunks):
        here = pl.ds(c * depth, depth)
        for kind, weight in enumerate((gate_ref, up_ref)):
            copy = pltpu.make_async_copy(
                weight.at[here, columns], held.at[kind, here], sems.at[kind, c]
            )
            copy.start()
            copies.append((kind, here, copy))
    for kind, here, copy in copies:
        copy.wait()
        part = dot(x_ref[:, here], held[kind, here])
        sums[kind] = part if here.start == 0 else sums[kind] + part
    out_ref[...] = sums[...].astype(out_ref.dtype)


def base_half(side, x, gate_weight, up_weight, half, kind):
    rows, width = x.shape
    chunks = max(width // 512, 1)
    return pl.pallas_call(
        base_kernel,
        out_shape=jax.ShapeDtypeStruct((2, rows, half), kind),
        in_specs=[SCALARS, WHOLE, FAR, FAR],
        out_specs=WHOLE,
        scratch_shapes=[
            pltpu.VMEM((2, width, half), BF),
            pltpu.VMEM((2, rows, half), F32),
            pltpu.SemaphoreType.DMA((2, chunks)),
        ],
        compiler_params=params(48),
        cost_estimate=cost(4 * rows * width * half, 4 * width * half + 2 * rows * width),
    )(side, x, gate_weight, up_weight)


def hidden_kernel(cap, room, count, own_ref, got_ref, marks_ref, *refs):
    parts, hid_ref, out_refs = refs[:count], refs[count], refs[count + 1 :]
    half = hid_ref.shape[1]
    cells = sum(part.shape[0] for part in parts)
    first_cell = marks_ref[ARRIVE : ARRIVE + 1] * (2 * room) + marks_ref[PACKED : PACKED + 1]
    places = [one_hot(cells, first_cell + kind * room) for kind in range(2)]
    tall = out_refs[0].shape[0]
    leave = marks_ref[STEP : STEP + 1] * cap + marks_ref[PLACE : PLACE + 1]
    send = one_hot(tall * len(out_refs), leave)
    block = min(256, half)
    for first in range(0, half, block):
        here = pl.ds(first, block)
        delta = jnp.concatenate([part[:, here] for part in parts], axis=0)
        gate, up = [
            own_ref[kind, :, here]
            + got_ref[kind, :, here].astype(F32)
            + dot_first(places[kind], delta)
            for kind in range(2)
        ]
        hidden = (gate / (1.0 + jnp.exp(-gate)) * up).astype(BF)
        hid_ref[:, here] = hidden
        sent = dot(send, hidden).astype(BF)
        for n, out_ref in enumerate(out_refs):
            out_ref[:, here] = sent[n * tall : (n + 1) * tall]


def hidden_half(own, got, parts, marks, cap, room, shards, count):
    rows, half = own.shape[1:]
    cells = shards * cap
    return pl.pallas_call(
        functools.partial(hidden_kernel, cap, room, len(parts)),
        out_shape=(jax.ShapeDtypeStruct((rows, half), BF),)
        + (jax.ShapeDtypeStruct((cells // count, half), BF),) * count,
        compiler_params=params(40),
        cost_estimate=cost(10 * half * cells * rows, 2 * half * (6 * rows + 3 * cells)),
    )(own, got, marks, *parts)


def pack_kernel(cap, facts_ref, own_ref, got_ref, *out_refs):
    column = lax.broadcasted_iota(I32, (1, 4 * cap), 1)
    from_got = column >= 2 * cap
    column = column - jnp.where(from_got, 2 * cap, 0)
    kind = jnp.where(column >= cap, 1, 0)
    row = column - kind * cap
    live = row < jnp.where(from_got, facts_ref[2], facts_ref[1])
    row = row + jnp.where(from_got, facts_ref[1], 0)
    room = out_refs[0].shape[0] // 2
    packing = one_hot(2 * room, jnp.where(live, row + kind * room, -1))
    for a, out_ref in enumerate(out_refs):
        here = pl.ds(a * 2 * cap, 2 * cap)
        both = jnp.concatenate([own_ref[here], got_ref[here]], axis=0)
        out_ref[...] = dot(packing, both).astype(BF)


def pack(facts, own, got, cap, room, count):
    half = own.shape[1]
    return pl.pallas_call(
        functools.partial(pack_kernel, cap),
        out_shape=(jax.ShapeDtypeStruct((2 * room, half), BF),) * count,
        in_specs=[SCALARS, WHOLE, WHOLE],
        compiler_params=params(16),
        cost_estimate=cost(0, 8 * own.size),
    )(facts, own, got)


def relay_kernel(own_ref, got_ref, *out_refs):
    cap = out_refs[0].shape[0] // 2
    for a, out_ref in enumerate(out_refs):
        here = pl.ds(a * cap, cap)
        out_ref[:cap] = own_ref[here]
        out_ref[cap:] = got_ref[here]


def relay(own, got, count):
    tall, half = own.shape
    return pl.pallas_call(
        relay_kernel,
        out_shape=(jax.ShapeDtypeStruct((2 * tall // count, half), BF),) * count,
        compiler_params=params(16),
        cost_estimate=cost(0, 8 * tall * half),
    )(own, got)


def down_kernel(start, core_ref, near_ref, far_ref, weight_ref, *refs):
    out_refs, held, sems = refs[:-2], refs[-2], refs[-1]
    chunks = sems.shape[1]
    half, width = held.shape[1:]
    block = width // chunks
    tall = out_refs[0].shape[0]
    copies = []
    for c in range(chunks):
        here = pl.ds(c * block, block)
        for side, at in enumerate((core_ref[0], 1 - core_ref[0])):
            lines = pl.ds(pl.multiple_of(at * half, half), half)
            copy = pltpu.make_async_copy(
                weight_ref.at[lines, pl.ds(start + c * block, block)],
                held.at[side, :, here],
                sems.at[side, c],
            )
            copy.start()
            copies.append(copy)
    for c in range(chunks):
        here = pl.ds(c * block, block)
        copies[2 * c].wait()
        copies[2 * c + 1].wait()
        total = dot(near_ref[...], held[0, :, here]) + dot(far_ref[...], held[1, :, here])
        for n, out_ref in enumerate(out_refs):
            out_ref[:, here] = total[n * tall : (n + 1) * tall].astype(out_ref.dtype)


def down_base(core, near, far, weight, start, width, kinds):
    rows, half = near.shape
    chunks = max(width // 512, 1)
    outs = tuple(jax.ShapeDtypeStruct((rows // len(kinds), width), kind) for kind in kinds)
    return pl.pallas_call(
        functools.partial(down_kernel, start),
        out_shape=outs,
        in_specs=[SCALARS, WHOLE, WHOLE, FAR],
        out_specs=(WHOLE,) * len(outs),
        scratch_shapes=[
            pltpu.VMEM((2, half, width), BF),
            pltpu.SemaphoreType.DMA((2, chunks)),
        ],
        compiler_params=params(48),
        cost_estimate=cost(4 * rows * half * width, 4 * half * width + 4 * rows * width),
    )(core, near, far, weight)


def low_out_kernel(cap, count, at_ref, marks_ref, slot_ref, shrink_ref, *refs):
    parts, out_ref = refs[:count], refs[count]
    half = parts[0].shape[1]
    blocks = [part[r : r + cap] for r in range(0, parts[0].shape[0], cap) for part in parts]
    pairs = jnp.zeros(out_ref.shape, F32)
    for b, block in enumerate(blocks):
        columns = pl.ds(pl.multiple_of(at_ref[b] * half, half), half)
        pairs += dot_last(block, shrink_ref[:, columns])
    mask = dot(one_hot(cap, marks_ref[MINE : MINE + 1]), slot_ref[...])
    out_ref[...] = jnp.where(mask > 0.5, pairs, 0.0)


def low_out_pairs(at, marks, slot_mask, shrink, parts, cap):
    count = len(parts)
    half = parts[0].shape[1]
    depth = shrink.shape[0]
    return pl.pallas_call(
        functools.partial(low_out_kernel, cap, count),
        out_shape=jax.ShapeDtypeStruct((cap, depth), F32),
        in_specs=[SCALARS] + [WHOLE] * (3 + count),
        compiler_params=params(16),
        cost_estimate=cost(
            2 * cap * depth * at.shape[0] * half, 2 * at.shape[0] * half * (depth + cap)
        ),
    )(at, marks, slot_mask, shrink, *parts)


def add_kernel(owners, sides, *refs):
    base_refs, refs = refs[: owners * sides], refs[owners * sides :]
    low_refs, refs = refs[: 2 * owners], refs[2 * owners :]
    marks_ref, expand_refs, out_refs = refs[0], refs[1 : owners + 1], refs[owners + 1 :]
    rows = base_refs[0].shape[0]
    spreads = []
    for n in range(owners):
        low = (low_refs[2 * n][...] + low_refs[2 * n + 1][...]).astype(BF)
        pick = one_hot(low.shape[0], marks_ref[MINE + n : MINE + n + 1, :rows])
        spreads.append(dot_first(pick, low).astype(BF))
    spread = jnp.concatenate(spreads, axis=1)
    own_rows, width = out_refs[0].shape
    side = width // sides
    block = min(1024, side)
    for first in range(0, width, block):
        here = pl.ds(first, block)
        inside = pl.ds(first % side, block)
        expand = jnp.concatenate([ref[:, here] for ref in expand_refs], axis=0)
        total = dot(spread, expand)
        for base_ref in base_refs[first // side :: sides]:
            total += base_ref[:, inside].astype(F32)
        for b, out_ref in enumerate(out_refs):
            out_ref[:, here] = total[b * own_rows : (b + 1) * own_rows].astype(BF)


def add_delta(bases, lows, marks, expands, count):
    owners = len(expands)
    rows = bases[0].shape[0]
    depth, width = expands[0].shape
    return pl.pallas_call(
        functools.partial(add_kernel, owners, len(bases) // owners),
        out_shape=(jax.ShapeDtypeStruct((rows // count, width), BF),) * count,
        compiler_params=params(32),
        cost_estimate=cost(
            2 * rows * depth * owners * width, width * (6 * rows + 2 * depth) * owners
        ),
    )(*bases, *lows, marks, *expands)


def tied(first, *others):
    return lax.optimization_barrier((first, *others))


def per_device(
    tokens,
    gate_weight,
    up_weight,
    down_weight,
    shrink_gu,
    expand_gu,
    shrink_down,
    expand_down,
    variant_ids,
    variant_slot,
):
    ways = Ways()
    shards, order = ways.shards, ways.order
    me = lax.axis_index("ff").astype(I32)
    core = lax.axis_index("var").astype(I32)
    groups = lax.axis_size("groups")
    own_rows, width = tokens.shape
    rows = own_rows * shards
    slots = shrink_gu.shape[0]
    variants = variant_slot.shape[0]
    rank = shrink_down.shape[1]
    half_rank = expand_gu.shape[2]
    half = gate_weight.shape[1] // 2
    most = min(slots * MOST, rows)
    here = core.reshape(1)
    there = 1 - here
    at_here = 2 * order + core
    split = ways.fast if ways.direct else 1
    swap = lambda a: lax.ppermute(a, "var", [(0, 1), (1, 0)])

    near = expand_gu.reshape(slots * 2 * half_rank, -1)
    token_parts, far = ways.gather(tokens, swap(near))
    shrink_in = shrink_gu.reshape(slots * 2 * rank, width)
    marks, mask_in, slot_mask, facts, token_parts[0], shrink_in = tables(
        ways,
        me.reshape(1),
        variant_ids,
        variant_slot.reshape(1, variants),
        token_parts[0],
        shrink_in,
        slots,
        rank,
    )
    most_facts = facts
    for turn in range(1, 1 if ways.direct else groups):
        pairs = [(g, (g + turn) % groups) for g in range(groups)]
        most_facts = jnp.maximum(most_facts, lax.ppermute(facts, "groups", pairs))
    kinds = jnp.arange(2, dtype=I32)
    in_cols = jnp.arange(slots * 2 * rank, dtype=I32)
    rank_at = in_cols % rank
    kind_at = in_cols // rank % 2
    row_at = in_cols // (2 * rank) * (2 * half_rank) + kind_at * half_rank + rank_at % half_rank
    depth = slots * 2 * half_rank
    both_cols = jnp.arange(2 * depth, dtype=I32)
    wanted = row_at + jnp.where(rank_at // half_rank == core, 0, depth)
    hit = wanted[:, None] == both_cols[None, :]
    cols = (hit[None] & (kind_at[None, :] == kinds[:, None])[:, :, None]).astype(BF)

    x, low_own = low_in_pairs(token_parts, shrink_in, mask_in)
    low_got = swap(low_own)

    def partial_sums(cap, room):
        made = expand_rows(at_here, low_own, low_got, marks, cols, near, far, cap, split)
        held, *made = tied(x, *made)
        expand = expand_down.reshape(slots * rank, width)
        if split == 2:
            beside = lax.ppermute(made[1], "ff", ways.back(0, 1))
            base_there = base_half(there, held, gate_weight, up_weight, half, BF)
            base_there, beside, expand = tied(base_there, beside, expand)
            made = pack(facts, made[0], beside, cap, room, ways.slow)
            held, *made = tied(held, *made)
            delta = ways.slow_steps(made)
            expand_beside = lax.ppermute(expand, "ff", ways.back(0, 1))
        else:
            base_there = base_half(there, held, gate_weight, up_weight, half, BF)
            delta = ways.spread(made[0].reshape(shards, 2 * cap, half))
            delta = [delta.reshape(2 * shards * cap, half)]
        base_got = swap(base_there)
        base_own = base_half(here, held, gate_weight, up_weight, half, F32)
        hidden, *sent = hidden_half(
            base_own, base_got, delta, marks, cap, room, shards, split
        )
        hidden_far = swap(hidden)
        shrink = shrink_down.reshape(slots * rank, -1)
        side = width // 2
        down = functools.partial(down_base, here, hidden, hidden_far, down_weight)
        if split == 2:
            beside = lax.ppermute(sent[1], "ff", ways.back(0, 1))
            left, left_sent = down(0, side, (F32, BF))
            left_sent, beside, expand_beside = tied(left_sent, beside, expand_beside)
            left_beside = lax.ppermute(left_sent, "ff", ways.back(0, 1))
            sent = relay(sent[0], beside, ways.slow)
            hidden, *sent = tied(hidden, *sent)
            down = functools.partial(down_base, here, hidden, hidden_far, down_weight)
            got = ways.slow_steps(sent)
            right, right_sent = down(side, side, (F32, BF))
            right_sent, left_beside, *got = tied(right_sent, left_beside, *got)
            right_beside = lax.ppermute(right_sent, "ff", ways.back(0, 1))
            bases = [left, right, left_beside, right_beside]
        else:
            bases = [down(0, side, (F32,))[0], down(side, side, (F32,))[0]]
            got = [ways.spread(sent[0].reshape(shards, cap, half)).reshape(shards * cap, half)]
        bases[1], *got = tied(bases[1], *got)
        out_own = low_out_pairs(at_here, marks, slot_mask, shrink, got, cap)
        out_got = swap(out_own)
        if split == 1:
            parts = add_delta(bases, [out_own, out_got], marks, [expand], shards)
            return list(ways.spread(jnp.stack(parts)))
        out_beside = lax.ppermute(out_own, "ff", ways.back(0, 1))
        across = [
            (2 * f + v, 2 * g + 1 - v) for f, g in ways.back(0, 1) for v in range(2)
        ]
        out_across = lax.ppermute(out_own, ("ff", "var"), across)
        parts = add_delta(
            bases,
            [out_own, out_got, out_beside, out_across],
            marks,
            [expand, expand_beside],
            ways.slow,
        )
        return ways.slow_steps(parts)

    most_room = 2 * most if split == 2 else most
    if most <= USUAL:
        parts = partial_sums(most, most_room)
    else:
        parts = lax.cond(
            most_facts[0] == 0,
            lambda: partial_sums(USUAL, USUAL_PAIR if split == 2 else USUAL),
            lambda: partial_sums(most, most_room),
        )
    return sum(part.astype(F32) for part in parts).astype(BF)


def solution(mesh):
    placed = (
        P(("groups", "ff"), "var"),
        P("var", "ff"),
        P("var", "ff"),
        P("ff", "var"),
        P(("groups", "ff"), None, "var"),
        P(("groups", "ff"), None, "var", None),
        P(("groups", "ff"), None, None),
        P(("groups", "ff"), None, "var"),
        P("groups", None),
        P("groups"),
    )
    return jax.shard_map(
        per_device,
        mesh=mesh,
        in_specs=placed,
        out_specs=P(("groups", "ff"), "var"),
        check_vma=False,
    )
```

```python
import functools

import jax
import jax.numpy as jnp
from jax import lax
from jax.experimental import pallas as pl
from jax.experimental.pallas import tpu as pltpu
from jax.sharding import PartitionSpec as P

MOST = 8
DIRECT = 8
MINE, NEXT, STEP, PLACE, ARRIVE, PACKED = range(6)
USUAL = 16
USUAL_PAIR = 24
BF = jnp.bfloat16
F32 = jnp.float32
I32 = jnp.int32
MIB = 1024 * 1024


def dot(a, b):
    return jnp.dot(a, b, preferred_element_type=F32)


def dot_last(a, b):
    return lax.dot_general(a, b, (((1,), (1,)), ((), ())), preferred_element_type=F32)


def params(mib):
    return pltpu.CompilerParams(vmem_limit_bytes=int(mib * MIB))


def cost(flops, moved):
    return pl.CostEstimate(flops=flops, bytes_accessed=moved, transcendentals=0)


SCALARS = pl.BlockSpec(memory_space=pltpu.SMEM)
WHOLE = pl.BlockSpec(memory_space=pltpu.VMEM)
FAR = pl.BlockSpec(memory_space=pltpu.HBM)


def fixed(array):
    zeros = (0,) * array.ndim
    return pl.BlockSpec(array.shape, lambda *_: zeros)


def one_hot(count, cell):
    lines = lax.broadcasted_iota(I32, (count, cell.shape[1]), 0)
    return (lines == cell).astype(F32).astype(BF)


def dot_first(a, b):
    return lax.dot_general(a, b, (((0,), (0,)), ((), ())), preferred_element_type=F32)


class Ways:
    def __init__(self):
        self.shards = lax.axis_size("ff")
        self.fast = 2 if self.shards % 2 == 0 else 1
        self.slow = self.shards // self.fast
        self.direct = self.shards <= DIRECT
        me = lax.axis_index("ff").astype(I32)
        steps = jnp.arange(self.shards, dtype=I32)
        if self.direct:
            slow = (me // self.fast - steps % self.slow) % self.slow
            fast = (me % self.fast - steps // self.slow) % self.fast
            self.order = slow * self.fast + fast
        else:
            self.order = steps

    def back(self, a, c):
        S, F = self.slow, self.fast
        return [(s * F + f, (s - a) % S * F + (f - c) % F) for s in range(S) for f in range(F)]

    def gather(self, block, other):
        if not self.direct:
            return list(lax.all_gather(block, "ff")), other
        got = [block] + [
            lax.ppermute(block, "ff", self.back(-a, 0)) for a in range(1, self.slow)
        ]
        other, got[1] = tied(other, got[1])
        for c in range(1, self.fast):
            got += [lax.ppermute(part, "ff", self.back(0, -c)) for part in got[: self.slow]]
        return got, other

    def spread(self, blocks):
        return lax.all_to_all(blocks, "ff", 0, 0, tiled=True)

    def slow_steps(self, blocks):
        got = [blocks[0]] + [None] * (self.slow - 1)
        for a in range(1, self.slow):
            got[(-a) % self.slow] = lax.ppermute(blocks[a], "ff", self.back(a, 0))
        return got


def tables_kernel(
    ways,
    slots,
    order_ref,
    me_ref,
    at_ref,
    slot_ref,
    ids_ref,
    x_ref,
    shrink_ref,
    expand_ref,
    marks_ref,
    in_ref,
    out_ref,
    facts_ref,
    kept_ref,
    held_ref,
    near_ref,
    sems,
):
    shards = order_ref.shape[0]
    half = near_ref.shape[1] // shards
    copies = [
        pltpu.make_async_copy(x_ref, kept_ref, sems.at[0]),
        pltpu.make_async_copy(shrink_ref, held_ref, sems.at[1]),
    ]
    for b in range(shards):
        columns = pl.ds(pl.multiple_of(at_ref[b] * half, half), half)
        put = near_ref.at[:, pl.ds(b * half, half)]
        copies.append(pltpu.make_async_copy(expand_ref.at[:, columns], put, sems.at[2 + b]))
    for copy in copies:
        copy.start()
    rows, variants = ids_ref.shape[1], slot_ref.shape[0]
    own_rows = rows // shards
    me = me_ref[0].astype(F32)
    order = [order_ref[b].astype(F32) for b in range(shards)]
    beside_me = order[ways.slow % shards]
    count = lambda shape, axis: lax.broadcasted_iota(I32, shape, axis).astype(F32)
    across = lambda a: jnp.sum(a, axis=1, keepdims=True)
    along = lambda a: jnp.sum(a, axis=0, keepdims=True)
    line, lane = count((rows, rows), 0), count((rows, rows), 1)
    diagonal = line == lane
    at_along, at_down = count((1, rows), 1), count((rows, 1), 0)
    for b in range(shards):
        shift = (order[b] - b) * own_rows
        low, high = b * own_rows, (b + 1) * own_rows
        at_along = jnp.where(
            (lane[:1] >= low) & (lane[:1] < high), lane[:1] + shift, at_along
        )
        at_down = jnp.where(
            (line[:, :1] >= low) & (line[:, :1] < high), line[:, :1] + shift, at_down
        )
    ids = across(jnp.where(lane == at_down, ids_ref[...].astype(F32), 0.0))
    ids = along(jnp.where(diagonal, ids, 0.0))
    slot = jnp.zeros_like(ids)
    for v in range(variants):
        slot = jnp.where(ids == float(v), slot_ref[v].astype(F32), slot)
    slot_down = across(jnp.where(diagonal, slot, 0.0))
    owner_of = lambda a: sum((a >= float(o * slots)).astype(F32) for o in range(1, shards))
    owner, owner_down = owner_of(slot), owner_of(slot_down)
    same = owner_down == owner
    place = along((same & (at_down < at_along)).astype(F32))
    packed, pair = place, jnp.zeros_like(place)
    step = arrive = jnp.zeros_like(place)
    paired = ways.direct and ways.fast == 2
    if paired:
        odd = sum((owner == float(o)).astype(F32) for o in range(1, shards, 2))
        beside = along((owner_down == owner + 1.0 - 2.0 * odd).astype(F32))
        pair = along(same.astype(F32)) + beside
    for b in range(shards):
        hit = owner == order[b]
        step = jnp.where(hit, float(b), step)
        arrive = jnp.where(hit, float(b % ways.slow if paired else b), arrive)
        if paired and b >= ways.slow:
            packed = jnp.where(hit, place + beside, packed)
    crowded = (place >= float(USUAL)) | (pair > float(USUAL_PAIR))
    facts_ref[0] = jnp.max(crowded.astype(F32)).astype(I32)
    facts_ref[1] = jnp.sum((owner == me).astype(F32)).astype(I32)
    facts_ref[2] = jnp.sum((owner == beside_me).astype(F32)).astype(I32)
    lines = {
        MINE: jnp.where(owner == me, place, -1.0),
        NEXT: jnp.where(owner == beside_me, place, -1.0),
        STEP: step,
        PLACE: place,
        ARRIVE: arrive,
        PACKED: packed,
    }
    for n, values in lines.items():
        marks_ref[n : n + 1] = values.astype(I32)
    local = slot_down - me * slots
    for ref in (in_ref, out_ref):
        wide = ref.shape[1] // slots
        column = count(ref.shape, 1)
        inside = (column >= local * wide) & (column < (local + 1.0) * wide)
        ref[...] = inside.astype(F32).astype(ref.dtype)
    for copy in copies:
        copy.wait()


def tables(ways, me, at, ids, variant_slot, x, shrink, expand, slots, rank):
    rows = ids.shape[1]
    shards = at.shape[0]
    depth, width = expand.shape
    return pl.pallas_call(
        functools.partial(tables_kernel, ways, slots),
        out_shape=(
            jax.ShapeDtypeStruct((8, rows), I32),
            jax.ShapeDtypeStruct((rows, slots * 2 * rank), F32),
            jax.ShapeDtypeStruct((rows, slots * rank), BF),
            jax.ShapeDtypeStruct((3,), I32),
            jax.ShapeDtypeStruct(x.shape, BF),
            jax.ShapeDtypeStruct(shrink.shape, BF),
            jax.ShapeDtypeStruct((depth, width // 2), BF),
        ),
        in_specs=[SCALARS] * 4 + [WHOLE] + [FAR] * 3,
        out_specs=(WHOLE, WHOLE, WHOLE, SCALARS, WHOLE, WHOLE, WHOLE),
        scratch_shapes=[pltpu.SemaphoreType.DMA((2 + shards,))],
        compiler_params=params(52),
        cost_estimate=cost(0, 4 * x.size + 4 * shrink.size + 2 * expand.size),
    )(ways.order, me, at, variant_slot, ids, x, shrink, expand)


def low_in_kernel(count, shrink_ref, mask_ref, *refs):
    parts, x_ref, out_ref = refs[:count], refs[count], refs[count + 1]
    x = jnp.concatenate([part[...].astype(F32) for part in parts], axis=0).astype(BF)
    x_ref[...] = x

    @pl.when(pl.program_id(0) == 0)
    def _():
        out_ref[...] = jnp.zeros_like(out_ref)

    out_ref[...] += jnp.where(mask_ref[...] > 0, dot_last(x, shrink_ref[...]), 0.0)


def low_in_pairs(parts, shrink, mask):
    count = len(parts)
    own_rows, width = parts[0].shape
    rows, block = count * own_rows, min(1024, width)
    return pl.pallas_call(
        lambda *refs: low_in_kernel(count, *refs),
        out_shape=(
            jax.ShapeDtypeStruct((rows, width), BF),
            jax.ShapeDtypeStruct(mask.shape, F32),
        ),
        grid=(width // block,),
        in_specs=[pl.BlockSpec((shrink.shape[0], block), lambda n: (0, n)), fixed(mask)]
        + [pl.BlockSpec((own_rows, block), lambda n: (0, n))] * count,
        out_specs=(pl.BlockSpec((rows, block), lambda n: (0, n)), fixed(mask)),
        compiler_params=params(16),
        cost_estimate=cost(2 * rows * width * shrink.shape[0], 2 * shrink.size + 4 * rows * width),
    )(shrink, mask, *parts)


def expand_kernel(
    cap, fast, at_ref, own_ref, got_ref, marks_ref, cols_ref, near_ref, far_ref, *out_refs
):
    low = (own_ref[...] + got_ref[...]).astype(BF)
    picked = dot(one_hot(cap, marks_ref[MINE : MINE + 1]), low).astype(BF)
    lhs = jnp.concatenate([dot(picked, cols_ref[kind]) for kind in range(2)], axis=0).astype(BF)
    tall = lhs.shape[0]
    half = out_refs[0].shape[1]
    count = at_ref.shape[0]
    for b in range(count):
        here = pl.ds(b * half, half)
        columns = pl.ds(pl.multiple_of(at_ref[b] * half, half), half)
        both = jnp.concatenate([near_ref[:, here], far_ref[:, columns]], axis=0)
        at = b % (count // fast)
        out_refs[b * fast // count][pl.ds(at * tall, tall)] = dot(lhs, both).astype(BF)


def expand_rows(at, own, got, marks, cols, near, far, cap, fast):
    depth, width = far.shape
    shards = at.shape[0]
    half = width // (2 * shards)
    out = jax.ShapeDtypeStruct((2 * cap * shards // fast, half), BF)
    return pl.pallas_call(
        functools.partial(expand_kernel, cap, fast),
        out_shape=(out,) * fast,
        in_specs=[SCALARS] + [WHOLE] * 6,
        compiler_params=params(16),
        cost_estimate=cost(8 * cap * depth * width, 4 * (depth + cap) * width),
    )(at, own, got, marks, cols, near, far)


def base_kernel(side_ref, x_ref, gate_ref, up_ref, out_ref, held, sums, sems):
    half = held.shape[2]
    chunks = sems.shape[1]
    depth = held.shape[1] // chunks
    columns = pl.ds(pl.multiple_of(side_ref[0] * half, half), half)
    copies = []
    for c in range(chunks):
        here = pl.ds(c * depth, depth)
        for kind, weight in enumerate((gate_ref, up_ref)):
            copy = pltpu.make_async_copy(
                weight.at[here, columns], held.at[kind, here], sems.at[kind, c]
            )
            copy.start()
            copies.append((kind, here, copy))
    for kind, here, copy in copies:
        copy.wait()
        part = dot(x_ref[:, here], held[kind, here])
        sums[kind] = part if here.start == 0 else sums[kind] + part
    out_ref[...] = sums[...].astype(out_ref.dtype)


def base_half(side, x, gate_weight, up_weight, half, kind):
    rows, width = x.shape
    chunks = max(width // 512, 1)
    return pl.pallas_call(
        base_kernel,
        out_shape=jax.ShapeDtypeStruct((2, rows, half), kind),
        in_specs=[SCALARS, WHOLE, FAR, FAR],
        out_specs=WHOLE,
        scratch_shapes=[
            pltpu.VMEM((2, width, half), BF),
            pltpu.VMEM((2, rows, half), F32),
            pltpu.SemaphoreType.DMA((2, chunks)),
        ],
        compiler_params=params(48),
        cost_estimate=cost(4 * rows * width * half, 4 * width * half + 2 * rows * width),
    )(side, x, gate_weight, up_weight)


def hidden_kernel(cap, room, count, own_ref, got_ref, marks_ref, *refs):
    parts, hid_ref, out_refs = refs[:count], refs[count], refs[count + 1 :]
    half = hid_ref.shape[1]
    cells = sum(part.shape[0] for part in parts)
    first_cell = marks_ref[ARRIVE : ARRIVE + 1] * (2 * room) + marks_ref[PACKED : PACKED + 1]
    places = [one_hot(cells, first_cell + kind * room) for kind in range(2)]
    tall = out_refs[0].shape[0]
    leave = marks_ref[STEP : STEP + 1] * cap + marks_ref[PLACE : PLACE + 1]
    send = one_hot(tall * len(out_refs), leave)
    block = min(256, half)
    for first in range(0, half, block):
        here = pl.ds(first, block)
        delta = jnp.concatenate([part[:, here] for part in parts], axis=0)
        gate, up = [
            own_ref[kind, :, here]
            + got_ref[kind, :, here].astype(F32)
            + dot_first(places[kind], delta)
            for kind in range(2)
        ]
        hidden = (gate / (1.0 + jnp.exp(-gate)) * up).astype(BF)
        hid_ref[:, here] = hidden
        sent = dot(send, hidden).astype(BF)
        for n, out_ref in enumerate(out_refs):
            out_ref[:, here] = sent[n * tall : (n + 1) * tall]


def hidden_half(own, got, parts, marks, cap, room, shards, count):
    rows, half = own.shape[1:]
    cells = shards * cap
    return pl.pallas_call(
        functools.partial(hidden_kernel, cap, room, len(parts)),
        out_shape=(jax.ShapeDtypeStruct((rows, half), BF),)
        + (jax.ShapeDtypeStruct((cells // count, half), BF),) * count,
        compiler_params=params(40),
        cost_estimate=cost(10 * half * cells * rows, 2 * half * (6 * rows + 3 * cells)),
    )(own, got, marks, *parts)


def pack_kernel(cap, facts_ref, own_ref, got_ref, *out_refs):
    column = lax.broadcasted_iota(I32, (1, 4 * cap), 1)
    from_got = column >= 2 * cap
    column = column - jnp.where(from_got, 2 * cap, 0)
    kind = jnp.where(column >= cap, 1, 0)
    row = column - kind * cap
    live = row < jnp.where(from_got, facts_ref[2], facts_ref[1])
    row = row + jnp.where(from_got, facts_ref[1], 0)
    room = out_refs[0].shape[0] // 2
    packing = one_hot(2 * room, jnp.where(live, row + kind * room, -1))
    for a, out_ref in enumerate(out_refs):
        here = pl.ds(a * 2 * cap, 2 * cap)
        both = jnp.concatenate([own_ref[here], got_ref[here]], axis=0)
        out_ref[...] = dot(packing, both).astype(BF)


def pack(facts, own, got, cap, room, count):
    half = own.shape[1]
    return pl.pallas_call(
        functools.partial(pack_kernel, cap),
        out_shape=(jax.ShapeDtypeStruct((2 * room, half), BF),) * count,
        in_specs=[SCALARS, WHOLE, WHOLE],
        compiler_params=params(16),
        cost_estimate=cost(0, 8 * own.size),
    )(facts, own, got)


def relay_kernel(own_ref, got_ref, *out_refs):
    cap = out_refs[0].shape[0] // 2
    for a, out_ref in enumerate(out_refs):
        here = pl.ds(a * cap, cap)
        out_ref[:cap] = own_ref[here]
        out_ref[cap:] = got_ref[here]


def relay(own, got, count):
    tall, half = own.shape
    return pl.pallas_call(
        relay_kernel,
        out_shape=(jax.ShapeDtypeStruct((2 * tall // count, half), BF),) * count,
        compiler_params=params(16),
        cost_estimate=cost(0, 8 * tall * half),
    )(own, got)


def down_kernel(start, core_ref, near_ref, far_ref, weight_ref, *refs):
    out_refs, held, sems = refs[:-2], refs[-2], refs[-1]
    chunks = sems.shape[1]
    half, width = held.shape[1:]
    block = width // chunks
    tall = out_refs[0].shape[0]
    copies = []
    for c in range(chunks):
        here = pl.ds(c * block, block)
        for side, at in enumerate((core_ref[0], 1 - core_ref[0])):
            lines = pl.ds(pl.multiple_of(at * half, half), half)
            copy = pltpu.make_async_copy(
                weight_ref.at[lines, pl.ds(start + c * block, block)],
                held.at[side, :, here],
                sems.at[side, c],
            )
            copy.start()
            copies.append(copy)
    for c in range(chunks):
        here = pl.ds(c * block, block)
        copies[2 * c].wait()
        copies[2 * c + 1].wait()
        total = dot(near_ref[...], held[0, :, here]) + dot(far_ref[...], held[1, :, here])
        for n, out_ref in enumerate(out_refs):
            out_ref[:, here] = total[n * tall : (n + 1) * tall].astype(out_ref.dtype)


def down_base(core, near, far, weight, start, width, kinds):
    rows, half = near.shape
    chunks = max(width // 512, 1)
    outs = tuple(jax.ShapeDtypeStruct((rows // len(kinds), width), kind) for kind in kinds)
    return pl.pallas_call(
        functools.partial(down_kernel, start),
        out_shape=outs,
        in_specs=[SCALARS, WHOLE, WHOLE, FAR],
        out_specs=(WHOLE,) * len(outs),
        scratch_shapes=[
            pltpu.VMEM((2, half, width), BF),
            pltpu.SemaphoreType.DMA((2, chunks)),
        ],
        compiler_params=params(48),
        cost_estimate=cost(4 * rows * half * width, 4 * half * width + 4 * rows * width),
    )(core, near, far, weight)


def low_out_kernel(cap, count, at_ref, marks_ref, slot_ref, shrink_ref, *refs):
    parts, out_ref = refs[:count], refs[count]
    half = parts[0].shape[1]
    blocks = [part[r : r + cap] for r in range(0, parts[0].shape[0], cap) for part in parts]
    pairs = jnp.zeros(out_ref.shape, F32)
    for b, block in enumerate(blocks):
        columns = pl.ds(pl.multiple_of(at_ref[b] * half, half), half)
        pairs += dot_last(block, shrink_ref[:, columns])
    mask = dot(one_hot(cap, marks_ref[MINE : MINE + 1]), slot_ref[...])
    out_ref[...] = jnp.where(mask > 0.5, pairs, 0.0)


def low_out_pairs(at, marks, slot_mask, shrink, parts, cap):
    count = len(parts)
    half = parts[0].shape[1]
    depth = shrink.shape[0]
    return pl.pallas_call(
        functools.partial(low_out_kernel, cap, count),
        out_shape=jax.ShapeDtypeStruct((cap, depth), F32),
        in_specs=[SCALARS] + [WHOLE] * (3 + count),
        compiler_params=params(16),
        cost_estimate=cost(
            2 * cap * depth * at.shape[0] * half, 2 * at.shape[0] * half * (depth + cap)
        ),
    )(at, marks, slot_mask, shrink, *parts)


def add_kernel(owners, sides, *refs):
    base_refs, refs = refs[: owners * sides], refs[owners * sides :]
    low_refs, refs = refs[: 2 * owners], refs[2 * owners :]
    marks_ref, expand_refs, out_refs = refs[0], refs[1 : owners + 1], refs[owners + 1 :]
    rows = base_refs[0].shape[0]
    spreads = []
    for n in range(owners):
        low = (low_refs[2 * n][...] + low_refs[2 * n + 1][...]).astype(BF)
        pick = one_hot(low.shape[0], marks_ref[MINE + n : MINE + n + 1, :rows])
        spreads.append(dot_first(pick, low).astype(BF))
    spread = jnp.concatenate(spreads, axis=1)
    own_rows, width = out_refs[0].shape
    side = width // sides
    block = min(1024, side)
    for first in range(0, width, block):
        here = pl.ds(first, block)
        inside = pl.ds(first % side, block)
        expand = jnp.concatenate([ref[:, here] for ref in expand_refs], axis=0)
        total = dot(spread, expand)
        for base_ref in base_refs[first // side :: sides]:
            total += base_ref[:, inside].astype(F32)
        for b, out_ref in enumerate(out_refs):
            out_ref[:, here] = total[b * own_rows : (b + 1) * own_rows].astype(BF)


def add_delta(bases, lows, marks, expands, count):
    owners = len(expands)
    rows = bases[0].shape[0]
    depth, width = expands[0].shape
    return pl.pallas_call(
        functools.partial(add_kernel, owners, len(bases) // owners),
        out_shape=(jax.ShapeDtypeStruct((rows // count, width), BF),) * count,
        compiler_params=params(32),
        cost_estimate=cost(
            2 * rows * depth * owners * width, width * (6 * rows + 2 * depth) * owners
        ),
    )(*bases, *lows, marks, *expands)


def tied(first, *others):
    return lax.optimization_barrier((first, *others))


def per_device(
    tokens,
    gate_weight,
    up_weight,
    down_weight,
    shrink_gu,
    expand_gu,
    shrink_down,
    expand_down,
    variant_ids,
    variant_slot,
):
    ways = Ways()
    shards, order = ways.shards, ways.order
    me = lax.axis_index("ff").astype(I32)
    core = lax.axis_index("var").astype(I32)
    groups = lax.axis_size("groups")
    own_rows, width = tokens.shape
    rows = own_rows * shards
    slots = shrink_gu.shape[0]
    rank = shrink_down.shape[1]
    half_rank = expand_gu.shape[2]
    half = gate_weight.shape[1] // 2
    most = min(slots * MOST, rows)
    here = core.reshape(1)
    there = 1 - here
    at_here = 2 * order + core
    split = ways.fast if ways.direct else 1
    swap = lambda a: lax.ppermute(a, "var", [(0, 1), (1, 0)])

    near = expand_gu.reshape(slots * 2 * half_rank, -1)
    token_parts, far = ways.gather(tokens, swap(near))
    shrink_in = shrink_gu.reshape(slots * 2 * rank, width)
    marks, mask_in, slot_mask, facts, token_parts[0], shrink_in, near = tables(
        ways,
        me.reshape(1),
        at_here,
        variant_ids.reshape(1, rows),
        variant_slot,
        token_parts[0],
        shrink_in,
        near,
        slots,
        rank,
    )
    most_facts = facts
    for turn in range(1, 1 if ways.direct else groups):
        pairs = [(g, (g + turn) % groups) for g in range(groups)]
        most_facts = jnp.maximum(most_facts, lax.ppermute(facts, "groups", pairs))
    kinds = jnp.arange(2, dtype=I32)
    in_cols = jnp.arange(slots * 2 * rank, dtype=I32)
    rank_at = in_cols % rank
    kind_at = in_cols // rank % 2
    row_at = in_cols // (2 * rank) * (2 * half_rank) + kind_at * half_rank + rank_at % half_rank
    depth = slots * 2 * half_rank
    both_cols = jnp.arange(2 * depth, dtype=I32)
    wanted = row_at + jnp.where(rank_at // half_rank == core, 0, depth)
    hit = wanted[:, None] == both_cols[None, :]
    cols = (hit[None] & (kind_at[None, :] == kinds[:, None])[:, :, None]).astype(BF)

    x, low_own = low_in_pairs(token_parts, shrink_in, mask_in)
    low_got = swap(low_own)

    def partial_sums(cap, room):
        made = expand_rows(at_here, low_own, low_got, marks, cols, near, far, cap, split)
        held, *made = tied(x, *made)
        expand = expand_down.reshape(slots * rank, width)
        if split == 2:
            beside = lax.ppermute(made[1], "ff", ways.back(0, 1))
            base_there = base_half(there, held, gate_weight, up_weight, half, BF)
            base_there, beside, expand = tied(base_there, beside, expand)
            made = pack(facts, made[0], beside, cap, room, ways.slow)
            held, *made = tied(held, *made)
            delta = ways.slow_steps(made)
            expand_beside = lax.ppermute(expand, "ff", ways.back(0, 1))
        else:
            base_there = base_half(there, held, gate_weight, up_weight, half, BF)
            delta = ways.spread(made[0].reshape(shards, 2 * cap, half))
            delta = [delta.reshape(2 * shards * cap, half)]
        base_got = swap(base_there)
        base_own = base_half(here, held, gate_weight, up_weight, half, F32)
        hidden, *sent = hidden_half(
            base_own, base_got, delta, marks, cap, room, shards, split
        )
        hidden_far = swap(hidden)
        shrink = shrink_down.reshape(slots * rank, -1)
        side = width // 2
        down = functools.partial(down_base, here, hidden, hidden_far, down_weight)
        if split == 2:
            beside = lax.ppermute(sent[1], "ff", ways.back(0, 1))
            left, left_sent = down(0, side, (F32, BF))
            left_sent, beside, expand_beside = tied(left_sent, beside, expand_beside)
            left_beside = lax.ppermute(left_sent, "ff", ways.back(0, 1))
            sent = relay(sent[0], beside, ways.slow)
            hidden, *sent = tied(hidden, *sent)
            down = functools.partial(down_base, here, hidden, hidden_far, down_weight)
            got = ways.slow_steps(sent)
            right, right_sent = down(side, side, (F32, BF))
            right_sent, left_beside, *got = tied(right_sent, left_beside, *got)
            right_beside = lax.ppermute(right_sent, "ff", ways.back(0, 1))
            bases = [left, right, left_beside, right_beside]
        else:
            bases = [down(0, side, (F32,))[0], down(side, side, (F32,))[0]]
            got = [ways.spread(sent[0].reshape(shards, cap, half)).reshape(shards * cap, half)]
        bases[1], *got = tied(bases[1], *got)
        out_own = low_out_pairs(at_here, marks, slot_mask, shrink, got, cap)
        out_got = swap(out_own)
        if split == 1:
            parts = add_delta(bases, [out_own, out_got], marks, [expand], shards)
            return list(ways.spread(jnp.stack(parts)))
        out_beside = lax.ppermute(out_own, "ff", ways.back(0, 1))
        across = [
            (2 * f + v, 2 * g + 1 - v) for f, g in ways.back(0, 1) for v in range(2)
        ]
        out_across = lax.ppermute(out_own, ("ff", "var"), across)
        parts = add_delta(
            bases,
            [out_own, out_got, out_beside, out_across],
            marks,
            [expand, expand_beside],
            ways.slow,
        )
        return ways.slow_steps(parts)

    most_room = 2 * most if split == 2 else most
    if most <= USUAL:
        parts = partial_sums(most, most_room)
    else:
        parts = lax.cond(
            most_facts[0] == 0,
            lambda: partial_sums(USUAL, USUAL_PAIR if split == 2 else USUAL),
            lambda: partial_sums(most, most_room),
        )
    return sum(part.astype(F32) for part in parts).astype(BF)


def solution(mesh):
    placed = (
        P(("groups", "ff"), "var"),
        P("var", "ff"),
        P("var", "ff"),
        P("ff", "var"),
        P(("groups", "ff"), None, "var"),
        P(("groups", "ff"), None, "var", None),
        P(("groups", "ff"), None, None),
        P(("groups", "ff"), None, "var"),
        P("groups", None),
        P("groups"),
    )
    return jax.shard_map(
        per_device,
        mesh=mesh,
        in_specs=placed,
        out_specs=P(("groups", "ff"), "var"),
        check_vma=False,
    )
```

```python
import functools

import jax
import jax.numpy as jnp
from jax import lax
from jax.experimental import pallas as pl
from jax.experimental.pallas import tpu as pltpu
from jax.sharding import PartitionSpec as P

MOST = 8
DIRECT = 8
MINE, NEXT, STEP, PLACE, ARRIVE, PACKED = range(6)
USUAL = 16
USUAL_PAIR = 24
BF = jnp.bfloat16
F32 = jnp.float32
I32 = jnp.int32
MIB = 1024 * 1024


def dot(a, b):
    return jnp.dot(a, b, preferred_element_type=F32)


def dot_last(a, b):
    return lax.dot_general(a, b, (((1,), (1,)), ((), ())), preferred_element_type=F32)


def params(mib):
    return pltpu.CompilerParams(vmem_limit_bytes=int(mib * MIB))


def cost(flops, moved):
    return pl.CostEstimate(flops=flops, bytes_accessed=moved, transcendentals=0)


SCALARS = pl.BlockSpec(memory_space=pltpu.SMEM)
WHOLE = pl.BlockSpec(memory_space=pltpu.VMEM)
FAR = pl.BlockSpec(memory_space=pltpu.HBM)


def fixed(array):
    zeros = (0,) * array.ndim
    return pl.BlockSpec(array.shape, lambda *_: zeros)


def one_hot(count, cell):
    lines = lax.broadcasted_iota(I32, (count, cell.shape[1]), 0)
    return (lines == cell).astype(F32).astype(BF)


def dot_first(a, b):
    return lax.dot_general(a, b, (((0,), (0,)), ((), ())), preferred_element_type=F32)


class Ways:
    def __init__(self):
        self.shards = lax.axis_size("ff")
        self.fast = 2 if self.shards % 2 == 0 else 1
        self.slow = self.shards // self.fast
        self.direct = self.shards <= DIRECT
        me = lax.axis_index("ff").astype(I32)
        steps = jnp.arange(self.shards, dtype=I32)
        if self.direct:
            slow = (me // self.fast - steps % self.slow) % self.slow
            fast = (me % self.fast - steps // self.slow) % self.fast
            self.order = slow * self.fast + fast
        else:
            self.order = steps

    def back(self, a, c):
        S, F = self.slow, self.fast
        return [(s * F + f, (s - a) % S * F + (f - c) % F) for s in range(S) for f in range(F)]

    def gather(self, block, other):
        if not self.direct:
            return list(lax.all_gather(block, "ff")), other
        got = [block] + [
            lax.ppermute(block, "ff", self.back(-a, 0)) for a in range(1, self.slow)
        ]
        other, got[1] = tied(other, got[1])
        for c in range(1, self.fast):
            got += [lax.ppermute(part, "ff", self.back(0, -c)) for part in got[: self.slow]]
        return got, other

    def spread(self, blocks):
        return lax.all_to_all(blocks, "ff", 0, 0, tiled=True)

    def slow_steps(self, blocks):
        got = [blocks[0]] + [None] * (self.slow - 1)
        for a in range(1, self.slow):
            got[(-a) % self.slow] = lax.ppermute(blocks[a], "ff", self.back(a, 0))
        return got


def tables_kernel(
    ways,
    slots,
    order_ref,
    me_ref,
    at_ref,
    slot_ref,
    ids_ref,
    x_ref,
    shrink_ref,
    expand_ref,
    marks_ref,
    in_ref,
    out_ref,
    facts_ref,
    kept_ref,
    held_ref,
    near_ref,
    sems,
):
    shards = order_ref.shape[0]
    half = near_ref.shape[1] // shards
    copies = [
        pltpu.make_async_copy(x_ref, kept_ref, sems.at[0]),
        pltpu.make_async_copy(shrink_ref, held_ref, sems.at[1]),
    ]
    for b in range(shards):
        columns = pl.ds(pl.multiple_of(at_ref[b] * half, half), half)
        put = near_ref.at[:, pl.ds(b * half, half)]
        copies.append(pltpu.make_async_copy(expand_ref.at[:, columns], put, sems.at[2 + b]))
    for copy in copies:
        copy.start()
    rows, variants = ids_ref.shape[1], slot_ref.shape[0]
    own_rows = rows // shards
    me = me_ref[0].astype(F32)
    order = [order_ref[b].astype(F32) for b in range(shards)]
    beside_me = order[ways.slow % shards]
    count = lambda shape, axis: lax.broadcasted_iota(I32, shape, axis).astype(F32)
    across = lambda a: jnp.sum(a, axis=1, keepdims=True)
    along = lambda a: jnp.sum(a, axis=0, keepdims=True)
    line, lane = count((rows, rows), 0), count((rows, rows), 1)
    diagonal = line == lane
    at_along, at_down = count((1, rows), 1), count((rows, 1), 0)
    for b in range(shards):
        shift = (order[b] - b) * own_rows
        low, high = b * own_rows, (b + 1) * own_rows
        at_along = jnp.where(
            (lane[:1] >= low) & (lane[:1] < high), lane[:1] + shift, at_along
        )
        at_down = jnp.where(
            (line[:, :1] >= low) & (line[:, :1] < high), line[:, :1] + shift, at_down
        )
    ids = across(jnp.where(lane == at_down, ids_ref[...].astype(F32), 0.0))
    ids = along(jnp.where(diagonal, ids, 0.0))
    slot = jnp.zeros_like(ids)
    for v in range(variants):
        slot = jnp.where(ids == float(v), slot_ref[v].astype(F32), slot)
    slot_down = across(jnp.where(diagonal, slot, 0.0))
    owner_of = lambda a: sum((a >= float(o * slots)).astype(F32) for o in range(1, shards))
    owner, owner_down = owner_of(slot), owner_of(slot_down)
    same = owner_down == owner
    place = along((same & (at_down < at_along)).astype(F32))
    packed, pair = place, jnp.zeros_like(place)
    step = arrive = jnp.zeros_like(place)
    paired = ways.direct and ways.fast == 2
    if paired:
        odd = sum((owner == float(o)).astype(F32) for o in range(1, shards, 2))
        beside = along((owner_down == owner + 1.0 - 2.0 * odd).astype(F32))
        pair = along(same.astype(F32)) + beside
    for b in range(shards):
        hit = owner == order[b]
        step = jnp.where(hit, float(b), step)
        arrive = jnp.where(hit, float(b % ways.slow if paired else b), arrive)
        if paired and b >= ways.slow:
            packed = jnp.where(hit, place + beside, packed)
    over = (place >= float(USUAL)).astype(F32)
    far_over = (place >= float(USUAL_PAIR)) | (pair > float(USUAL_PAIR))
    facts_ref[0] = jnp.max(jnp.where(far_over, 2.0, over)).astype(I32)
    facts_ref[1] = jnp.sum((owner == me).astype(F32)).astype(I32)
    facts_ref[2] = jnp.sum((owner == beside_me).astype(F32)).astype(I32)
    lines = {
        MINE: jnp.where(owner == me, place, -1.0),
        NEXT: jnp.where(owner == beside_me, place, -1.0),
        STEP: step,
        PLACE: place,
        ARRIVE: arrive,
        PACKED: packed,
    }
    for n, values in lines.items():
        marks_ref[n : n + 1] = values.astype(I32)
    local = slot_down - me * slots
    for ref in (in_ref, out_ref):
        wide = ref.shape[1] // slots
        column = count(ref.shape, 1)
        inside = (column >= local * wide) & (column < (local + 1.0) * wide)
        ref[...] = inside.astype(F32).astype(ref.dtype)
    for copy in copies:
        copy.wait()


def tables(ways, me, at, ids, variant_slot, x, shrink, expand, slots, rank):
    rows = ids.shape[1]
    shards = at.shape[0]
    depth, width = expand.shape
    return pl.pallas_call(
        functools.partial(tables_kernel, ways, slots),
        out_shape=(
            jax.ShapeDtypeStruct((8, rows), I32),
            jax.ShapeDtypeStruct((rows, slots * 2 * rank), F32),
            jax.ShapeDtypeStruct((rows, slots * rank), BF),
            jax.ShapeDtypeStruct((3,), I32),
            jax.ShapeDtypeStruct(x.shape, BF),
            jax.ShapeDtypeStruct(shrink.shape, BF),
            jax.ShapeDtypeStruct((depth, width // 2), BF),
        ),
        in_specs=[SCALARS] * 4 + [WHOLE] + [FAR] * 3,
        out_specs=(WHOLE, WHOLE, WHOLE, SCALARS, WHOLE, WHOLE, WHOLE),
        scratch_shapes=[pltpu.SemaphoreType.DMA((2 + shards,))],
        compiler_params=params(52),
        cost_estimate=cost(0, 4 * x.size + 4 * shrink.size + 2 * expand.size),
    )(ways.order, me, at, variant_slot, ids, x, shrink, expand)


def low_in_kernel(count, shrink_ref, mask_ref, *refs):
    parts, x_ref, out_ref = refs[:count], refs[count], refs[count + 1]
    x = jnp.concatenate([part[...].astype(F32) for part in parts], axis=0).astype(BF)
    x_ref[...] = x

    @pl.when(pl.program_id(0) == 0)
    def _():
        out_ref[...] = jnp.zeros_like(out_ref)

    out_ref[...] += jnp.where(mask_ref[...] > 0, dot_last(x, shrink_ref[...]), 0.0)


def low_in_pairs(parts, shrink, mask):
    count = len(parts)
    own_rows, width = parts[0].shape
    rows, block = count * own_rows, min(1024, width)
    return pl.pallas_call(
        lambda *refs: low_in_kernel(count, *refs),
        out_shape=(
            jax.ShapeDtypeStruct((rows, width), BF),
            jax.ShapeDtypeStruct(mask.shape, F32),
        ),
        grid=(width // block,),
        in_specs=[pl.BlockSpec((shrink.shape[0], block), lambda n: (0, n)), fixed(mask)]
        + [pl.BlockSpec((own_rows, block), lambda n: (0, n))] * count,
        out_specs=(pl.BlockSpec((rows, block), lambda n: (0, n)), fixed(mask)),
        compiler_params=params(16),
        cost_estimate=cost(2 * rows * width * shrink.shape[0], 2 * shrink.size + 4 * rows * width),
    )(shrink, mask, *parts)


def expand_kernel(
    cap, fast, at_ref, own_ref, got_ref, marks_ref, cols_ref, near_ref, far_ref, *out_refs
):
    low = (own_ref[...] + got_ref[...]).astype(BF)
    picked = dot(one_hot(cap, marks_ref[MINE : MINE + 1]), low).astype(BF)
    lhs = jnp.concatenate([dot(picked, cols_ref[kind]) for kind in range(2)], axis=0).astype(BF)
    tall = lhs.shape[0]
    half = out_refs[0].shape[1]
    count = at_ref.shape[0]
    for b in range(count):
        here = pl.ds(b * half, half)
        columns = pl.ds(pl.multiple_of(at_ref[b] * half, half), half)
        both = jnp.concatenate([near_ref[:, here], far_ref[:, columns]], axis=0)
        at = b % (count // fast)
        out_refs[b * fast // count][pl.ds(at * tall, tall)] = dot(lhs, both).astype(BF)


def expand_rows(at, own, got, marks, cols, near, far, cap, fast):
    depth, width = far.shape
    shards = at.shape[0]
    half = width // (2 * shards)
    out = jax.ShapeDtypeStruct((2 * cap * shards // fast, half), BF)
    return pl.pallas_call(
        functools.partial(expand_kernel, cap, fast),
        out_shape=(out,) * fast,
        in_specs=[SCALARS] + [WHOLE] * 6,
        compiler_params=params(16),
        cost_estimate=cost(8 * cap * depth * width, 4 * (depth + cap) * width),
    )(at, own, got, marks, cols, near, far)


def base_kernel(side_ref, x_ref, gate_ref, up_ref, out_ref, held, sums, sems):
    half = held.shape[2]
    chunks = sems.shape[1]
    depth = held.shape[1] // chunks
    columns = pl.ds(pl.multiple_of(side_ref[0] * half, half), half)
    copies = []
    for c in range(chunks):
        here = pl.ds(c * depth, depth)
        for kind, weight in enumerate((gate_ref, up_ref)):
            copy = pltpu.make_async_copy(
                weight.at[here, columns], held.at[kind, here], sems.at[kind, c]
            )
            copy.start()
            copies.append((kind, here, copy))
    for kind, here, copy in copies:
        copy.wait()
        part = dot(x_ref[:, here], held[kind, here])
        sums[kind] = part if here.start == 0 else sums[kind] + part
    out_ref[...] = sums[...].astype(out_ref.dtype)


def base_half(side, x, gate_weight, up_weight, half, kind):
    rows, width = x.shape
    chunks = max(width // 512, 1)
    return pl.pallas_call(
        base_kernel,
        out_shape=jax.ShapeDtypeStruct((2, rows, half), kind),
        in_specs=[SCALARS, WHOLE, FAR, FAR],
        out_specs=WHOLE,
        scratch_shapes=[
            pltpu.VMEM((2, width, half), BF),
            pltpu.VMEM((2, rows, half), F32),
            pltpu.SemaphoreType.DMA((2, chunks)),
        ],
        compiler_params=params(48),
        cost_estimate=cost(4 * rows * width * half, 4 * width * half + 2 * rows * width),
    )(side, x, gate_weight, up_weight)


def hidden_kernel(cap, room, count, own_ref, got_ref, marks_ref, *refs):
    parts, hid_ref, out_refs = refs[:count], refs[count], refs[count + 1 :]
    half = hid_ref.shape[1]
    cells = sum(part.shape[0] for part in parts)
    first_cell = marks_ref[ARRIVE : ARRIVE + 1] * (2 * room) + marks_ref[PACKED : PACKED + 1]
    places = [one_hot(cells, first_cell + kind * room) for kind in range(2)]
    tall = out_refs[0].shape[0]
    leave = marks_ref[STEP : STEP + 1] * cap + marks_ref[PLACE : PLACE + 1]
    send = one_hot(tall * len(out_refs), leave)
    block = min(256, half)
    for first in range(0, half, block):
        here = pl.ds(first, block)
        delta = jnp.concatenate([part[:, here] for part in parts], axis=0)
        gate, up = [
            own_ref[kind, :, here]
            + got_ref[kind, :, here].astype(F32)
            + dot_first(places[kind], delta)
            for kind in range(2)
        ]
        hidden = (gate / (1.0 + jnp.exp(-gate)) * up).astype(BF)
        hid_ref[:, here] = hidden
        sent = dot(send, hidden).astype(BF)
        for n, out_ref in enumerate(out_refs):
            out_ref[:, here] = sent[n * tall : (n + 1) * tall]


def hidden_half(own, got, parts, marks, cap, room, shards, count):
    rows, half = own.shape[1:]
    cells = shards * cap
    return pl.pallas_call(
        functools.partial(hidden_kernel, cap, room, len(parts)),
        out_shape=(jax.ShapeDtypeStruct((rows, half), BF),)
        + (jax.ShapeDtypeStruct((cells // count, half), BF),) * count,
        compiler_params=params(40),
        cost_estimate=cost(10 * half * cells * rows, 2 * half * (6 * rows + 3 * cells)),
    )(own, got, marks, *parts)


def pack_kernel(cap, facts_ref, own_ref, got_ref, *out_refs):
    column = lax.broadcasted_iota(I32, (1, 4 * cap), 1)
    from_got = column >= 2 * cap
    column = column - jnp.where(from_got, 2 * cap, 0)
    kind = jnp.where(column >= cap, 1, 0)
    row = column - kind * cap
    live = row < jnp.where(from_got, facts_ref[2], facts_ref[1])
    row = row + jnp.where(from_got, facts_ref[1], 0)
    room = out_refs[0].shape[0] // 2
    packing = one_hot(2 * room, jnp.where(live, row + kind * room, -1))
    for a, out_ref in enumerate(out_refs):
        here = pl.ds(a * 2 * cap, 2 * cap)
        both = jnp.concatenate([own_ref[here], got_ref[here]], axis=0)
        out_ref[...] = dot(packing, both).astype(BF)


def pack(facts, own, got, cap, room, count):
    half = own.shape[1]
    return pl.pallas_call(
        functools.partial(pack_kernel, cap),
        out_shape=(jax.ShapeDtypeStruct((2 * room, half), BF),) * count,
        in_specs=[SCALARS, WHOLE, WHOLE],
        compiler_params=params(16),
        cost_estimate=cost(0, 8 * own.size),
    )(facts, own, got)


def relay_kernel(own_ref, got_ref, *out_refs):
    cap = out_refs[0].shape[0] // 2
    for a, out_ref in enumerate(out_refs):
        here = pl.ds(a * cap, cap)
        out_ref[:cap] = own_ref[here]
        out_ref[cap:] = got_ref[here]


def relay(own, got, count):
    tall, half = own.shape
    return pl.pallas_call(
        relay_kernel,
        out_shape=(jax.ShapeDtypeStruct((2 * tall // count, half), BF),) * count,
        compiler_params=params(16),
        cost_estimate=cost(0, 8 * tall * half),
    )(own, got)


def down_kernel(start, core_ref, near_ref, far_ref, weight_ref, *refs):
    out_refs, held, sems = refs[:-2], refs[-2], refs[-1]
    chunks = sems.shape[1]
    half, width = held.shape[1:]
    block = width // chunks
    tall = out_refs[0].shape[0]
    copies = []
    for c in range(chunks):
        here = pl.ds(c * block, block)
        for side, at in enumerate((core_ref[0], 1 - core_ref[0])):
            lines = pl.ds(pl.multiple_of(at * half, half), half)
            copy = pltpu.make_async_copy(
                weight_ref.at[lines, pl.ds(start + c * block, block)],
                held.at[side, :, here],
                sems.at[side, c],
            )
            copy.start()
            copies.append(copy)
    for c in range(chunks):
        here = pl.ds(c * block, block)
        copies[2 * c].wait()
        copies[2 * c + 1].wait()
        total = dot(near_ref[...], held[0, :, here]) + dot(far_ref[...], held[1, :, here])
        for n, out_ref in enumerate(out_refs):
            out_ref[:, here] = total[n * tall : (n + 1) * tall].astype(out_ref.dtype)


def down_base(core, near, far, weight, start, width, kinds):
    rows, half = near.shape
    chunks = max(width // 512, 1)
    outs = tuple(jax.ShapeDtypeStruct((rows // len(kinds), width), kind) for kind in kinds)
    return pl.pallas_call(
        functools.partial(down_kernel, start),
        out_shape=outs,
        in_specs=[SCALARS, WHOLE, WHOLE, FAR],
        out_specs=(WHOLE,) * len(outs),
        scratch_shapes=[
            pltpu.VMEM((2, half, width), BF),
            pltpu.SemaphoreType.DMA((2, chunks)),
        ],
        compiler_params=params(48),
        cost_estimate=cost(4 * rows * half * width, 4 * half * width + 4 * rows * width),
    )(core, near, far, weight)


def low_out_kernel(cap, count, at_ref, marks_ref, slot_ref, shrink_ref, *refs):
    parts, out_ref = refs[:count], refs[count]
    half = parts[0].shape[1]
    blocks = [part[r : r + cap] for r in range(0, parts[0].shape[0], cap) for part in parts]
    pairs = jnp.zeros(out_ref.shape, F32)
    for b, block in enumerate(blocks):
        columns = pl.ds(pl.multiple_of(at_ref[b] * half, half), half)
        pairs += dot_last(block, shrink_ref[:, columns])
    mask = dot(one_hot(cap, marks_ref[MINE : MINE + 1]), slot_ref[...])
    out_ref[...] = jnp.where(mask > 0.5, pairs, 0.0)


def low_out_pairs(at, marks, slot_mask, shrink, parts, cap):
    count = len(parts)
    half = parts[0].shape[1]
    depth = shrink.shape[0]
    return pl.pallas_call(
        functools.partial(low_out_kernel, cap, count),
        out_shape=jax.ShapeDtypeStruct((cap, depth), F32),
        in_specs=[SCALARS] + [WHOLE] * (3 + count),
        compiler_params=params(16),
        cost_estimate=cost(
            2 * cap * depth * at.shape[0] * half, 2 * at.shape[0] * half * (depth + cap)
        ),
    )(at, marks, slot_mask, shrink, *parts)


def add_kernel(owners, sides, *refs):
    base_refs, refs = refs[: owners * sides], refs[owners * sides :]
    low_refs, refs = refs[: 2 * owners], refs[2 * owners :]
    marks_ref, expand_refs, out_refs = refs[0], refs[1 : owners + 1], refs[owners + 1 :]
    rows = base_refs[0].shape[0]
    spreads = []
    for n in range(owners):
        low = (low_refs[2 * n][...] + low_refs[2 * n + 1][...]).astype(BF)
        pick = one_hot(low.shape[0], marks_ref[MINE + n : MINE + n + 1, :rows])
        spreads.append(dot_first(pick, low).astype(BF))
    spread = jnp.concatenate(spreads, axis=1)
    own_rows, width = out_refs[0].shape
    side = width // sides
    block = min(1024, side)
    for first in range(0, width, block):
        here = pl.ds(first, block)
        inside = pl.ds(first % side, block)
        expand = jnp.concatenate([ref[:, here] for ref in expand_refs], axis=0)
        total = dot(spread, expand)
        for base_ref in base_refs[first // side :: sides]:
            total += base_ref[:, inside].astype(F32)
        for b, out_ref in enumerate(out_refs):
            out_ref[:, here] = total[b * own_rows : (b + 1) * own_rows].astype(BF)


def add_delta(bases, lows, marks, expands, count):
    owners = len(expands)
    rows = bases[0].shape[0]
    depth, width = expands[0].shape
    return pl.pallas_call(
        functools.partial(add_kernel, owners, len(bases) // owners),
        out_shape=(jax.ShapeDtypeStruct((rows // count, width), BF),) * count,
        compiler_params=params(32),
        cost_estimate=cost(
            2 * rows * depth * owners * width, width * (6 * rows + 2 * depth) * owners
        ),
    )(*bases, *lows, marks, *expands)


def tied(first, *others):
    return lax.optimization_barrier((first, *others))


def per_device(
    tokens,
    gate_weight,
    up_weight,
    down_weight,
    shrink_gu,
    expand_gu,
    shrink_down,
    expand_down,
    variant_ids,
    variant_slot,
):
    ways = Ways()
    shards, order = ways.shards, ways.order
    me = lax.axis_index("ff").astype(I32)
    core = lax.axis_index("var").astype(I32)
    groups = lax.axis_size("groups")
    own_rows, width = tokens.shape
    rows = own_rows * shards
    slots = shrink_gu.shape[0]
    rank = shrink_down.shape[1]
    half_rank = expand_gu.shape[2]
    half = gate_weight.shape[1] // 2
    most = min(slots * MOST, rows)
    here = core.reshape(1)
    there = 1 - here
    at_here = 2 * order + core
    split = ways.fast if ways.direct else 1
    swap = lambda a: lax.ppermute(a, "var", [(0, 1), (1, 0)])

    near = expand_gu.reshape(slots * 2 * half_rank, -1)
    token_parts, far = ways.gather(tokens, swap(near))
    shrink_in = shrink_gu.reshape(slots * 2 * rank, width)
    marks, mask_in, slot_mask, facts, token_parts[0], shrink_in, near = tables(
        ways,
        me.reshape(1),
        at_here,
        variant_ids.reshape(1, rows),
        variant_slot,
        token_parts[0],
        shrink_in,
        near,
        slots,
        rank,
    )
    most_facts = facts
    for turn in range(1, 1 if ways.direct else groups):
        pairs = [(g, (g + turn) % groups) for g in range(groups)]
        most_facts = jnp.maximum(most_facts, lax.ppermute(facts, "groups", pairs))
    kinds = jnp.arange(2, dtype=I32)
    in_cols = jnp.arange(slots * 2 * rank, dtype=I32)
    rank_at = in_cols % rank
    kind_at = in_cols // rank % 2
    row_at = in_cols // (2 * rank) * (2 * half_rank) + kind_at * half_rank + rank_at % half_rank
    depth = slots * 2 * half_rank
    both_cols = jnp.arange(2 * depth, dtype=I32)
    wanted = row_at + jnp.where(rank_at // half_rank == core, 0, depth)
    hit = wanted[:, None] == both_cols[None, :]
    cols = (hit[None] & (kind_at[None, :] == kinds[:, None])[:, :, None]).astype(BF)

    x, low_own = low_in_pairs(token_parts, shrink_in, mask_in)
    low_got = swap(low_own)

    def partial_sums(cap, room):
        made = expand_rows(at_here, low_own, low_got, marks, cols, near, far, cap, split)
        held, *made = tied(x, *made)
        expand = expand_down.reshape(slots * rank, width)
        if split == 2:
            beside = lax.ppermute(made[1], "ff", ways.back(0, 1))
            base_there = base_half(there, held, gate_weight, up_weight, half, BF)
            base_there, beside = tied(base_there, beside)
            made = pack(facts, made[0], beside, cap, room, ways.slow)
            held, expand, *made = tied(held, expand, *made)
            delta = ways.slow_steps(made)
            expand_beside = lax.ppermute(expand, "ff", ways.back(0, 1))
        else:
            base_there = base_half(there, held, gate_weight, up_weight, half, BF)
            delta = ways.spread(made[0].reshape(shards, 2 * cap, half))
            delta = [delta.reshape(2 * shards * cap, half)]
        base_got = swap(base_there)
        base_own = base_half(here, held, gate_weight, up_weight, half, F32)
        hidden, *sent = hidden_half(
            base_own, base_got, delta, marks, cap, room, shards, split
        )
        hidden_far = swap(hidden)
        shrink = shrink_down.reshape(slots * rank, -1)
        side = width // 2
        down = functools.partial(down_base, here, hidden, hidden_far, down_weight)
        if split == 2:
            beside = lax.ppermute(sent[1], "ff", ways.back(0, 1))
            left, left_sent = down(0, side, (F32, BF))
            left_sent, beside, expand_beside = tied(left_sent, beside, expand_beside)
            left_beside = lax.ppermute(left_sent, "ff", ways.back(0, 1))
            sent = relay(sent[0], beside, ways.slow)
            hidden, *sent = tied(hidden, *sent)
            down = functools.partial(down_base, here, hidden, hidden_far, down_weight)
            got = ways.slow_steps(sent)
            right, right_sent = down(side, side, (F32, BF))
            right_sent, left_beside, *got = tied(right_sent, left_beside, *got)
            right_beside = lax.ppermute(right_sent, "ff", ways.back(0, 1))
            bases = [left, right, left_beside, right_beside]
        else:
            bases = [down(0, side, (F32,))[0], down(side, side, (F32,))[0]]
            got = [ways.spread(sent[0].reshape(shards, cap, half)).reshape(shards * cap, half)]
        bases[1], *got = tied(bases[1], *got)
        out_own = low_out_pairs(at_here, marks, slot_mask, shrink, got, cap)
        out_got = swap(out_own)
        if split == 1:
            parts = add_delta(bases, [out_own, out_got], marks, [expand], shards)
            return list(ways.spread(jnp.stack(parts)))
        out_beside = lax.ppermute(out_own, "ff", ways.back(0, 1))
        across = [
            (2 * f + v, 2 * g + 1 - v) for f, g in ways.back(0, 1) for v in range(2)
        ]
        out_across = lax.ppermute(out_own, ("ff", "var"), across)
        parts = add_delta(
            bases,
            [out_own, out_got, out_beside, out_across],
            marks,
            [expand, expand_beside],
            ways.slow,
        )
        return ways.slow_steps(parts)

    most_room = 2 * most if split == 2 else most
    if most <= USUAL_PAIR:
        parts = partial_sums(most, most_room)
    else:
        rooms = [(USUAL, USUAL_PAIR), (USUAL_PAIR, USUAL_PAIR), (most, 2 * most)]
        branches = [
            functools.partial(partial_sums, cap, room if split == 2 else cap) for cap, room in rooms
        ]
        parts = lax.switch(most_facts[0], branches)
    return sum(part.astype(F32) for part in parts).astype(BF)


def solution(mesh):
    placed = (
        P(("groups", "ff"), "var"),
        P("var", "ff"),
        P("var", "ff"),
        P("ff", "var"),
        P(("groups", "ff"), None, "var"),
        P(("groups", "ff"), None, "var", None),
        P(("groups", "ff"), None, None),
        P(("groups", "ff"), None, "var"),
        P("groups", None),
        P("groups"),
    )
    return jax.shard_map(
        per_device,
        mesh=mesh,
        in_specs=placed,
        out_specs=P(("groups", "ff"), "var"),
        check_vma=False,
    )
```

```python
import functools

import jax
import jax.numpy as jnp
from jax import lax
from jax.experimental import pallas as pl
from jax.experimental.pallas import tpu as pltpu
from jax.sharding import PartitionSpec as P

MOST = 8
DIRECT = 8
MINE, NEXT, STEP, PLACE, ARRIVE, PACKED = range(6)
USUAL = 16
USUAL_PAIR = 24
BF = jnp.bfloat16
F32 = jnp.float32
I32 = jnp.int32
MIB = 1024 * 1024


def dot(a, b):
    return jnp.dot(a, b, preferred_element_type=F32)


def dot_last(a, b):
    return lax.dot_general(a, b, (((1,), (1,)), ((), ())), preferred_element_type=F32)


def params(mib):
    return pltpu.CompilerParams(vmem_limit_bytes=int(mib * MIB))


def cost(flops, moved):
    return pl.CostEstimate(flops=flops, bytes_accessed=moved, transcendentals=0)


SCALARS = pl.BlockSpec(memory_space=pltpu.SMEM)
WHOLE = pl.BlockSpec(memory_space=pltpu.VMEM)
FAR = pl.BlockSpec(memory_space=pltpu.HBM)


def fixed(array):
    zeros = (0,) * array.ndim
    return pl.BlockSpec(array.shape, lambda *_: zeros)


def one_hot(count, cell):
    lines = lax.broadcasted_iota(I32, (count, cell.shape[1]), 0)
    return (lines == cell).astype(F32).astype(BF)


def dot_first(a, b):
    return lax.dot_general(a, b, (((0,), (0,)), ((), ())), preferred_element_type=F32)


class Ways:
    def __init__(self):
        self.shards = lax.axis_size("ff")
        self.fast = 2 if self.shards % 2 == 0 else 1
        self.slow = self.shards // self.fast
        self.direct = self.shards <= DIRECT
        me = lax.axis_index("ff").astype(I32)
        steps = jnp.arange(self.shards, dtype=I32)
        if self.direct:
            slow = (me // self.fast - steps % self.slow) % self.slow
            fast = (me % self.fast - steps // self.slow) % self.fast
            self.order = slow * self.fast + fast
        else:
            self.order = steps

    def back(self, a, c):
        S, F = self.slow, self.fast
        return [(s * F + f, (s - a) % S * F + (f - c) % F) for s in range(S) for f in range(F)]

    def gather(self, block, *others):
        if not self.direct:
            return list(lax.all_gather(block, "ff")), *others
        got = [block] + [
            lax.ppermute(block, "ff", self.back(-a, 0)) for a in range(1, self.slow)
        ]
        got[1], *others = tied(got[1], *others)
        for c in range(1, self.fast):
            got += [lax.ppermute(part, "ff", self.back(0, -c)) for part in got[: self.slow]]
        return got, *others

    def spread(self, blocks):
        return lax.all_to_all(blocks, "ff", 0, 0, tiled=True)

    def slow_steps(self, blocks):
        got = [blocks[0]] + [None] * (self.slow - 1)
        for a in range(1, self.slow):
            got[(-a) % self.slow] = lax.ppermute(blocks[a], "ff", self.back(a, 0))
        return got


def tables_kernel(
    ways,
    slots,
    order_ref,
    me_ref,
    at_ref,
    named_ref,
    x_ref,
    shrink_ref,
    expand_ref,
    marks_ref,
    in_ref,
    out_ref,
    facts_ref,
    kept_ref,
    held_ref,
    near_ref,
    sems,
):
    shards = order_ref.shape[0]
    half = near_ref.shape[1] // shards
    copies = [
        pltpu.make_async_copy(x_ref, kept_ref, sems.at[0]),
        pltpu.make_async_copy(shrink_ref, held_ref, sems.at[1]),
    ]
    for b in range(shards):
        columns = pl.ds(pl.multiple_of(at_ref[b] * half, half), half)
        put = near_ref.at[:, pl.ds(b * half, half)]
        copies.append(pltpu.make_async_copy(expand_ref.at[:, columns], put, sems.at[2 + b]))
    for copy in copies:
        copy.start()
    rows, size = in_ref.shape[0], named_ref.shape[1]
    own_rows = rows // shards
    me = me_ref[0].astype(F32)
    order = [order_ref[b].astype(F32) for b in range(shards)]
    beside_me = order[ways.slow % shards]
    count = lambda shape, axis: lax.broadcasted_iota(I32, shape, axis).astype(F32)
    across = lambda a: jnp.sum(a, axis=1, keepdims=True)
    along = lambda a: jnp.sum(a, axis=0, keepdims=True)
    line, lane = count((rows, rows), 0), count((rows, rows), 1)
    diagonal = line == lane
    at_along, at_down = count((1, rows), 1), count((rows, 1), 0)
    for b in range(shards):
        shift = (order[b] - b) * own_rows
        low, high = b * own_rows, (b + 1) * own_rows
        at_along = jnp.where(
            (lane[:1] >= low) & (lane[:1] < high), lane[:1] + shift, at_along
        )
        at_down = jnp.where(
            (line[:, :1] >= low) & (line[:, :1] < high), line[:, :1] + shift, at_down
        )
    named = named_ref[...].astype(F32)
    ids = across(jnp.where(count((rows, size), 1) == at_down, named, 0.0))
    ids = along(jnp.where(diagonal, ids, 0.0))
    variants = size - rows
    of_variant = count((variants, size), 1) == count((variants, size), 0) + rows
    slots_down = across(jnp.where(of_variant, named, 0.0))
    slot = along(jnp.where(count((variants, rows), 0) == ids, slots_down, 0.0))
    slot_down = across(jnp.where(diagonal, slot, 0.0))
    owner_of = lambda a: sum((a >= float(o * slots)).astype(F32) for o in range(1, shards))
    owner, owner_down = owner_of(slot), owner_of(slot_down)
    same = owner_down == owner
    place = along((same & (at_down < at_along)).astype(F32))
    packed, pair = place, jnp.zeros_like(place)
    step = arrive = jnp.zeros_like(place)
    paired = ways.direct and ways.fast == 2
    if paired:
        odd = sum((owner == float(o)).astype(F32) for o in range(1, shards, 2))
        beside = along((owner_down == owner + 1.0 - 2.0 * odd).astype(F32))
        pair = along(same.astype(F32)) + beside
    for b in range(shards):
        hit = owner == order[b]
        step = jnp.where(hit, float(b), step)
        arrive = jnp.where(hit, float(b % ways.slow if paired else b), arrive)
        if paired and b >= ways.slow:
            packed = jnp.where(hit, place + beside, packed)
    over = (place >= float(USUAL)).astype(F32)
    far_over = (place >= float(USUAL_PAIR)) | (pair > float(USUAL_PAIR))
    facts_ref[0] = jnp.max(jnp.where(far_over, 2.0, over)).astype(I32)
    facts_ref[1] = jnp.sum((owner == me).astype(F32)).astype(I32)
    facts_ref[2] = jnp.sum((owner == beside_me).astype(F32)).astype(I32)
    lines = {
        MINE: jnp.where(owner == me, place, -1.0),
        NEXT: jnp.where(owner == beside_me, place, -1.0),
        STEP: step,
        PLACE: place,
        ARRIVE: arrive,
        PACKED: packed,
    }
    for n, values in lines.items():
        marks_ref[n : n + 1] = values.astype(I32)
    local = slot_down - me * slots
    for ref in (in_ref, out_ref):
        wide = ref.shape[1] // slots
        column = count(ref.shape, 1)
        inside = (column >= local * wide) & (column < (local + 1.0) * wide)
        ref[...] = inside.astype(F32).astype(ref.dtype)
    for copy in copies:
        copy.wait()


def tables(ways, me, at, named, x, shrink, expand, rows, slots, rank):
    shards = at.shape[0]
    depth, width = expand.shape
    return pl.pallas_call(
        functools.partial(tables_kernel, ways, slots),
        out_shape=(
            jax.ShapeDtypeStruct((8, rows), I32),
            jax.ShapeDtypeStruct((rows, slots * 2 * rank), F32),
            jax.ShapeDtypeStruct((rows, slots * rank), BF),
            jax.ShapeDtypeStruct((3,), I32),
            jax.ShapeDtypeStruct(x.shape, BF),
            jax.ShapeDtypeStruct(shrink.shape, BF),
            jax.ShapeDtypeStruct((depth, width // 2), BF),
        ),
        in_specs=[SCALARS] * 3 + [WHOLE] + [FAR] * 3,
        out_specs=(WHOLE, WHOLE, WHOLE, SCALARS, WHOLE, WHOLE, WHOLE),
        scratch_shapes=[pltpu.SemaphoreType.DMA((2 + shards,))],
        compiler_params=params(52),
        cost_estimate=cost(0, 4 * x.size + 4 * shrink.size + 2 * expand.size),
    )(ways.order, me, at, named, x, shrink, expand)


def low_in_kernel(count, shrink_ref, mask_ref, *refs):
    parts, x_ref, out_ref = refs[:count], refs[count], refs[count + 1]
    x = jnp.concatenate([part[...].astype(F32) for part in parts], axis=0).astype(BF)
    x_ref[...] = x

    @pl.when(pl.program_id(0) == 0)
    def _():
        out_ref[...] = jnp.zeros_like(out_ref)

    out_ref[...] += jnp.where(mask_ref[...] > 0, dot_last(x, shrink_ref[...]), 0.0)


def low_in_pairs(parts, shrink, mask):
    count = len(parts)
    own_rows, width = parts[0].shape
    rows, block = count * own_rows, min(1024, width)
    return pl.pallas_call(
        lambda *refs: low_in_kernel(count, *refs),
        out_shape=(
            jax.ShapeDtypeStruct((rows, width), BF),
            jax.ShapeDtypeStruct(mask.shape, F32),
        ),
        grid=(width // block,),
        in_specs=[pl.BlockSpec((shrink.shape[0], block), lambda n: (0, n)), fixed(mask)]
        + [pl.BlockSpec((own_rows, block), lambda n: (0, n))] * count,
        out_specs=(pl.BlockSpec((rows, block), lambda n: (0, n)), fixed(mask)),
        compiler_params=params(16),
        cost_estimate=cost(2 * rows * width * shrink.shape[0], 2 * shrink.size + 4 * rows * width),
    )(shrink, mask, *parts)


def expand_kernel(
    cap, fast, at_ref, own_ref, got_ref, marks_ref, cols_ref, near_ref, far_ref, *out_refs
):
    low = (own_ref[...] + got_ref[...]).astype(BF)
    picked = dot(one_hot(cap, marks_ref[MINE : MINE + 1]), low).astype(BF)
    lhs = jnp.concatenate([dot(picked, cols_ref[kind]) for kind in range(2)], axis=0).astype(BF)
    tall = lhs.shape[0]
    half = out_refs[0].shape[1]
    count = at_ref.shape[0]
    for b in range(count):
        here = pl.ds(b * half, half)
        columns = pl.ds(pl.multiple_of(at_ref[b] * half, half), half)
        both = jnp.concatenate([near_ref[:, here], far_ref[:, columns]], axis=0)
        at = b % (count // fast)
        out_refs[b * fast // count][pl.ds(at * tall, tall)] = dot(lhs, both).astype(BF)


def expand_rows(at, own, got, marks, cols, near, far, cap, fast):
    depth, width = far.shape
    shards = at.shape[0]
    half = width // (2 * shards)
    out = jax.ShapeDtypeStruct((2 * cap * shards // fast, half), BF)
    return pl.pallas_call(
        functools.partial(expand_kernel, cap, fast),
        out_shape=(out,) * fast,
        in_specs=[SCALARS] + [WHOLE] * 6,
        compiler_params=params(16),
        cost_estimate=cost(8 * cap * depth * width, 4 * (depth + cap) * width),
    )(at, own, got, marks, cols, near, far)


def base_kernel(side_ref, x_ref, gate_ref, up_ref, out_ref, held, sums, sems):
    half = held.shape[2]
    chunks = sems.shape[1]
    depth = held.shape[1] // chunks
    columns = pl.ds(pl.multiple_of(side_ref[0] * half, half), half)
    copies = []
    for c in range(chunks):
        here = pl.ds(c * depth, depth)
        for kind, weight in enumerate((gate_ref, up_ref)):
            copy = pltpu.make_async_copy(
                weight.at[here, columns], held.at[kind, here], sems.at[kind, c]
            )
            copy.start()
            copies.append((kind, here, copy))
    for kind, here, copy in copies:
        copy.wait()
        part = dot(x_ref[:, here], held[kind, here])
        sums[kind] = part if here.start == 0 else sums[kind] + part
    out_ref[...] = sums[...].astype(out_ref.dtype)


def base_half(side, x, gate_weight, up_weight, half, kind):
    rows, width = x.shape
    chunks = max(width // 512, 1)
    return pl.pallas_call(
        base_kernel,
        out_shape=jax.ShapeDtypeStruct((2, rows, half), kind),
        in_specs=[SCALARS, WHOLE, FAR, FAR],
        out_specs=WHOLE,
        scratch_shapes=[
            pltpu.VMEM((2, width, half), BF),
            pltpu.VMEM((2, rows, half), F32),
            pltpu.SemaphoreType.DMA((2, chunks)),
        ],
        compiler_params=params(48),
        cost_estimate=cost(4 * rows * width * half, 4 * width * half + 2 * rows * width),
    )(side, x, gate_weight, up_weight)


def hidden_kernel(cap, room, count, own_ref, got_ref, marks_ref, *refs):
    parts, hid_ref, out_refs = refs[:count], refs[count], refs[count + 1 :]
    half = hid_ref.shape[1]
    cells = sum(part.shape[0] for part in parts)
    first_cell = marks_ref[ARRIVE : ARRIVE + 1] * (2 * room) + marks_ref[PACKED : PACKED + 1]
    places = [one_hot(cells, first_cell + kind * room) for kind in range(2)]
    tall = out_refs[0].shape[0]
    leave = marks_ref[STEP : STEP + 1] * cap + marks_ref[PLACE : PLACE + 1]
    send = one_hot(tall * len(out_refs), leave)
    block = min(256, half)
    for first in range(0, half, block):
        here = pl.ds(first, block)
        delta = jnp.concatenate([part[:, here] for part in parts], axis=0)
        gate, up = [
            own_ref[kind, :, here]
            + got_ref[kind, :, here].astype(F32)
            + dot_first(places[kind], delta)
            for kind in range(2)
        ]
        hidden = (gate / (1.0 + jnp.exp(-gate)) * up).astype(BF)
        hid_ref[:, here] = hidden
        sent = dot(send, hidden).astype(BF)
        for n, out_ref in enumerate(out_refs):
            out_ref[:, here] = sent[n * tall : (n + 1) * tall]


def hidden_half(own, got, parts, marks, cap, room, shards, count):
    rows, half = own.shape[1:]
    cells = shards * cap
    return pl.pallas_call(
        functools.partial(hidden_kernel, cap, room, len(parts)),
        out_shape=(jax.ShapeDtypeStruct((rows, half), BF),)
        + (jax.ShapeDtypeStruct((cells // count, half), BF),) * count,
        compiler_params=params(40),
        cost_estimate=cost(10 * half * cells * rows, 2 * half * (6 * rows + 3 * cells)),
    )(own, got, marks, *parts)


def pack_kernel(cap, facts_ref, own_ref, got_ref, *out_refs):
    column = lax.broadcasted_iota(I32, (1, 4 * cap), 1)
    from_got = column >= 2 * cap
    column = column - jnp.where(from_got, 2 * cap, 0)
    kind = jnp.where(column >= cap, 1, 0)
    row = column - kind * cap
    live = row < jnp.where(from_got, facts_ref[2], facts_ref[1])
    row = row + jnp.where(from_got, facts_ref[1], 0)
    room = out_refs[0].shape[0] // 2
    packing = one_hot(2 * room, jnp.where(live, row + kind * room, -1))
    for a, out_ref in enumerate(out_refs):
        here = pl.ds(a * 2 * cap, 2 * cap)
        both = jnp.concatenate([own_ref[here], got_ref[here]], axis=0)
        out_ref[...] = dot(packing, both).astype(BF)


def pack(facts, own, got, cap, room, count):
    half = own.shape[1]
    return pl.pallas_call(
        functools.partial(pack_kernel, cap),
        out_shape=(jax.ShapeDtypeStruct((2 * room, half), BF),) * count,
        in_specs=[SCALARS, WHOLE, WHOLE],
        compiler_params=params(16),
        cost_estimate=cost(0, 8 * own.size),
    )(facts, own, got)


def relay_kernel(own_ref, got_ref, *out_refs):
    cap = out_refs[0].shape[0] // 2
    for a, out_ref in enumerate(out_refs):
        here = pl.ds(a * cap, cap)
        out_ref[:cap] = own_ref[here]
        out_ref[cap:] = got_ref[here]


def relay(own, got, count):
    tall, half = own.shape
    return pl.pallas_call(
        relay_kernel,
        out_shape=(jax.ShapeDtypeStruct((2 * tall // count, half), BF),) * count,
        compiler_params=params(16),
        cost_estimate=cost(0, 8 * tall * half),
    )(own, got)


def down_kernel(start, core_ref, near_ref, far_ref, weight_ref, *refs):
    out_refs, held, sems = refs[:-2], refs[-2], refs[-1]
    chunks = sems.shape[1]
    half, width = held.shape[1:]
    block = width // chunks
    tall = out_refs[0].shape[0]
    copies = []
    for c in range(chunks):
        here = pl.ds(c * block, block)
        for side, at in enumerate((core_ref[0], 1 - core_ref[0])):
            lines = pl.ds(pl.multiple_of(at * half, half), half)
            copy = pltpu.make_async_copy(
                weight_ref.at[lines, pl.ds(start + c * block, block)],
                held.at[side, :, here],
                sems.at[side, c],
            )
            copy.start()
            copies.append(copy)
    for c in range(chunks):
        here = pl.ds(c * block, block)
        copies[2 * c].wait()
        copies[2 * c + 1].wait()
        total = dot(near_ref[...], held[0, :, here]) + dot(far_ref[...], held[1, :, here])
        for n, out_ref in enumerate(out_refs):
            out_ref[:, here] = total[n * tall : (n + 1) * tall].astype(out_ref.dtype)


def down_base(core, near, far, weight, start, width, kinds):
    rows, half = near.shape
    chunks = max(width // 512, 1)
    outs = tuple(jax.ShapeDtypeStruct((rows // len(kinds), width), kind) for kind in kinds)
    return pl.pallas_call(
        functools.partial(down_kernel, start),
        out_shape=outs,
        in_specs=[SCALARS, WHOLE, WHOLE, FAR],
        out_specs=(WHOLE,) * len(outs),
        scratch_shapes=[
            pltpu.VMEM((2, half, width), BF),
            pltpu.SemaphoreType.DMA((2, chunks)),
        ],
        compiler_params=params(48),
        cost_estimate=cost(4 * rows * half * width, 4 * half * width + 4 * rows * width),
    )(core, near, far, weight)


def low_out_kernel(cap, count, at_ref, marks_ref, slot_ref, shrink_ref, *refs):
    parts, out_ref = refs[:count], refs[count]
    half = parts[0].shape[1]
    blocks = [part[r : r + cap] for r in range(0, parts[0].shape[0], cap) for part in parts]
    pairs = jnp.zeros(out_ref.shape, F32)
    for b, block in enumerate(blocks):
        columns = pl.ds(pl.multiple_of(at_ref[b] * half, half), half)
        pairs += dot_last(block, shrink_ref[:, columns])
    mask = dot(one_hot(cap, marks_ref[MINE : MINE + 1]), slot_ref[...])
    out_ref[...] = jnp.where(mask > 0.5, pairs, 0.0)


def low_out_pairs(at, marks, slot_mask, shrink, parts, cap):
    count = len(parts)
    half = parts[0].shape[1]
    depth = shrink.shape[0]
    return pl.pallas_call(
        functools.partial(low_out_kernel, cap, count),
        out_shape=jax.ShapeDtypeStruct((cap, depth), F32),
        in_specs=[SCALARS] + [WHOLE] * (3 + count),
        compiler_params=params(16),
        cost_estimate=cost(
            2 * cap * depth * at.shape[0] * half, 2 * at.shape[0] * half * (depth + cap)
        ),
    )(at, marks, slot_mask, shrink, *parts)


def add_kernel(owners, sides, *refs):
    base_refs, refs = refs[: owners * sides], refs[owners * sides :]
    low_refs, refs = refs[: 2 * owners], refs[2 * owners :]
    marks_ref, expand_refs, out_refs = refs[0], refs[1 : owners + 1], refs[owners + 1 :]
    rows = base_refs[0].shape[0]
    spreads = []
    for n in range(owners):
        low = (low_refs[2 * n][...] + low_refs[2 * n + 1][...]).astype(BF)
        pick = one_hot(low.shape[0], marks_ref[MINE + n : MINE + n + 1, :rows])
        spreads.append(dot_first(pick, low).astype(BF))
    spread = jnp.concatenate(spreads, axis=1)
    own_rows, width = out_refs[0].shape
    side = width // sides
    block = min(1024, side)
    for first in range(0, width, block):
        here = pl.ds(first, block)
        inside = pl.ds(first % side, block)
        expand = jnp.concatenate([ref[:, here] for ref in expand_refs], axis=0)
        total = dot(spread, expand)
        for base_ref in base_refs[first // side :: sides]:
            total += base_ref[:, inside].astype(F32)
        for b, out_ref in enumerate(out_refs):
            out_ref[:, here] = total[b * own_rows : (b + 1) * own_rows].astype(BF)


def add_delta(bases, lows, marks, expands, count):
    owners = len(expands)
    rows = bases[0].shape[0]
    depth, width = expands[0].shape
    return pl.pallas_call(
        functools.partial(add_kernel, owners, len(bases) // owners),
        out_shape=(jax.ShapeDtypeStruct((rows // count, width), BF),) * count,
        compiler_params=params(32),
        cost_estimate=cost(
            2 * rows * depth * owners * width, width * (6 * rows + 2 * depth) * owners
        ),
    )(*bases, *lows, marks, *expands)


def tied(first, *others):
    return lax.optimization_barrier((first, *others))


def per_device(
    tokens,
    gate_weight,
    up_weight,
    down_weight,
    shrink_gu,
    expand_gu,
    shrink_down,
    expand_down,
    variant_ids,
    variant_slot,
):
    ways = Ways()
    shards, order = ways.shards, ways.order
    me = lax.axis_index("ff").astype(I32)
    core = lax.axis_index("var").astype(I32)
    groups = lax.axis_size("groups")
    own_rows, width = tokens.shape
    rows = own_rows * shards
    slots = shrink_gu.shape[0]
    rank = shrink_down.shape[1]
    half_rank = expand_gu.shape[2]
    half = gate_weight.shape[1] // 2
    most = min(slots * MOST, rows)
    here = core.reshape(1)
    there = 1 - here
    at_here = 2 * order + core
    split = ways.fast if ways.direct else 1
    swap = lambda a: lax.ppermute(a, "var", [(0, 1), (1, 0)])

    near = expand_gu.reshape(slots * 2 * half_rank, -1)
    named = jnp.concatenate([variant_ids[:, 0], variant_slot]).reshape(1, -1)
    token_parts, far, named = ways.gather(tokens, swap(near), named)
    shrink_in = shrink_gu.reshape(slots * 2 * rank, width)
    marks, mask_in, slot_mask, facts, token_parts[0], shrink_in, near = tables(
        ways,
        me.reshape(1),
        at_here,
        named,
        token_parts[0],
        shrink_in,
        near,
        rows,
        slots,
        rank,
    )
    most_facts = facts
    for turn in range(1, 1 if ways.direct else groups):
        pairs = [(g, (g + turn) % groups) for g in range(groups)]
        most_facts = jnp.maximum(most_facts, lax.ppermute(facts, "groups", pairs))
    kinds = jnp.arange(2, dtype=I32)
    in_cols = jnp.arange(slots * 2 * rank, dtype=I32)
    rank_at = in_cols % rank
    kind_at = in_cols // rank % 2
    row_at = in_cols // (2 * rank) * (2 * half_rank) + kind_at * half_rank + rank_at % half_rank
    depth = slots * 2 * half_rank
    both_cols = jnp.arange(2 * depth, dtype=I32)
    wanted = row_at + jnp.where(rank_at // half_rank == core, 0, depth)
    hit = wanted[:, None] == both_cols[None, :]
    cols = (hit[None] & (kind_at[None, :] == kinds[:, None])[:, :, None]).astype(BF)

    x, low_own = low_in_pairs(token_parts, shrink_in, mask_in)
    low_got = swap(low_own)

    def partial_sums(cap, room):
        made = expand_rows(at_here, low_own, low_got, marks, cols, near, far, cap, split)
        held, *made = tied(x, *made)
        expand = expand_down.reshape(slots * rank, width)
        if split == 2:
            beside = lax.ppermute(made[1], "ff", ways.back(0, 1))
            base_there = base_half(there, held, gate_weight, up_weight, half, BF)
            base_there, beside = tied(base_there, beside)
            made = pack(facts, made[0], beside, cap, room, ways.slow)
            held, expand, *made = tied(held, expand, *made)
            delta = ways.slow_steps(made)
            expand_beside = lax.ppermute(expand, "ff", ways.back(0, 1))
        else:
            base_there = base_half(there, held, gate_weight, up_weight, half, BF)
            delta = ways.spread(made[0].reshape(shards, 2 * cap, half))
            delta = [delta.reshape(2 * shards * cap, half)]
        base_got = swap(base_there)
        base_own = base_half(here, held, gate_weight, up_weight, half, F32)
        hidden, *sent = hidden_half(
            base_own, base_got, delta, marks, cap, room, shards, split
        )
        hidden_far = swap(hidden)
        shrink = shrink_down.reshape(slots * rank, -1)
        side = width // 2
        down = functools.partial(down_base, here, hidden, hidden_far, down_weight)
        if split == 2:
            beside = lax.ppermute(sent[1], "ff", ways.back(0, 1))
            left, left_sent = down(0, side, (F32, BF))
            left_sent, beside, expand_beside = tied(left_sent, beside, expand_beside)
            left_beside = lax.ppermute(left_sent, "ff", ways.back(0, 1))
            sent = relay(sent[0], beside, ways.slow)
            hidden, *sent = tied(hidden, *sent)
            down = functools.partial(down_base, here, hidden, hidden_far, down_weight)
            got = ways.slow_steps(sent)
            right, right_sent = down(side, side, (F32, BF))
            right_sent, left_beside, *got = tied(right_sent, left_beside, *got)
            right_beside = lax.ppermute(right_sent, "ff", ways.back(0, 1))
            bases = [left, right, left_beside, right_beside]
        else:
            bases = [down(0, side, (F32,))[0], down(side, side, (F32,))[0]]
            got = [ways.spread(sent[0].reshape(shards, cap, half)).reshape(shards * cap, half)]
        bases[1], *got = tied(bases[1], *got)
        out_own = low_out_pairs(at_here, marks, slot_mask, shrink, got, cap)
        out_got = swap(out_own)
        if split == 1:
            parts = add_delta(bases, [out_own, out_got], marks, [expand], shards)
            return list(ways.spread(jnp.stack(parts)))
        out_beside = lax.ppermute(out_own, "ff", ways.back(0, 1))
        across = [
            (2 * f + v, 2 * g + 1 - v) for f, g in ways.back(0, 1) for v in range(2)
        ]
        out_across = lax.ppermute(out_own, ("ff", "var"), across)
        parts = add_delta(
            bases,
            [out_own, out_got, out_beside, out_across],
            marks,
            [expand, expand_beside],
            ways.slow,
        )
        return ways.slow_steps(parts)

    most_room = 2 * most if split == 2 else most
    if most <= USUAL_PAIR:
        parts = partial_sums(most, most_room)
    else:
        rooms = [(USUAL, USUAL_PAIR), (USUAL_PAIR, USUAL_PAIR), (most, 2 * most)]
        branches = [
            functools.partial(partial_sums, cap, room if split == 2 else cap) for cap, room in rooms
        ]
        parts = lax.switch(most_facts[0], branches)
    return sum(part.astype(F32) for part in parts).astype(BF)


def solution(mesh):
    placed = (
        P(("groups", "ff"), "var"),
        P("var", "ff"),
        P("var", "ff"),
        P("ff", "var"),
        P(("groups", "ff"), None, "var"),
        P(("groups", "ff"), None, "var", None),
        P(("groups", "ff"), None, None),
        P(("groups", "ff"), None, "var"),
        P("groups", None),
        P("groups"),
    )
    return jax.shard_map(
        per_device,
        mesh=mesh,
        in_specs=placed,
        out_specs=P(("groups", "ff"), "var"),
        check_vma=False,
    )
```

```python
import functools

import jax
import jax.numpy as jnp
from jax import lax
from jax.experimental import pallas as pl
from jax.experimental.pallas import tpu as pltpu
from jax.sharding import PartitionSpec as P

MOST = 8
DIRECT = 8
MINE, NEXT, STEP, PLACE, ARRIVE, PACKED = range(6)
USUAL = 16
USUAL_PAIR = 24
CROWDED = 24
CROWDED_PAIR = 32
BF = jnp.bfloat16
F32 = jnp.float32
I32 = jnp.int32
MIB = 1024 * 1024


def dot(a, b):
    return jnp.dot(a, b, preferred_element_type=F32)


def dot_last(a, b):
    return lax.dot_general(a, b, (((1,), (1,)), ((), ())), preferred_element_type=F32)


def params(mib):
    return pltpu.CompilerParams(vmem_limit_bytes=int(mib * MIB))


def cost(flops, moved):
    return pl.CostEstimate(flops=flops, bytes_accessed=moved, transcendentals=0)


SCALARS = pl.BlockSpec(memory_space=pltpu.SMEM)
WHOLE = pl.BlockSpec(memory_space=pltpu.VMEM)
FAR = pl.BlockSpec(memory_space=pltpu.HBM)


def fixed(array):
    zeros = (0,) * array.ndim
    return pl.BlockSpec(array.shape, lambda *_: zeros)


def one_hot(count, cell):
    lines = lax.broadcasted_iota(I32, (count, cell.shape[1]), 0)
    return (lines == cell).astype(F32).astype(BF)


def dot_first(a, b):
    return lax.dot_general(a, b, (((0,), (0,)), ((), ())), preferred_element_type=F32)


class Ways:
    def __init__(self):
        self.shards = lax.axis_size("ff")
        self.fast = 2 if self.shards % 2 == 0 else 1
        self.slow = self.shards // self.fast
        self.direct = self.shards <= DIRECT
        me = lax.axis_index("ff").astype(I32)
        steps = jnp.arange(self.shards, dtype=I32)
        if self.direct:
            slow = (me // self.fast - steps % self.slow) % self.slow
            fast = (me % self.fast - steps // self.slow) % self.fast
            self.order = slow * self.fast + fast
        else:
            self.order = steps

    def back(self, a, c):
        S, F = self.slow, self.fast
        return [(s * F + f, (s - a) % S * F + (f - c) % F) for s in range(S) for f in range(F)]

    def gather(self, block, *others):
        if not self.direct:
            return list(lax.all_gather(block, "ff")), *others
        got = [block] + [
            lax.ppermute(block, "ff", self.back(-a, 0)) for a in range(1, self.slow)
        ]
        got[1], *others = tied(got[1], *others)
        for c in range(1, self.fast):
            got += [lax.ppermute(part, "ff", self.back(0, -c)) for part in got[: self.slow]]
        return got, *others

    def spread(self, blocks):
        return lax.all_to_all(blocks, "ff", 0, 0, tiled=True)

    def slow_steps(self, blocks):
        got = [blocks[0]] + [None] * (self.slow - 1)
        for a in range(1, self.slow):
            got[(-a) % self.slow] = lax.ppermute(blocks[a], "ff", self.back(a, 0))
        return got


def tables_kernel(
    ways,
    slots,
    order_ref,
    me_ref,
    at_ref,
    named_ref,
    x_ref,
    shrink_ref,
    expand_ref,
    marks_ref,
    in_ref,
    out_ref,
    facts_ref,
    kept_ref,
    held_ref,
    near_ref,
    sems,
):
    shards = order_ref.shape[0]
    half = near_ref.shape[1] // shards
    copies = [
        pltpu.make_async_copy(x_ref, kept_ref, sems.at[0]),
        pltpu.make_async_copy(shrink_ref, held_ref, sems.at[1]),
    ]
    for b in range(shards):
        columns = pl.ds(pl.multiple_of(at_ref[b] * half, half), half)
        put = near_ref.at[:, pl.ds(b * half, half)]
        copies.append(pltpu.make_async_copy(expand_ref.at[:, columns], put, sems.at[2 + b]))
    for copy in copies:
        copy.start()
    rows, size = in_ref.shape[0], named_ref.shape[1]
    own_rows = rows // shards
    me = me_ref[0].astype(F32)
    order = [order_ref[b].astype(F32) for b in range(shards)]
    beside_me = order[ways.slow % shards]
    count = lambda shape, axis: lax.broadcasted_iota(I32, shape, axis).astype(F32)
    across = lambda a: jnp.sum(a, axis=1, keepdims=True)
    along = lambda a: jnp.sum(a, axis=0, keepdims=True)
    line, lane = count((rows, rows), 0), count((rows, rows), 1)
    diagonal = line == lane
    at_along, at_down = count((1, rows), 1), count((rows, 1), 0)
    for b in range(shards):
        shift = (order[b] - b) * own_rows
        low, high = b * own_rows, (b + 1) * own_rows
        at_along = jnp.where(
            (lane[:1] >= low) & (lane[:1] < high), lane[:1] + shift, at_along
        )
        at_down = jnp.where(
            (line[:, :1] >= low) & (line[:, :1] < high), line[:, :1] + shift, at_down
        )
    named = named_ref[...].astype(F32)
    ids = across(jnp.where(count((rows, size), 1) == at_down, named, 0.0))
    ids = along(jnp.where(diagonal, ids, 0.0))
    variants = size - rows
    of_variant = count((variants, size), 1) == count((variants, size), 0) + rows
    slots_down = across(jnp.where(of_variant, named, 0.0))
    slot = along(jnp.where(count((variants, rows), 0) == ids, slots_down, 0.0))
    slot_down = across(jnp.where(diagonal, slot, 0.0))
    owner_of = lambda a: sum((a >= float(o * slots)).astype(F32) for o in range(1, shards))
    owner, owner_down = owner_of(slot), owner_of(slot_down)
    same = owner_down == owner
    place = along((same & (at_down < at_along)).astype(F32))
    packed, pair = place, jnp.zeros_like(place)
    step = arrive = jnp.zeros_like(place)
    paired = ways.direct and ways.fast == 2
    if paired:
        odd = sum((owner == float(o)).astype(F32) for o in range(1, shards, 2))
        beside = along((owner_down == owner + 1.0 - 2.0 * odd).astype(F32))
        pair = along(same.astype(F32)) + beside
    for b in range(shards):
        hit = owner == order[b]
        step = jnp.where(hit, float(b), step)
        arrive = jnp.where(hit, float(b % ways.slow if paired else b), arrive)
        if paired and b >= ways.slow:
            packed = jnp.where(hit, place + beside, packed)
    over = (place >= float(USUAL)) | (pair > float(USUAL_PAIR))
    far_over = (place >= float(CROWDED)) | (pair > float(CROWDED_PAIR))
    facts_ref[0] = jnp.max(jnp.where(far_over, 2.0, over.astype(F32))).astype(I32)
    facts_ref[1] = jnp.sum((owner == me).astype(F32)).astype(I32)
    facts_ref[2] = jnp.sum((owner == beside_me).astype(F32)).astype(I32)
    lines = {
        MINE: jnp.where(owner == me, place, -1.0),
        NEXT: jnp.where(owner == beside_me, place, -1.0),
        STEP: step,
        PLACE: place,
        ARRIVE: arrive,
        PACKED: packed,
    }
    for n, values in lines.items():
        marks_ref[n : n + 1] = values.astype(I32)
    local = slot_down - me * slots
    for ref in (in_ref, out_ref):
        wide = ref.shape[1] // slots
        column = count(ref.shape, 1)
        inside = (column >= local * wide) & (column < (local + 1.0) * wide)
        ref[...] = inside.astype(F32).astype(ref.dtype)
    for copy in copies:
        copy.wait()


def tables(ways, me, at, named, x, shrink, expand, rows, slots, rank):
    shards = at.shape[0]
    depth, width = expand.shape
    return pl.pallas_call(
        functools.partial(tables_kernel, ways, slots),
        out_shape=(
            jax.ShapeDtypeStruct((8, rows), I32),
            jax.ShapeDtypeStruct((rows, slots * 2 * rank), F32),
            jax.ShapeDtypeStruct((rows, slots * rank), BF),
            jax.ShapeDtypeStruct((3,), I32),
            jax.ShapeDtypeStruct(x.shape, BF),
            jax.ShapeDtypeStruct(shrink.shape, BF),
            jax.ShapeDtypeStruct((depth, width // 2), BF),
        ),
        in_specs=[SCALARS] * 3 + [WHOLE] + [FAR] * 3,
        out_specs=(WHOLE, WHOLE, WHOLE, SCALARS, WHOLE, WHOLE, WHOLE),
        scratch_shapes=[pltpu.SemaphoreType.DMA((2 + shards,))],
        compiler_params=params(52),
        cost_estimate=cost(0, 4 * x.size + 4 * shrink.size + 2 * expand.size),
    )(ways.order, me, at, named, x, shrink, expand)


def low_in_kernel(count, shrink_ref, mask_ref, *refs):
    parts, x_ref, out_ref = refs[:count], refs[count], refs[count + 1]
    x = jnp.concatenate([part[...].astype(F32) for part in parts], axis=0).astype(BF)
    x_ref[...] = x

    @pl.when(pl.program_id(0) == 0)
    def _():
        out_ref[...] = jnp.zeros_like(out_ref)

    out_ref[...] += jnp.where(mask_ref[...] > 0, dot_last(x, shrink_ref[...]), 0.0)


def low_in_pairs(parts, shrink, mask):
    count = len(parts)
    own_rows, width = parts[0].shape
    rows, block = count * own_rows, min(1024, width)
    return pl.pallas_call(
        lambda *refs: low_in_kernel(count, *refs),
        out_shape=(
            jax.ShapeDtypeStruct((rows, width), BF),
            jax.ShapeDtypeStruct(mask.shape, F32),
        ),
        grid=(width // block,),
        in_specs=[pl.BlockSpec((shrink.shape[0], block), lambda n: (0, n)), fixed(mask)]
        + [pl.BlockSpec((own_rows, block), lambda n: (0, n))] * count,
        out_specs=(pl.BlockSpec((rows, block), lambda n: (0, n)), fixed(mask)),
        compiler_params=params(16),
        cost_estimate=cost(2 * rows * width * shrink.shape[0], 2 * shrink.size + 4 * rows * width),
    )(shrink, mask, *parts)


def expand_kernel(
    cap, fast, at_ref, own_ref, got_ref, marks_ref, cols_ref, near_ref, far_ref, *out_refs
):
    low = (own_ref[...] + got_ref[...]).astype(BF)
    picked = dot(one_hot(cap, marks_ref[MINE : MINE + 1]), low).astype(BF)
    lhs = jnp.concatenate([dot(picked, cols_ref[kind]) for kind in range(2)], axis=0).astype(BF)
    tall = lhs.shape[0]
    half = out_refs[0].shape[1]
    count = at_ref.shape[0]
    for b in range(count):
        here = pl.ds(b * half, half)
        columns = pl.ds(pl.multiple_of(at_ref[b] * half, half), half)
        both = jnp.concatenate([near_ref[:, here], far_ref[:, columns]], axis=0)
        at = b % (count // fast)
        out_refs[b * fast // count][pl.ds(at * tall, tall)] = dot(lhs, both).astype(BF)


def expand_rows(at, own, got, marks, cols, near, far, cap, fast):
    depth, width = far.shape
    shards = at.shape[0]
    half = width // (2 * shards)
    out = jax.ShapeDtypeStruct((2 * cap * shards // fast, half), BF)
    return pl.pallas_call(
        functools.partial(expand_kernel, cap, fast),
        out_shape=(out,) * fast,
        in_specs=[SCALARS] + [WHOLE] * 6,
        compiler_params=params(16),
        cost_estimate=cost(8 * cap * depth * width, 4 * (depth + cap) * width),
    )(at, own, got, marks, cols, near, far)


def base_kernel(side_ref, x_ref, gate_ref, up_ref, out_ref, held, sums, sems):
    half = held.shape[2]
    chunks = sems.shape[1]
    depth = held.shape[1] // chunks
    columns = pl.ds(pl.multiple_of(side_ref[0] * half, half), half)
    copies = []
    for c in range(chunks):
        here = pl.ds(c * depth, depth)
        for kind, weight in enumerate((gate_ref, up_ref)):
            copy = pltpu.make_async_copy(
                weight.at[here, columns], held.at[kind, here], sems.at[kind, c]
            )
            copy.start()
            copies.append((kind, here, copy))
    for kind, here, copy in copies:
        copy.wait()
        part = dot(x_ref[:, here], held[kind, here])
        sums[kind] = part if here.start == 0 else sums[kind] + part
    out_ref[...] = sums[...].astype(out_ref.dtype)


def base_half(side, x, gate_weight, up_weight, half, kind):
    rows, width = x.shape
    chunks = max(width // 512, 1)
    return pl.pallas_call(
        base_kernel,
        out_shape=jax.ShapeDtypeStruct((2, rows, half), kind),
        in_specs=[SCALARS, WHOLE, FAR, FAR],
        out_specs=WHOLE,
        scratch_shapes=[
            pltpu.VMEM((2, width, half), BF),
            pltpu.VMEM((2, rows, half), F32),
            pltpu.SemaphoreType.DMA((2, chunks)),
        ],
        compiler_params=params(48),
        cost_estimate=cost(4 * rows * width * half, 4 * width * half + 2 * rows * width),
    )(side, x, gate_weight, up_weight)


def hidden_kernel(cap, room, count, own_ref, got_ref, marks_ref, *refs):
    parts, hid_ref, out_refs = refs[:count], refs[count], refs[count + 1 :]
    half = hid_ref.shape[1]
    cells = sum(part.shape[0] for part in parts)
    first_cell = marks_ref[ARRIVE : ARRIVE + 1] * (2 * room) + marks_ref[PACKED : PACKED + 1]
    places = [one_hot(cells, first_cell + kind * room) for kind in range(2)]
    tall = out_refs[0].shape[0]
    leave = marks_ref[STEP : STEP + 1] * cap + marks_ref[PLACE : PLACE + 1]
    send = one_hot(tall * len(out_refs), leave)
    block = min(256, half)
    for first in range(0, half, block):
        here = pl.ds(first, block)
        delta = jnp.concatenate([part[:, here] for part in parts], axis=0)
        gate, up = [
            own_ref[kind, :, here]
            + got_ref[kind, :, here].astype(F32)
            + dot_first(places[kind], delta)
            for kind in range(2)
        ]
        hidden = (gate / (1.0 + jnp.exp(-gate)) * up).astype(BF)
        hid_ref[:, here] = hidden
        sent = dot(send, hidden).astype(BF)
        for n, out_ref in enumerate(out_refs):
            out_ref[:, here] = sent[n * tall : (n + 1) * tall]


def hidden_half(own, got, parts, marks, cap, room, shards, count):
    rows, half = own.shape[1:]
    cells = shards * cap
    return pl.pallas_call(
        functools.partial(hidden_kernel, cap, room, len(parts)),
        out_shape=(jax.ShapeDtypeStruct((rows, half), BF),)
        + (jax.ShapeDtypeStruct((cells // count, half), BF),) * count,
        compiler_params=params(40),
        cost_estimate=cost(10 * half * cells * rows, 2 * half * (6 * rows + 3 * cells)),
    )(own, got, marks, *parts)


def pack_kernel(cap, facts_ref, own_ref, got_ref, *out_refs):
    column = lax.broadcasted_iota(I32, (1, 4 * cap), 1)
    from_got = column >= 2 * cap
    column = column - jnp.where(from_got, 2 * cap, 0)
    kind = jnp.where(column >= cap, 1, 0)
    row = column - kind * cap
    live = row < jnp.where(from_got, facts_ref[2], facts_ref[1])
    row = row + jnp.where(from_got, facts_ref[1], 0)
    room = out_refs[0].shape[0] // 2
    packing = one_hot(2 * room, jnp.where(live, row + kind * room, -1))
    for a, out_ref in enumerate(out_refs):
        here = pl.ds(a * 2 * cap, 2 * cap)
        both = jnp.concatenate([own_ref[here], got_ref[here]], axis=0)
        out_ref[...] = dot(packing, both).astype(BF)


def pack(facts, own, got, cap, room, count):
    half = own.shape[1]
    return pl.pallas_call(
        functools.partial(pack_kernel, cap),
        out_shape=(jax.ShapeDtypeStruct((2 * room, half), BF),) * count,
        in_specs=[SCALARS, WHOLE, WHOLE],
        compiler_params=params(16),
        cost_estimate=cost(0, 8 * own.size),
    )(facts, own, got)


def relay_kernel(own_ref, got_ref, *out_refs):
    cap = out_refs[0].shape[0] // 2
    for a, out_ref in enumerate(out_refs):
        here = pl.ds(a * cap, cap)
        out_ref[:cap] = own_ref[here]
        out_ref[cap:] = got_ref[here]


def relay(own, got, count):
    tall, half = own.shape
    return pl.pallas_call(
        relay_kernel,
        out_shape=(jax.ShapeDtypeStruct((2 * tall // count, half), BF),) * count,
        compiler_params=params(16),
        cost_estimate=cost(0, 8 * tall * half),
    )(own, got)


def down_kernel(start, core_ref, near_ref, far_ref, weight_ref, *refs):
    out_refs, held, sems = refs[:-2], refs[-2], refs[-1]
    chunks = sems.shape[1]
    half, width = held.shape[1:]
    block = width // chunks
    tall = out_refs[0].shape[0]
    copies = []
    for c in range(chunks):
        here = pl.ds(c * block, block)
        for side, at in enumerate((core_ref[0], 1 - core_ref[0])):
            lines = pl.ds(pl.multiple_of(at * half, half), half)
            copy = pltpu.make_async_copy(
                weight_ref.at[lines, pl.ds(start + c * block, block)],
                held.at[side, :, here],
                sems.at[side, c],
            )
            copy.start()
            copies.append(copy)
    for c in range(chunks):
        here = pl.ds(c * block, block)
        copies[2 * c].wait()
        copies[2 * c + 1].wait()
        total = dot(near_ref[...], held[0, :, here]) + dot(far_ref[...], held[1, :, here])
        for n, out_ref in enumerate(out_refs):
            out_ref[:, here] = total[n * tall : (n + 1) * tall].astype(out_ref.dtype)


def down_base(core, near, far, weight, start, width, kinds):
    rows, half = near.shape
    chunks = max(width // 512, 1)
    outs = tuple(jax.ShapeDtypeStruct((rows // len(kinds), width), kind) for kind in kinds)
    return pl.pallas_call(
        functools.partial(down_kernel, start),
        out_shape=outs,
        in_specs=[SCALARS, WHOLE, WHOLE, FAR],
        out_specs=(WHOLE,) * len(outs),
        scratch_shapes=[
            pltpu.VMEM((2, half, width), BF),
            pltpu.SemaphoreType.DMA((2, chunks)),
        ],
        compiler_params=params(48),
        cost_estimate=cost(4 * rows * half * width, 4 * half * width + 4 * rows * width),
    )(core, near, far, weight)


def low_out_kernel(cap, count, at_ref, marks_ref, slot_ref, shrink_ref, *refs):
    parts, out_ref = refs[:count], refs[count]
    half = parts[0].shape[1]
    blocks = [part[r : r + cap] for r in range(0, parts[0].shape[0], cap) for part in parts]
    pairs = jnp.zeros(out_ref.shape, F32)
    for b, block in enumerate(blocks):
        columns = pl.ds(pl.multiple_of(at_ref[b] * half, half), half)
        pairs += dot_last(block, shrink_ref[:, columns])
    mask = dot(one_hot(cap, marks_ref[MINE : MINE + 1]), slot_ref[...])
    out_ref[...] = jnp.where(mask > 0.5, pairs, 0.0)


def low_out_pairs(at, marks, slot_mask, shrink, parts, cap):
    count = len(parts)
    half = parts[0].shape[1]
    depth = shrink.shape[0]
    return pl.pallas_call(
        functools.partial(low_out_kernel, cap, count),
        out_shape=jax.ShapeDtypeStruct((cap, depth), F32),
        in_specs=[SCALARS] + [WHOLE] * (3 + count),
        compiler_params=params(16),
        cost_estimate=cost(
            2 * cap * depth * at.shape[0] * half, 2 * at.shape[0] * half * (depth + cap)
        ),
    )(at, marks, slot_mask, shrink, *parts)


def add_kernel(owners, sides, *refs):
    base_refs, refs = refs[: owners * sides], refs[owners * sides :]
    low_refs, refs = refs[: 2 * owners], refs[2 * owners :]
    marks_ref, expand_refs, out_refs = refs[0], refs[1 : owners + 1], refs[owners + 1 :]
    rows = base_refs[0].shape[0]
    spreads = []
    for n in range(owners):
        low = (low_refs[2 * n][...] + low_refs[2 * n + 1][...]).astype(BF)
        pick = one_hot(low.shape[0], marks_ref[MINE + n : MINE + n + 1, :rows])
        spreads.append(dot_first(pick, low).astype(BF))
    spread = jnp.concatenate(spreads, axis=1)
    own_rows, width = out_refs[0].shape
    side = width // sides
    block = min(1024, side)
    for first in range(0, width, block):
        here = pl.ds(first, block)
        inside = pl.ds(first % side, block)
        expand = jnp.concatenate([ref[:, here] for ref in expand_refs], axis=0)
        total = dot(spread, expand)
        for base_ref in base_refs[first // side :: sides]:
            total += base_ref[:, inside].astype(F32)
        for b, out_ref in enumerate(out_refs):
            out_ref[:, here] = total[b * own_rows : (b + 1) * own_rows].astype(BF)


def add_delta(bases, lows, marks, expands, count):
    owners = len(expands)
    rows = bases[0].shape[0]
    depth, width = expands[0].shape
    return pl.pallas_call(
        functools.partial(add_kernel, owners, len(bases) // owners),
        out_shape=(jax.ShapeDtypeStruct((rows // count, width), BF),) * count,
        compiler_params=params(32),
        cost_estimate=cost(
            2 * rows * depth * owners * width, width * (6 * rows + 2 * depth) * owners
        ),
    )(*bases, *lows, marks, *expands)


def tied(first, *others):
    return lax.optimization_barrier((first, *others))


def per_device(
    tokens,
    gate_weight,
    up_weight,
    down_weight,
    shrink_gu,
    expand_gu,
    shrink_down,
    expand_down,
    variant_ids,
    variant_slot,
):
    ways = Ways()
    shards, order = ways.shards, ways.order
    me = lax.axis_index("ff").astype(I32)
    core = lax.axis_index("var").astype(I32)
    groups = lax.axis_size("groups")
    own_rows, width = tokens.shape
    rows = own_rows * shards
    slots = shrink_gu.shape[0]
    rank = shrink_down.shape[1]
    half_rank = expand_gu.shape[2]
    half = gate_weight.shape[1] // 2
    most = min(slots * MOST, rows)
    here = core.reshape(1)
    there = 1 - here
    at_here = 2 * order + core
    split = ways.fast if ways.direct else 1
    swap = lambda a: lax.ppermute(a, "var", [(0, 1), (1, 0)])

    near = expand_gu.reshape(slots * 2 * half_rank, -1)
    named = jnp.concatenate([variant_ids[:, 0], variant_slot]).reshape(1, -1)
    token_parts, far, named = ways.gather(tokens, swap(near), named)
    shrink_in = shrink_gu.reshape(slots * 2 * rank, width)
    marks, mask_in, slot_mask, facts, token_parts[0], shrink_in, near = tables(
        ways,
        me.reshape(1),
        at_here,
        named,
        token_parts[0],
        shrink_in,
        near,
        rows,
        slots,
        rank,
    )
    most_facts = facts
    for turn in range(1, 1 if ways.direct else groups):
        pairs = [(g, (g + turn) % groups) for g in range(groups)]
        most_facts = jnp.maximum(most_facts, lax.ppermute(facts, "groups", pairs))
    kinds = jnp.arange(2, dtype=I32)
    in_cols = jnp.arange(slots * 2 * rank, dtype=I32)
    rank_at = in_cols % rank
    kind_at = in_cols // rank % 2
    row_at = in_cols // (2 * rank) * (2 * half_rank) + kind_at * half_rank + rank_at % half_rank
    depth = slots * 2 * half_rank
    both_cols = jnp.arange(2 * depth, dtype=I32)
    wanted = row_at + jnp.where(rank_at // half_rank == core, 0, depth)
    hit = wanted[:, None] == both_cols[None, :]
    cols = (hit[None] & (kind_at[None, :] == kinds[:, None])[:, :, None]).astype(BF)

    x, low_own = low_in_pairs(token_parts, shrink_in, mask_in)
    low_got = swap(low_own)

    def partial_sums(cap, room):
        made = expand_rows(at_here, low_own, low_got, marks, cols, near, far, cap, split)
        held, *made = tied(x, *made)
        expand = expand_down.reshape(slots * rank, width)
        if split == 2:
            beside = lax.ppermute(made[1], "ff", ways.back(0, 1))
            base_there = base_half(there, held, gate_weight, up_weight, half, BF)
            base_there, beside = tied(base_there, beside)
            made = pack(facts, made[0], beside, cap, room, ways.slow)
            held, expand, *made = tied(held, expand, *made)
            delta = ways.slow_steps(made)
            expand_beside = lax.ppermute(expand, "ff", ways.back(0, 1))
        else:
            base_there = base_half(there, held, gate_weight, up_weight, half, BF)
            delta = ways.spread(made[0].reshape(shards, 2 * cap, half))
            delta = [delta.reshape(2 * shards * cap, half)]
        base_got = swap(base_there)
        base_own = base_half(here, held, gate_weight, up_weight, half, F32)
        hidden, *sent = hidden_half(
            base_own, base_got, delta, marks, cap, room, shards, split
        )
        hidden_far = swap(hidden)
        shrink = shrink_down.reshape(slots * rank, -1)
        side = width // 2
        down = functools.partial(down_base, here, hidden, hidden_far, down_weight)
        if split == 2:
            beside = lax.ppermute(sent[1], "ff", ways.back(0, 1))
            left, left_sent = down(0, side, (F32, BF))
            left_sent, beside, expand_beside = tied(left_sent, beside, expand_beside)
            left_beside = lax.ppermute(left_sent, "ff", ways.back(0, 1))
            sent = relay(sent[0], beside, ways.slow)
            hidden, *sent = tied(hidden, *sent)
            down = functools.partial(down_base, here, hidden, hidden_far, down_weight)
            got = ways.slow_steps(sent)
            right, right_sent = down(side, side, (F32, BF))
            right_sent, left_beside, *got = tied(right_sent, left_beside, *got)
            right_beside = lax.ppermute(right_sent, "ff", ways.back(0, 1))
            bases = [left, right, left_beside, right_beside]
        else:
            bases = [down(0, side, (F32,))[0], down(side, side, (F32,))[0]]
            got = [ways.spread(sent[0].reshape(shards, cap, half)).reshape(shards * cap, half)]
        bases[1], *got = tied(bases[1], *got)
        out_own = low_out_pairs(at_here, marks, slot_mask, shrink, got, cap)
        out_got = swap(out_own)
        if split == 1:
            parts = add_delta(bases, [out_own, out_got], marks, [expand], shards)
            return list(ways.spread(jnp.stack(parts)))
        out_beside = lax.ppermute(out_own, "ff", ways.back(0, 1))
        across = [
            (2 * f + v, 2 * g + 1 - v) for f, g in ways.back(0, 1) for v in range(2)
        ]
        out_across = lax.ppermute(out_own, ("ff", "var"), across)
        parts = add_delta(
            bases,
            [out_own, out_got, out_beside, out_across],
            marks,
            [expand, expand_beside],
            ways.slow,
        )
        return ways.slow_steps(parts)

    most_room = 2 * most if split == 2 else most
    if most <= CROWDED:
        parts = partial_sums(most, most_room)
    else:
        rooms = [(USUAL, USUAL_PAIR), (CROWDED, CROWDED_PAIR), (most, 2 * most)]
        branches = [
            functools.partial(partial_sums, cap, room if split == 2 else cap) for cap, room in rooms
        ]
        parts = lax.switch(most_facts[0], branches)
    return sum(part.astype(F32) for part in parts).astype(BF)


def solution(mesh):
    placed = (
        P(("groups", "ff"), "var"),
        P("var", "ff"),
        P("var", "ff"),
        P("ff", "var"),
        P(("groups", "ff"), None, "var"),
        P(("groups", "ff"), None, "var", None),
        P(("groups", "ff"), None, None),
        P(("groups", "ff"), None, "var"),
        P("groups", None),
        P("groups"),
    )
    return jax.shard_map(
        per_device,
        mesh=mesh,
        in_specs=placed,
        out_specs=P(("groups", "ff"), "var"),
        check_vma=False,
    )
```
